256 devices in a mesh: seq: 32 (over x, y, core), kvh: 8 (over z).
Axes of the slice: x: 4, y: 4, z: 8, core: 2. Of those that a mesh axis runs over, the one named last changes fastest.
Arguments:
- queries: bfloat16 [4096, 8192], P('seq', 'kvh'), may hold values from -8 to 8, as said below
- rotated_response_keys: bfloat16 [4096, 1024], P('seq', 'kvh'), may hold values from -8 to 8
- response_values: bfloat16 [4096, 1024], P('seq', 'kvh'), may hold values from -6 to 6
- prompt_keys: bfloat16 [16384, 1024], P('seq', 'kvh'), may hold values from -8 to 8
- prompt_values: bfloat16 [16384, 1024], P('seq', 'kvh'), may hold values from -6 to 6
- out_weight: bfloat16 [8192, 5120], P('kvh'), may hold values from -0.0625 to 0.0625
- segment_ids: int32 [4096], replicated, may hold values from 0 to 63, never falling along the last dimension, each value on 1 to 128 neighbouring positions
- block_mask: int32 [32, 128], replicated, may hold values from 0 to 1, as said below
Outputs:
- layer_out: bfloat16 [4096, 5120], P('seq', 'kvh')
The draws below stay inside these ranges and needn't reach their ends.
Inputs may be any that keep to these rules, and one draw needn't show every extreme that they name: `queries`: query entries lie within -8 to 8. `block_mask`: the prompt tiles fall into 4 runs of consecutive tiles, none empty; each response tile reads exactly one run.
All inputs are finite; a program needn't handle non-finite values.
Results may differ from the reference program's by a relative error of at most 0.0085.
Values may be sent and summed in bfloat16 or wider, within the bound.
No kernel may reach another device: no remote copies, remote signals or barrier semaphores. Data moves between devices by JAX's collectives and lax.ppermute only.
A program may use at most 192 MiB of HBM per device.

```python
import math
import jax
import jax.numpy as jnp
import numpy as np
from jax import lax

D = 5120
H = 64
KVH = 8
CHANNEL_WIDTH = 128
ANSWER_LINES = 128
TILE = 128
CONTEXT_COUNT = 4
ROWS = 4096
CONTEXT_LENGTH = 16384
RESP = 64
RTILES = 32
PTILES = 128


def recent_direction(key):
    signs = jax.random.randint(jax.random.fold_in(key, 901), (CHANNEL_WIDTH,), 0, 2)
    logit_offset = math.log(CONTEXT_LENGTH / (CONTEXT_COUNT * ANSWER_LINES)) + 1.0
    pattern_magnitude = math.sqrt(logit_offset / math.sqrt(CHANNEL_WIDTH))
    return pattern_magnitude * (2 * signs - 1).astype(jnp.float32)


def draw_queries(key, part):
    recent = jnp.tile(recent_direction(key), H)[None, :]
    key = jax.random.fold_in(key, 1)
    values = jnp.clip(1.6 * jax.random.normal(key, (ROWS, H * CHANNEL_WIDTH), jnp.float32), -6.0, 6.0) + recent
    return values.astype(jnp.bfloat16)


def draw_rotated_response_keys(key, part):
    recent = jnp.tile(recent_direction(key), KVH)[None, :]
    key = jax.random.fold_in(key, 4)
    base = jnp.clip(1.6 * jax.random.normal(key, (ROWS, KVH * CHANNEL_WIDTH), jnp.float32), -6.0, 6.0)
    return (base + recent).astype(jnp.bfloat16)


def draw_prompt_keys(key, part):
    key = jax.random.fold_in(key, 2)
    values = jnp.clip(1.6 * jax.random.normal(key, (CONTEXT_LENGTH, KVH * CHANNEL_WIDTH), jnp.float32), -8.0, 8.0)
    return values.astype(jnp.bfloat16)


def draw_block_mask(key, part):
    key = jax.random.fold_in(key, 3)
    first_key, second_key = jax.random.split(key)
    cuts = jnp.sort(jax.random.permutation(first_key, PTILES - 1)[:CONTEXT_COUNT - 1] + 1)
    prompt_group = jnp.sum(jnp.arange(PTILES)[:, None] >= cuts[None, :], axis=1)
    tile_group = jax.random.randint(second_key, (RTILES,), 0, CONTEXT_COUNT)
    return (tile_group[:, None] == prompt_group[None, :]).astype(jnp.int32)


def steps_of(stream_key, extent, pieces, low, largest):
    loudness = 1.0
    for position, blocks in pieces:
        draws = jax.random.uniform(jax.random.fold_in(jax.random.fold_in(stream_key, 6), position), (blocks,), jnp.float32, low / len(pieces), largest / len(pieces))
        loudness = loudness * jnp.repeat(jnp.exp(draws), extent[position] // blocks).reshape((-1,) + (1,) * (len(extent) - 1 - position))
    return loudness


def split_up(number_of, total, limit, lean):
    weights = [(1 << 20) // math.isqrt(grade ** lean) + 1 for grade in range(2, number_of + 1)]
    rest, holding = total - limit - (number_of - 1), [1] * (number_of - 1)
    while rest > 0:
        movable = [i for i in range(number_of - 1) if holding[i] < limit]
        whole, remaining = sum([weights[i] for i in movable]), rest
        for i in movable:
            more = min(limit - holding[i], max(1, remaining * weights[i] // whole), rest)
            holding[i] = holding[i] + more
            rest = rest - more
    return np.array([limit] + holding)


def uneven_parts(rng, amount, total, bound, lean):
    if amount == 2:
        one = jax.random.randint(rng, (), max(1, total - bound), min(bound, total - 1) + 1)
        return jnp.stack([one, total - one])
    sizes = jnp.asarray(split_up(amount, total, bound, lean), jnp.int32)
    couples = (amount - 1) // 2
    source_of, receiver = sizes[1:1 + 2 * couples:2], sizes[2:2 + 2 * couples:2]
    margin = jnp.minimum(source_of - 1, bound - receiver)
    shifted = jax.random.randint(jax.random.fold_in(rng, 1), (couples,), 0, 1 << 20) % (margin + 1)
    sizes = sizes.at[1:1 + 2 * couples:2].set(source_of - shifted).at[2:2 + 2 * couples:2].set(receiver + shifted)
    return sizes[jax.random.permutation(jax.random.fold_in(rng, 2), amount)]


def normal_values(stream_key, extent, deviation, reach, pieces=(), kind=jnp.bfloat16):
    result = deviation * jax.random.normal(stream_key, extent, jnp.float32)
    if pieces:
        result = result * steps_of(stream_key, extent, pieces, -0.22, 0.18)
    return jnp.clip(result, -reach, reach).astype(kind)


def setup_inputs(seed: int = 0) -> dict:
    seeds = jax.random.split(jax.random.key(seed), 9)
    queries = draw_queries(jax.random.fold_in(seeds[8], 71), 0)
    rotated_response_keys = draw_rotated_response_keys(jax.random.fold_in(seeds[8], 71), 0)
    response_values = normal_values(seeds[2], (ROWS, KVH * CHANNEL_WIDTH), 1.0, 6.0, ((0, 32), (1, 8)))
    prompt_keys = draw_prompt_keys(jax.random.fold_in(seeds[8], 71), 0)
    prompt_values = normal_values(seeds[4], (CONTEXT_LENGTH, KVH * CHANNEL_WIDTH), 1.0, 6.0, ((0, 32), (1, 8)))
    out_weight = normal_values(seeds[5], (H * CHANNEL_WIDTH, D), (H * CHANNEL_WIDTH) ** -0.5, 0.0625, ((0, 8),))
    segment_ids = jnp.searchsorted(jnp.cumsum(uneven_parts(seeds[6], RESP, ROWS, ANSWER_LINES, 2)), jnp.arange(ROWS), side="right").astype(jnp.int32)
    block_mask = draw_block_mask(jax.random.fold_in(seeds[8], 71), 0)
    return {"queries": queries, "rotated_response_keys": rotated_response_keys, "response_values": response_values, "prompt_keys": prompt_keys, "prompt_values": prompt_values, "out_weight": out_weight, "segment_ids": segment_ids, "block_mask": block_mask}


NEG_FILL = -1e+30

def reference(queries, rotated_response_keys, response_values, prompt_keys, prompt_values, out_weight, segment_ids, block_mask):
    group_heads = H // KVH
    tiles_count = ROWS // TILE
    scale = 1.0 / math.sqrt(CHANNEL_WIDTH)
    positions = jnp.arange(ROWS, dtype=jnp.int32)

    def one_tile(number):
        head_group = number // tiles_count
        tile = number % tiles_count
        first = tile * TILE
        query_block = lax.dynamic_slice(queries, (first, head_group * group_heads * CHANNEL_WIDTH), (TILE, group_heads * CHANNEL_WIDTH))
        query_block = query_block.astype(jnp.float32).reshape(TILE, group_heads, CHANNEL_WIDTH)
        key_prompt = lax.dynamic_slice_in_dim(prompt_keys, head_group * CHANNEL_WIDTH, CHANNEL_WIDTH, 1).astype(jnp.float32)
        value_prompt = lax.dynamic_slice_in_dim(prompt_values, head_group * CHANNEL_WIDTH, CHANNEL_WIDTH, 1).astype(jnp.float32)
        key_own = lax.dynamic_slice_in_dim(rotated_response_keys, head_group * CHANNEL_WIDTH, CHANNEL_WIDTH, 1).astype(jnp.float32)
        value_own = lax.dynamic_slice_in_dim(response_values, head_group * CHANNEL_WIDTH, CHANNEL_WIDTH, 1).astype(jnp.float32)
        keys_all = jnp.concatenate([key_prompt, key_own], 0)
        values_all = jnp.concatenate([value_prompt, value_own], 0)
        scores = jnp.einsum('rjd,nd->rjn', query_block, keys_all) * scale
        mask_row = lax.dynamic_index_in_dim(block_mask, tile, 0, keepdims=False)
        prompt_seen = jnp.repeat(mask_row, TILE, total_repeat_length=CONTEXT_LENGTH) > 0
        row_ids = first + jnp.arange(TILE, dtype=jnp.int32)
        row_segments = lax.dynamic_slice_in_dim(segment_ids, first, TILE)
        own_seen = (segment_ids[None, :] == row_segments[:, None]) & (positions[None, :] <= row_ids[:, None])
        visible = jnp.concatenate([jnp.broadcast_to(prompt_seen[None, :], (TILE, CONTEXT_LENGTH)), own_seen], 1)[:, None, :]
        row_max = lax.optimization_barrier(jnp.max(jnp.where(visible, scores, NEG_FILL), axis=-1, keepdims=True))
        weights = jnp.where(visible, jnp.exp(scores - row_max), 0.0)
        totals = lax.optimization_barrier(jnp.sum(weights, axis=-1))
        rounded = lax.optimization_barrier(weights.astype(jnp.bfloat16)).astype(jnp.float32)
        mixed = jnp.einsum('rjn,nd->rjd', rounded, values_all) / totals[..., None]
        return mixed.astype(jnp.bfloat16)
    heads_out = lax.map(one_tile, jnp.arange(KVH * tiles_count, dtype=jnp.int32))
    attended = heads_out.reshape(KVH, tiles_count, TILE, group_heads, CHANNEL_WIDTH).transpose(1, 2, 0, 3, 4).reshape(ROWS, H * CHANNEL_WIDTH)
    return jnp.dot(attended, out_weight, preferred_element_type=jnp.float32).astype(jnp.bfloat16)
```

```python
import functools
import math

import jax
import jax.numpy as jnp
from jax import lax
from jax.experimental import pallas as pl
from jax.experimental.pallas import tpu as pltpu
from jax.sharding import Mesh, PartitionSpec as P

H = 64
KVH = 8
CW = 128
TILE = 128
HEADS = H // KVH
XS, YS, CORES, ZS = 4, 4, 2, 8
PIECES = (0, 1, -1, 2)
PIECE = 1024
BLOCK = 256
NEG_FILL = -1e30
SCALE2 = math.log2(math.e) / math.sqrt(CW)
STATS = 3
QROWS = HEADS * TILE
OUT_BLOCK = 640


def seq_index(x, y, c):
    return ((x % XS) * YS + y % YS) * CORES + c


def shifted(block, axis, step):
    n = lax.axis_size(axis)
    return lax.ppermute(block, axis, [((i + step) % n, i) for i in range(n)])


def attend_kernel(own, flags_ref, q_ref, *refs):
    kv_refs = refs[:4]
    refs = refs[4:]
    if own:
        (prev_ref, mine_ref, bias_ref), refs = refs[:3], refs[3:]
    out_ref, q_s, s_s, m_s, l_s, acc_s = refs
    for h in range(HEADS):
        q_s[h * TILE : (h + 1) * TILE, :] = q_ref[:, h * CW : (h + 1) * CW]
    m_s[...] = jnp.full_like(m_s, NEG_FILL)
    l_s[...] = jnp.zeros_like(l_s)
    acc_s[...] = jnp.zeros_like(acc_s)
    per_piece = PIECE // BLOCK

    def flag(piece, b, half):
        return flags_ref[piece * (PIECE // TILE) + 2 * b + half]

    def qk(k):
        return lax.dot_general(
            q_s[...], k, (((1,), (1,)), ((), ())), preferred_element_type=jnp.float32
        )

    def weigh(slot, v):
        m = m_s[...]
        s = s_s[slot]
        p0 = jnp.exp2(s[:, :TILE] * SCALE2 - m)
        p1 = jnp.exp2(s[:, TILE:] * SCALE2 - m)
        l_s[...] += p0 + p1
        p = jnp.concatenate([p0, p1], axis=1).astype(jnp.bfloat16)
        acc_s[...] += jnp.dot(p, v, preferred_element_type=jnp.float32)

    for piece in range(4):

        def score_block(b, _):
            f0, f1 = flag(piece, b, 0), flag(piece, b, 1)

            @pl.when(f0 + f1 > 0)
            def _():
                start = pl.multiple_of(b * BLOCK, BLOCK)
                s = qk(kv_refs[piece][pl.ds(start, BLOCK), :CW])
                s0 = s[:, :TILE] + jnp.where(f0 > 0, 0.0, NEG_FILL)
                s1 = s[:, TILE:] + jnp.where(f1 > 0, 0.0, NEG_FILL)
                s_s[piece * per_piece + b] = jnp.concatenate([s0, s1], axis=1)
                m_s[...] = jnp.maximum(m_s[...], jnp.maximum(s0, s1))

            return 0

        lax.fori_loop(0, per_piece, score_block, 0)
    last = 4 * per_piece
    if own:
        s = qk(jnp.concatenate([prev_ref[:, :CW], mine_ref[:, :CW]], axis=0))
        s = (s.reshape(HEADS, TILE, 2 * TILE) + bias_ref[...][None]).reshape(QROWS, 2 * TILE)
        s_s[last] = s
        m_s[...] = jnp.maximum(m_s[...], jnp.maximum(s[:, :TILE], s[:, TILE:]))
    m_s[...] = jnp.broadcast_to(jnp.max(m_s[...], axis=1, keepdims=True) * SCALE2, m_s.shape)
    for piece in range(4):

        def weigh_block(b, _):
            @pl.when(flag(piece, b, 0) + flag(piece, b, 1) > 0)
            def _():
                start = pl.multiple_of(b * BLOCK, BLOCK)
                weigh(piece * per_piece + b, kv_refs[piece][pl.ds(start, BLOCK), CW:])

            return 0

        lax.fori_loop(0, per_piece, weigh_block, 0)
    if own:
        weigh(last, jnp.concatenate([prev_ref[:, CW:], mine_ref[:, CW:]], axis=0))
    total = jnp.maximum(jnp.sum(l_s[...], axis=1, keepdims=True), 1e-30)
    inverse = 1.0 / total
    lse = m_s[...][:, :1] + jnp.log2(total)
    lanes = lax.broadcasted_iota(jnp.int32, (TILE, CW), 1)
    stats = jnp.zeros((TILE, CW), jnp.float32)
    for h in range(HEADS):
        rows = slice(h * TILE, (h + 1) * TILE)
        out_ref[:, h * CW : (h + 1) * CW] = (acc_s[rows, :] * inverse[rows]).astype(out_ref.dtype)
        rest = lse[rows]
        if own:
            stats = jnp.where(lanes == STATS * h, rest, stats)
            continue
        for i in range(STATS):
            part = rest.astype(jnp.bfloat16).astype(jnp.float32)
            stats = jnp.where(lanes == STATS * h + i, part, stats)
            rest = rest - part
    out_ref[:, HEADS * CW :] = stats.astype(out_ref.dtype)


def attend(flags, q, pieces, own_parts=None):
    own = own_parts is not None
    args = [flags, q, *pieces, *(own_parts or ())]
    vmem = pl.BlockSpec(memory_space=pltpu.VMEM)
    slots = 4 * PIECE // BLOCK + own
    return pl.pallas_call(
        functools.partial(attend_kernel, own),
        out_shape=jax.ShapeDtypeStruct(
            (TILE, HEADS * CW + CW), jnp.float32 if own else jnp.bfloat16
        ),
        in_specs=[pl.BlockSpec(memory_space=pltpu.SMEM)] + [vmem] * (len(args) - 1),
        out_specs=vmem,
        scratch_shapes=[
            pltpu.VMEM((QROWS, CW), jnp.bfloat16),
            pltpu.VMEM((slots, QROWS, BLOCK), jnp.float32),
            pltpu.VMEM((QROWS, TILE), jnp.float32),
            pltpu.VMEM((QROWS, TILE), jnp.float32),
            pltpu.VMEM((QROWS, CW), jnp.float32),
        ],
        compiler_params=pltpu.CompilerParams(vmem_limit_bytes=36 << 20),
        cost_estimate=pl.CostEstimate(
            flops=QROWS * 1536 * CW * 4, bytes_accessed=2 << 20, transcendentals=QROWS * 1536
        ),
        name="attend_own" if own else "attend_other",
    )(*args)


def project_first_kernel(idx_ref, own_ref, a_ref, b_ref, c_ref, w_ref, one_ref, two_ref, att_ref):
    step = pl.program_id(0)

    @pl.when(step == 0)
    def _():
        refs = (own_ref, a_ref, b_ref, c_ref)
        stats = [r[:, HEADS * CW :].astype(jnp.float32) for r in refs]
        for h in range(HEADS):
            cols = slice(h * CW, (h + 1) * CW)
            lses = []
            for st in stats:
                i = STATS * h
                lses.append(st[:, i : i + 1] + st[:, i + 1 : i + 2] + st[:, i + 2 : i + 3])
            top = functools.reduce(jnp.maximum, lses)
            weights = [jnp.exp2(x - top) for x in lses]
            inverse = 1.0 / sum(weights)
            mixed = sum(r[:, cols].astype(jnp.float32) * (w * inverse) for r, w in zip(refs, weights))
            att_ref[:, cols] = mixed.astype(jnp.bfloat16)

    term = jnp.dot(att_ref[...], w_ref[...], preferred_element_type=jnp.float32).astype(jnp.bfloat16)

    @pl.when(step < 2)
    def _():
        one_ref[0] = term

    @pl.when(step >= 2)
    def _():
        two_ref[0] = term


def project_first(idx, own, others, weight):
    rows, width = TILE, HEADS * CW
    whole = pl.BlockSpec((rows, width + CW), lambda j, i: (0, 0))
    pair = jax.ShapeDtypeStruct((2, rows, OUT_BLOCK), jnp.bfloat16)
    return pl.pallas_call(
        project_first_kernel,
        grid_spec=pltpu.PrefetchScalarGridSpec(
            num_scalar_prefetch=1,
            grid=(4,),
            in_specs=[whole] * 4 + [pl.BlockSpec((width, OUT_BLOCK), lambda j, i: (0, i[j]))],
            out_specs=[
                pl.BlockSpec((1, rows, OUT_BLOCK), lambda j, i: (jnp.minimum(j, 1), 0, 0)),
                pl.BlockSpec((1, rows, OUT_BLOCK), lambda j, i: (jnp.maximum(j - 2, 0), 0, 0)),
                pl.BlockSpec((rows, width), lambda j, i: (0, 0)),
            ],
        ),
        out_shape=[pair, pair, jax.ShapeDtypeStruct((rows, width), jnp.bfloat16)],
        compiler_params=pltpu.CompilerParams(vmem_limit_bytes=20 << 20),
        cost_estimate=pl.CostEstimate(
            flops=2 * rows * width * OUT_BLOCK * 4, bytes_accessed=6 << 20, transcendentals=0
        ),
        name="project_first",
    )(idx, own, *others, weight)


def project_second_kernel(idx_ref, att_ref, w_ref, out_ref):
    out_ref[0] = jnp.dot(att_ref[...], w_ref[...], preferred_element_type=jnp.float32)


def project_second(idx, att, weight):
    rows, width = att.shape
    return pl.pallas_call(
        project_second_kernel,
        grid_spec=pltpu.PrefetchScalarGridSpec(
            num_scalar_prefetch=1,
            grid=(4,),
            in_specs=[
                pl.BlockSpec((rows, width), lambda j, i: (0, 0)),
                pl.BlockSpec((width, OUT_BLOCK), lambda j, i: (0, i[j + 4])),
            ],
            out_specs=pl.BlockSpec((1, rows, OUT_BLOCK), lambda j, i: (j, 0, 0)),
        ),
        out_shape=jax.ShapeDtypeStruct((4, rows, OUT_BLOCK), jnp.float32),
        compiler_params=pltpu.CompilerParams(vmem_limit_bytes=20 << 20),
        cost_estimate=pl.CostEstimate(
            flops=2 * rows * width * OUT_BLOCK * 4, bytes_accessed=6 << 20, transcendentals=0
        ),
        name="project_second",
    )(idx, att, weight)


def along_z(block, step):
    route = [
        (c * ZS + z, c * ZS + (z + (step if c == 0 else -step)) % ZS)
        for c in range(CORES)
        for z in range(ZS)
    ]
    return lax.ppermute(block, ("core", "z"), route)


def body(q, rkeys, rvalues, pkeys, pvalues, weight, segment_ids, block_mask):
    x, y, core, z = (lax.axis_index(a) for a in ("x", "y", "core", "z"))
    device = (x * YS + y) * CORES + core
    kv = jnp.concatenate([pkeys, pvalues], axis=1)
    rkv = jnp.concatenate([rkeys, rvalues], axis=1)

    kvs = [kv] + [shifted(kv, "x", step) for step in PIECES[1:]]
    steps = (2, 1, -1)
    qs = [shifted(q, "y", step) for step in steps]
    route = [
        (seq, seq + 1) for seq in range(XS * YS * CORES - 1)
    ]
    prev = lax.ppermute(rkv, ("x", "y", "core"), route)
    pieces = [lax.all_gather(p, "core", axis=0, tiled=True) for p in kvs]

    seen = lax.dynamic_slice(
        block_mask.reshape(XS, YS, CORES, XS, YS, PIECE // TILE),
        (x, 0, core, 0, y, 0),
        (1, YS, 1, XS, 1, PIECE // TILE),
    ).reshape(YS, XS, PIECE // TILE)
    seen = jnp.roll(seen, (-y, -x), (0, 1))
    seen = jnp.take(seen, jnp.array([p % XS for p in PIECES]), axis=1).reshape(YS, -1)

    padded = jnp.concatenate([jnp.full((TILE,), -1, jnp.int32), segment_ids])
    key_segments = lax.dynamic_slice_in_dim(padded, device * TILE, 2 * TILE, 0)
    row_segments = key_segments[TILE:]
    key_places = jnp.arange(2 * TILE, dtype=jnp.int32) - TILE
    row_places = jnp.arange(TILE, dtype=jnp.int32)
    visible = (key_segments[None, :] == row_segments[:, None]) & (
        key_places[None, :] <= row_places[:, None]
    )
    bias = jnp.where(visible, 0.0, NEG_FILL).astype(jnp.float32)

    others = []
    for step, other_q in zip(steps, qs):
        part = attend(seen[step % YS], other_q, pieces)
        others.append(shifted(part, "y", -step))
    own = attend(seen[0], q, pieces, (prev, rkv, bias))

    sign = 1 - 2 * core
    offsets = jnp.array([-4, -2, 3, 1, -3, -1, 2, 0], jnp.int32)
    idx = (z + sign * offsets) % ZS
    one, two, att = project_first(idx, own, others, weight)
    got_one = along_z(one, -1)
    got_two = along_z(two, 1)
    rest = project_second(idx, att, weight)
    back3 = along_z((rest[0] + got_one[0].astype(jnp.float32)).astype(jnp.bfloat16), -3)
    on2 = along_z((rest[2] + got_two[0].astype(jnp.float32)).astype(jnp.bfloat16), 2)
    back1 = along_z((rest[1] + got_one[1].astype(jnp.float32)).astype(jnp.bfloat16), -1)
    total = rest[3] + got_two[1].astype(jnp.float32)
    for part in (back1, on2, back3):
        total = total + part.astype(jnp.float32)
    return total.astype(jnp.bfloat16)


def solution(mesh):
    split = Mesh(mesh.devices.reshape(XS, YS, CORES, ZS), ("x", "y", "core", "z"))
    seq = ("x", "y", "core")
    placed = (P(seq, "z"),) * 5 + (P("z", None), P(), P())
    return jax.shard_map(
        body, mesh=split, in_specs=placed, out_specs=P(seq, "z"), check_vma=False
    )
```

```python
import functools
import math

import jax
import jax.numpy as jnp
from jax import lax
from jax.experimental import pallas as pl
from jax.experimental.pallas import tpu as pltpu
from jax.sharding import Mesh, PartitionSpec as P

H = 64
KVH = 8
CW = 128
TILE = 128
HEADS = H // KVH
XS, YS, CORES, ZS = 4, 4, 2, 8
X_STEPS = (0, 1, -1, 2)
Q_STEPS = (2, 1, -1)
PIECE = 512
PIECES = CORES * len(X_STEPS)
BLOCK = 256
NEG_FILL = -1e30
SCALE2 = math.log2(math.e) / math.sqrt(CW)
STATS = 3
QUIET = 64.0
QROWS = HEADS * TILE
OUT_BLOCK = 640


def seq_index(x, y, c):
    return (lax.rem(x, XS) * YS + lax.rem(y, YS)) * CORES + c


def shifted(block, axis, step):
    n = lax.axis_size(axis)
    return lax.ppermute(block, axis, [((i + step) % n, i) for i in range(n)])


def prepare_kernel(mask_hbm, seg_hbm, pk_ref, pv_ref, rk_ref, rv_ref, kv_ref, rkv_ref, bias_ref, *refs):
    flag_refs, (mask_ref, seg_ref, sems) = refs[:4], refs[4:]
    x, y, core = (lax.axis_index(a) for a in ("x", "y", "core"))
    copies = [
        pltpu.make_async_copy(source, target, sems.at[i])
        for i, (source, target) in enumerate(
            (
                (mask_hbm, mask_ref),
                (seg_hbm, seg_ref),
                (pk_ref, kv_ref.at[:, :CW]),
                (pv_ref, kv_ref.at[:, CW:]),
                (rk_ref, rkv_ref.at[:, :CW]),
                (rv_ref, rkv_ref.at[:, CW:]),
            )
        )
    ]
    for copy in copies:
        copy.start()
    for copy in copies:
        copy.wait()
    tiles = PIECE // TILE
    for flags, dy in zip(flag_refs, (0, *Q_STEPS)):
        row = seq_index(x, y + dy + YS, core)
        for p in range(PIECES):
            dx = X_STEPS[p % len(X_STEPS)]
            first = seq_index(x + dx + XS, y, core if p < len(X_STEPS) else 1 - core) * tiles
            for t in range(tiles):
                flags[p * tiles + t] = mask_ref[row, first + t]
    device = seq_index(x, y, core)
    mine = seg_ref[pl.ds(device, 1), :]
    before = seg_ref[pl.ds(jnp.maximum(device - 1, 0), 1), :]
    before = jnp.where(device > 0, before, -1)
    rows = jnp.broadcast_to(mine, (TILE, TILE)).T
    r = lax.broadcasted_iota(jnp.int32, (TILE, TILE), 0)
    c = lax.broadcasted_iota(jnp.int32, (TILE, TILE), 1)
    bias_ref[:, :TILE] = jnp.where(rows == before, 0.0, NEG_FILL)
    bias_ref[:, TILE:] = jnp.where((rows == mine) & (c <= r), 0.0, NEG_FILL)


def prepare(block_mask, segment_ids, pkeys, pvalues, rkeys, rvalues):
    vmem = pl.BlockSpec(memory_space=pltpu.VMEM)
    smem = pl.BlockSpec(memory_space=pltpu.SMEM)
    flags = jax.ShapeDtypeStruct((PIECES * PIECE // TILE,), jnp.int32)
    return pl.pallas_call(
        prepare_kernel,
        out_shape=[
            jax.ShapeDtypeStruct((pkeys.shape[0], 2 * CW), jnp.bfloat16),
            jax.ShapeDtypeStruct((TILE, 2 * CW), jnp.bfloat16),
            jax.ShapeDtypeStruct((TILE, 2 * TILE), jnp.float32),
        ]
        + [flags] * 4,
        in_specs=[pl.BlockSpec(memory_space=pltpu.HBM)] * 6,
        out_specs=[vmem] * 3 + [smem] * 4,
        scratch_shapes=[
            pltpu.SMEM(block_mask.shape, jnp.int32),
            pltpu.VMEM((segment_ids.shape[0] // TILE, TILE), jnp.int32),
            pltpu.SemaphoreType.DMA((6,)),
        ],
        compiler_params=pltpu.CompilerParams(vmem_limit_bytes=8 << 20),
        name="prepare",
    )(
        *(
            pltpu.with_memory_space_constraint(a, pltpu.HBM)
            for a in (block_mask, segment_ids.reshape(-1, TILE), pkeys, pvalues, rkeys, rvalues)
        )
    )


def split_three(value):
    parts = []
    for _ in range(STATS):
        parts.append(value.astype(jnp.bfloat16).astype(jnp.float32))
        value = value - parts[-1]
    return parts


def attend_kernel(own, early, flags_ref, q_ref, *refs):
    kv_refs, refs = refs[:PIECES], refs[PIECES:]
    if own:
        (prev_ref, mine_ref, bias_ref), refs = refs[:3], refs[3:]
    elif early:
        refs = refs[1:]
    out_ref, kv_s, q_s, m_s, acc_s, list_s, again_s = refs
    tiles = PIECE // TILE
    lanes = lax.broadcasted_iota(jnp.int32, (TILE, CW), 1)

    count = 0
    for piece in range(PIECES):
        for b in range(tiles // 2):
            block = piece * (tiles // 2) + b
            seen = flags_ref[2 * block] + flags_ref[2 * block + 1] > 0
            list_s[count] = block

            @pl.when(seen)
            def _():
                rows = slice(block * BLOCK, (block + 1) * BLOCK)
                kv_s[rows, : 2 * CW] = kv_refs[piece][b * BLOCK : (b + 1) * BLOCK]
                kv_s[rows, 2 * CW :] = jnp.ones((BLOCK, CW), jnp.bfloat16)

            count = count + jnp.where(seen, 1, 0)
    last = PIECES * PIECE
    if own:
        kv_s[last : last + TILE, : 2 * CW] = prev_ref[...]
        kv_s[last + TILE :, : 2 * CW] = mine_ref[...]
        kv_s[last:, 2 * CW :] = jnp.ones((BLOCK, CW), jnp.bfloat16)
    for h in range(HEADS):
        q_s[h * TILE : (h + 1) * TILE, :] = q_ref[:, h * CW : (h + 1) * CW]

    def rows_of(i):
        return pl.ds(pl.multiple_of(list_s[i] * BLOCK, BLOCK), BLOCK)

    def joined(parts, axis):
        return parts[0] if len(parts) == 1 else jnp.concatenate(parts, axis=axis)

    def scores(first, size):
        k = joined([kv_s[rows_of(first + i), :CW] for i in range(size)], 0)
        s = lax.dot_general(q_s[...], k, (((1,), (1,)), ((), ())), preferred_element_type=jnp.float32)
        halves = []
        for i in range(size):
            b = list_s[first + i]
            for t in range(2):
                bias = jnp.where(flags_ref[2 * b + t] > 0, 0.0, NEG_FILL)
                at = 2 * i + t
                halves.append(s[:, at * TILE : (at + 1) * TILE] * SCALE2 + bias)
        return halves

    def own_scores():
        s = lax.dot_general(q_s[...], kv_s[last:, :CW], (((1,), (1,)), ((), ())), preferred_element_type=jnp.float32)
        s = (s.reshape(HEADS, TILE, BLOCK) * SCALE2 + bias_ref[...][None]).reshape(QROWS, BLOCK)
        return [s[:, :TILE], s[:, TILE:]]

    def top_of(halves):
        m = jnp.max(functools.reduce(jnp.maximum, halves), axis=1, keepdims=True)
        return jnp.broadcast_to(m, (QROWS, TILE))

    def weigh(halves, v):
        m = m_s[...]
        p = jnp.concatenate([jnp.exp2(s - m).astype(jnp.bfloat16) for s in halves], axis=1)
        return jnp.dot(p, v, preferred_element_type=jnp.float32)

    def absorb(first, size):
        v = joined([kv_s[rows_of(first + i), CW:] for i in range(size)], 0)
        acc_s[...] += weigh(scores(first, size), v)

    def attempt(a, _):
        @pl.when(jnp.logical_or(a == 0, again_s[0] == 1))
        def _():
            @pl.when(a == 0)
            def _():
                m_s[...] = jnp.zeros_like(m_s)

            @pl.when(a == 1)
            def _():
                m_s[...] = top_of(own_scores()) if own else jnp.full_like(m_s, NEG_FILL)

                def top(i, _):
                    m_s[...] = jnp.maximum(m_s[...], top_of(scores(i, 1)))
                    return 0

                lax.fori_loop(0, count, top, 0)

            acc_s[...] = weigh(own_scores(), kv_s[last:, CW:]) if own else jnp.zeros_like(acc_s)
            done = 0
            for size in (4, 2, 1):

                def group(j, _, size=size, done=done):
                    absorb(done + j * size, size)
                    return 0

                loops = (count - done) // size
                lax.fori_loop(0, loops, group, 0)
                done = done + loops * size
            raw = acc_s[:, CW:]
            total = jnp.maximum(raw, 1e-30)
            inverse = 1.0 / total
            log_total = jnp.log2(total)
            loud = jnp.max(jnp.abs(log_total)) > QUIET
            if not own:
                loud = jnp.logical_and(loud, count > 0)
            again_s[0] = jnp.where(loud, 1, 0)
            lse = m_s[...] + log_total
            if not own:
                lse = jnp.where(raw > 0, lse, NEG_FILL)
            head = lanes // STATS
            stats = lse[:TILE]
            for h in range(HEADS):
                rows = slice(h * TILE, (h + 1) * TILE)
                out_ref[:, h * CW : (h + 1) * CW] = (acc_s[rows, :CW] * inverse[rows]).astype(out_ref.dtype)
                stats = jnp.where(head == h, lse[rows], stats)
            if not own:
                a_, b_, c_ = split_three(stats)
                which = lanes % STATS
                stats = jnp.where(which == 0, a_, jnp.where(which == 1, b_, c_))
            out_ref[:, HEADS * CW :] = stats.astype(out_ref.dtype)
        return 0

    lax.fori_loop(0, 2, attempt, 0)


def attend(flags, q, pieces, own_parts=None, early=None):
    own = own_parts is not None
    args = [flags, q, *pieces, *(own_parts or ())]
    vmem = pl.BlockSpec(memory_space=pltpu.VMEM)
    keys = PIECES * PIECE + BLOCK * own
    return pl.pallas_call(
        functools.partial(attend_kernel, own, early is not None),
        out_shape=jax.ShapeDtypeStruct(
            (TILE, HEADS * CW + CW), jnp.float32 if own else jnp.bfloat16
        ),
        in_specs=[pl.BlockSpec(memory_space=pltpu.SMEM)]
        + [vmem] * (len(args) - 1)
        + [pl.BlockSpec(memory_space=pl.ANY)] * (early is not None),
        out_specs=vmem,
        scratch_shapes=[
            pltpu.VMEM((keys, 3 * CW), jnp.bfloat16),
            pltpu.VMEM((QROWS, CW), jnp.bfloat16),
            pltpu.VMEM((QROWS, TILE), jnp.float32),
            pltpu.VMEM((QROWS, 2 * CW), jnp.float32),
            pltpu.SMEM((keys // BLOCK + 1,), jnp.int32),
            pltpu.SMEM((1,), jnp.int32),
        ],
        compiler_params=pltpu.CompilerParams(vmem_limit_bytes=24 << 20),
        cost_estimate=pl.CostEstimate(
            flops=QROWS * 1024 * CW * 4, bytes_accessed=2 << 20, transcendentals=QROWS * 1024
        ),
        name="attend_own" if own else "attend_other",
    )(*args, *([] if early is None else [early]))


def combine(refs, att_s):
    stats = [r[:, HEADS * CW :].astype(jnp.float32) for r in refs]
    for h in range(HEADS):
        cols = slice(h * CW, (h + 1) * CW)
        i = STATS * h
        lses = [stats[0][:, i : i + 1]]
        for st in stats[1:]:
            lses.append(st[:, i : i + 1] + st[:, i + 1 : i + 2] + st[:, i + 2 : i + 3])
        top = functools.reduce(jnp.maximum, lses)
        weights = [jnp.exp2(v - top) for v in lses]
        inverse = 1.0 / sum(weights)
        mixed = sum(r[:, cols].astype(jnp.float32) * (w * inverse) for r, w in zip(refs, weights))
        att_s[:, cols] = mixed.astype(jnp.bfloat16)


def project_kernel(first, idx_ref, *refs):
    if first:
        own_ref, a_ref, b_ref, c_ref, w_ref, one_ref, two_ref, att_ref, w_s, sems = refs
    else:
        att_ref, w_ref, out_ref, w_s, sems = refs
    copies = []
    for j in range(4):
        start = pl.multiple_of(idx_ref[j if first else j + 4] * OUT_BLOCK, CW)
        copies.append(
            pltpu.make_async_copy(w_ref.at[:, pl.ds(start, OUT_BLOCK)], w_s.at[j], sems.at[j])
        )
        copies[-1].start()
    if first:
        combine((own_ref, a_ref, b_ref, c_ref), att_ref)
    for j in range(4):
        copies[j].wait()
        term = jnp.dot(att_ref[...], w_s[j], preferred_element_type=jnp.float32)
        if first:
            (one_ref, two_ref)[j // 2][j % 2] = term.astype(jnp.bfloat16)
        else:
            out_ref[j] = term


def project(idx, parts, weight):
    first = len(parts) > 1
    rows, width = TILE, HEADS * CW
    vmem = pl.BlockSpec(memory_space=pltpu.VMEM)
    pair = jax.ShapeDtypeStruct((2, rows, OUT_BLOCK), jnp.bfloat16)
    if first:
        out_shape = [pair, pair, jax.ShapeDtypeStruct((rows, width), jnp.bfloat16)]
    else:
        out_shape = [jax.ShapeDtypeStruct((4, rows, OUT_BLOCK), jnp.float32)]
    return pl.pallas_call(
        functools.partial(project_kernel, first),
        out_shape=out_shape,
        in_specs=[pl.BlockSpec(memory_space=pltpu.SMEM)]
        + [vmem] * len(parts)
        + [pl.BlockSpec(memory_space=pltpu.HBM)],
        out_specs=[vmem] * len(out_shape),
        scratch_shapes=[
            pltpu.VMEM((4, width, OUT_BLOCK), jnp.bfloat16),
            pltpu.SemaphoreType.DMA((4,)),
        ],
        compiler_params=pltpu.CompilerParams(vmem_limit_bytes=20 << 20),
        cost_estimate=pl.CostEstimate(
            flops=2 * rows * width * OUT_BLOCK * 4, bytes_accessed=6 << 20, transcendentals=0
        ),
        name="project_first" if first else "project_second",
    )(idx, *parts, pltpu.with_memory_space_constraint(weight, pltpu.HBM))


def along_z(block, step):
    route = [
        (c * ZS + z, c * ZS + (z + (step if c == 0 else -step)) % ZS)
        for c in range(CORES)
        for z in range(ZS)
    ]
    return lax.ppermute(block, ("core", "z"), route)


def body(q, rkeys, rvalues, pkeys, pvalues, weight, segment_ids, block_mask):
    core, z = lax.axis_index("core"), lax.axis_index("z")
    qs = [shifted(q, "y", step) for step in Q_STEPS]
    kv, rkv, bias, *seen = prepare(block_mask, segment_ids, pkeys, pvalues, rkeys, rvalues)
    kvs = [kv] + [shifted(kv, "x", step) for step in X_STEPS[1:]]
    route = [(seq, seq + 1) for seq in range(XS * YS * CORES - 1)]
    prev = lax.ppermute(rkv, ("x", "y", "core"), route)
    pieces = kvs + [shifted(p, "core", 1) for p in kvs]

    others = []
    for step, other_q, flags in zip(Q_STEPS, qs, seen[1:]):
        early = prev if step == Q_STEPS[1] else None
        others.append(shifted(attend(flags, other_q, pieces, early=early), "y", -step))
    own = attend(seen[0], q, pieces, (prev, rkv, bias))

    sign = 1 - 2 * core
    idx = jnp.stack([(z + sign * o) % ZS for o in (-4, -2, 3, 1, -3, -1, 2, 0)]).astype(jnp.int32)
    one, two, att = project(idx, [own, *others], weight)
    got_one = along_z(one, -1)
    got_two = along_z(two, 1)
    (rest,) = project(idx, [att], weight)
    back3 = along_z((rest[0] + got_one[0].astype(jnp.float32)).astype(jnp.bfloat16), -3)
    on2 = along_z((rest[2] + got_two[0].astype(jnp.float32)).astype(jnp.bfloat16), 2)
    back1 = along_z((rest[1] + got_one[1].astype(jnp.float32)).astype(jnp.bfloat16), -1)
    total = rest[3] + got_two[1].astype(jnp.float32)
    for part in (back1, on2, back3):
        total = total + part.astype(jnp.float32)
    return total.astype(jnp.bfloat16)


def solution(mesh):
    split = Mesh(mesh.devices.reshape(XS, YS, CORES, ZS), ("x", "y", "core", "z"))
    seq = ("x", "y", "core")
    placed = (P(seq, "z"),) * 5 + (P("z", None), P(), P())
    return jax.shard_map(
        body, mesh=split, in_specs=placed, out_specs=P(seq, "z"), check_vma=False
    )
```

```python
import functools
import math

import jax
import jax.numpy as jnp
from jax import lax
from jax.experimental import pallas as pl
from jax.experimental.pallas import tpu as pltpu
from jax.sharding import Mesh, PartitionSpec as P

H = 64
KVH = 8
CW = 128
TILE = 128
HEADS = H // KVH
XS, YS, CORES, ZS = 4, 4, 2, 8
SHARE = 512
SHARES = XS * CORES
BLOCK = 256
NEG_FILL = -1e30
SCALE2 = math.log2(math.e) / math.sqrt(CW)
STATS = 3
QUIET = 64.0
QROWS = HEADS * TILE
OUT_BLOCK = 640


def seq_index(x, y, c):
    return (lax.rem(x, XS) * YS + lax.rem(y, YS)) * CORES + c


def shifted(block, axis, step):
    n = lax.axis_size(axis)
    return lax.ppermute(block, axis, [((i + step) % n, i) for i in range(n)])


def prepare_kernel(
    mask_hbm, seg_hbm, pk_ref, pv_ref, rk_ref, rv_ref, q_hbm, kv_ref, rkv_ref, bias_ref, q_ref, *refs
):
    flag_refs, (mask_ref, seg_ref, sems) = refs[:4], refs[4:]
    x, y, core = (lax.axis_index(a) for a in ("x", "y", "core"))
    copies = [
        pltpu.make_async_copy(source, target, sems.at[i])
        for i, (source, target) in enumerate(
            (
                (mask_hbm, mask_ref),
                (seg_hbm, seg_ref),
                (pk_ref, kv_ref.at[:, :CW]),
                (pv_ref, kv_ref.at[:, CW:]),
                (rk_ref, rkv_ref.at[:, :CW]),
                (rv_ref, rkv_ref.at[:, CW:]),
            )
            + tuple(
                (q_hbm.at[:, i : i + 2 * CW], q_ref.at[i // 2 : i // 2 + TILE])
                for i in range(0, HEADS * CW, 2 * CW)
            )
        )
    ]
    for copy in copies:
        copy.start()
    for copy in copies:
        copy.wait()
    tiles = SHARE // TILE
    step = XS + 1 - 2 * core
    back = XS - 1 + 2 * core
    other = 1 - core
    shares = (
        (0, core), (0, other), (2, core), (2, other),
        (step, core), (step, other), (back, other), (back, core),
    )
    for flags, dy in zip(flag_refs, (0, 2, 1 - 2 * core, 2 * core - 1)):
        row = seq_index(x, y + dy + YS, core)
        for p, (dx, c) in enumerate(shares):
            first = seq_index(x + dx, y, c) * tiles
            for t in range(tiles):
                flags[p * tiles + t] = mask_ref[row, first + t]
    device = seq_index(x, y, core)
    mine = seg_ref[pl.ds(device, 1), :]
    before = seg_ref[pl.ds(jnp.maximum(device - 1, 0), 1), :]
    before = jnp.where(device > 0, before, -1)
    rows = jnp.broadcast_to(mine, (TILE, TILE)).T
    r = lax.broadcasted_iota(jnp.int32, (TILE, TILE), 0)
    c = lax.broadcasted_iota(jnp.int32, (TILE, TILE), 1)
    bias_ref[:, :TILE] = jnp.where(rows == before, 0.0, NEG_FILL)
    bias_ref[:, TILE:] = jnp.where((rows == mine) & (c <= r), 0.0, NEG_FILL)


def prepare(block_mask, segment_ids, pkeys, pvalues, rkeys, rvalues, q):
    vmem = pl.BlockSpec(memory_space=pltpu.VMEM)
    smem = pl.BlockSpec(memory_space=pltpu.SMEM)
    flags = jax.ShapeDtypeStruct((SHARES * SHARE // TILE,), jnp.int32)
    return pl.pallas_call(
        prepare_kernel,
        out_shape=[
            jax.ShapeDtypeStruct((pkeys.shape[0], 2 * CW), jnp.bfloat16),
            jax.ShapeDtypeStruct((TILE, 2 * CW), jnp.bfloat16),
            jax.ShapeDtypeStruct((TILE, 2 * TILE), jnp.float32),
            jax.ShapeDtypeStruct((QROWS // 2, 2 * CW), q.dtype),
        ]
        + [flags] * 4,
        in_specs=[pl.BlockSpec(memory_space=pltpu.HBM)] * 7,
        out_specs=[vmem] * 4 + [smem] * 4,
        scratch_shapes=[
            pltpu.SMEM(block_mask.shape, jnp.int32),
            pltpu.VMEM((segment_ids.shape[0] // TILE, TILE), jnp.int32),
            pltpu.SemaphoreType.DMA((10,)),
        ],
        compiler_params=pltpu.CompilerParams(vmem_limit_bytes=8 << 20),
        cost_estimate=pl.CostEstimate(flops=1, bytes_accessed=1, transcendentals=0),
        name="prepare",
    )(
        *(
            pltpu.with_memory_space_constraint(a, pltpu.HBM)
            for a in (block_mask, segment_ids.reshape(-1, TILE), pkeys, pvalues, rkeys, rvalues, q)
        )
    )


def pair_kernel(*refs):
    for i in range(2):
        a_ref, b_ref, out_ref = refs[2 * i], refs[2 * i + 1], refs[4 + i]
        rows = a_ref.shape[0]
        out_ref[:rows] = a_ref[...]
        out_ref[rows:] = b_ref[...]


def paired(*arrays):
    vmem = pl.BlockSpec(memory_space=pltpu.VMEM)
    return pl.pallas_call(
        pair_kernel,
        out_shape=[pltpu.VMEM((2 * a.shape[0], a.shape[1]), a.dtype) for a in arrays[::2]],
        in_specs=[vmem] * 4,
        out_specs=[vmem] * 2,
        compiler_params=pltpu.CompilerParams(vmem_limit_bytes=4 << 20),
        cost_estimate=pl.CostEstimate(flops=1, bytes_accessed=1, transcendentals=0),
        name="paired",
    )(*arrays)


def split_three(value):
    parts = []
    for _ in range(STATS):
        parts.append(value.astype(jnp.bfloat16).astype(jnp.float32))
        value = value - parts[-1]
    return parts


def opposite(block, axis, step):
    n = lax.axis_size(axis)
    route = [
        (((i + (step if c == 0 else -step)) % n) * CORES + c, i * CORES + c)
        for i in range(n)
        for c in range(CORES)
    ]
    return lax.ppermute(block, (axis, "core"), route)


def attend_kernel(own, first, early, flags_ref, q_ref, *refs):
    kv_refs, refs = refs[:5], refs[5:]
    if own:
        (prev_ref, mine_ref, bias_ref), refs = refs[:3], refs[3:]
    refs = refs[early:]
    out_ref, kv_s, q_s, m_s, acc_s, list_s, again_s = refs
    lanes = lax.broadcasted_iota(jnp.int32, (TILE, CW), 1)

    count = 0
    block = 0
    for ref in kv_refs:
        for b in range(ref.shape[0] // BLOCK):
            seen = flags_ref[2 * block] + flags_ref[2 * block + 1] > 0
            list_s[count] = block

            @pl.when(seen)
            def _():
                rows = slice(block * BLOCK, (block + 1) * BLOCK)
                kv_s[rows, : 2 * CW] = ref[b * BLOCK : (b + 1) * BLOCK]
                kv_s[rows, 2 * CW :] = jnp.ones((BLOCK, CW), jnp.bfloat16)

            count = count + jnp.where(seen, 1, 0)
            block += 1
    last = SHARES * SHARE
    if own:
        kv_s[last : last + TILE, : 2 * CW] = prev_ref[...]
        kv_s[last + TILE :, : 2 * CW] = mine_ref[...]
        kv_s[last:, 2 * CW :] = jnp.ones((BLOCK, CW), jnp.bfloat16)
    for h in range(HEADS):
        at = first + h // 2 * TILE
        q_s[h * TILE : (h + 1) * TILE, :] = q_ref[at : at + TILE, h % 2 * CW : (h % 2 + 1) * CW]

    def rows_of(i):
        return pl.ds(pl.multiple_of(list_s[i] * BLOCK, BLOCK), BLOCK)

    def joined(parts, axis):
        return parts[0] if len(parts) == 1 else jnp.concatenate(parts, axis=axis)

    def scores(first, size):
        k = joined([kv_s[rows_of(first + i), :CW] for i in range(size)], 0)
        s = lax.dot_general(q_s[...], k, (((1,), (1,)), ((), ())), preferred_element_type=jnp.float32)
        halves = []
        for i in range(size):
            b = list_s[first + i]
            for t in range(2):
                bias = jnp.where(flags_ref[2 * b + t] > 0, 0.0, NEG_FILL)
                at = 2 * i + t
                halves.append(s[:, at * TILE : (at + 1) * TILE] * SCALE2 + bias)
        return halves

    def own_scores():
        s = lax.dot_general(q_s[...], kv_s[last:, :CW], (((1,), (1,)), ((), ())), preferred_element_type=jnp.float32)
        s = (s.reshape(HEADS, TILE, BLOCK) * SCALE2 + bias_ref[...][None]).reshape(QROWS, BLOCK)
        return [s[:, :TILE], s[:, TILE:]]

    def top_of(halves):
        m = jnp.max(functools.reduce(jnp.maximum, halves), axis=1, keepdims=True)
        return jnp.broadcast_to(m, (QROWS, TILE))

    def weigh(halves, v):
        m = m_s[...]
        p = jnp.concatenate([jnp.exp2(s - m).astype(jnp.bfloat16) for s in halves], axis=1)
        return jnp.dot(p, v, preferred_element_type=jnp.float32)

    def absorb(first, size):
        v = joined([kv_s[rows_of(first + i), CW:] for i in range(size)], 0)
        acc_s[...] += weigh(scores(first, size), v)

    def attempt(a, _):
        @pl.when(jnp.logical_or(a == 0, again_s[0] == 1))
        def _():
            @pl.when(a == 0)
            def _():
                m_s[...] = jnp.zeros_like(m_s)

            @pl.when(a == 1)
            def _():
                m_s[...] = top_of(own_scores()) if own else jnp.full_like(m_s, NEG_FILL)

                def top(i, _):
                    m_s[...] = jnp.maximum(m_s[...], top_of(scores(i, 1)))
                    return 0

                lax.fori_loop(0, count, top, 0)

            acc_s[...] = weigh(own_scores(), kv_s[last:, CW:]) if own else jnp.zeros_like(acc_s)
            done = 0
            for size in (4, 2, 1):

                def group(j, _, size=size, done=done):
                    absorb(done + j * size, size)
                    return 0

                loops = (count - done) // size
                lax.fori_loop(0, loops, group, 0)
                done = done + loops * size
            raw = acc_s[:, CW:]
            total = jnp.maximum(raw, 1e-30)
            inverse = 1.0 / total
            log_total = jnp.log2(total)
            loud = jnp.max(jnp.abs(log_total)) > QUIET
            if not own:
                loud = jnp.logical_and(loud, count > 0)
            again_s[0] = jnp.where(loud, 1, 0)
            lse = m_s[...] + log_total
            if not own:
                lse = jnp.where(raw > 0, lse, NEG_FILL)
            head = lanes // STATS
            stats = lse[:TILE]
            for h in range(HEADS):
                rows = slice(h * TILE, (h + 1) * TILE)
                out_ref[:, h * CW : (h + 1) * CW] = (acc_s[rows, :CW] * inverse[rows]).astype(out_ref.dtype)
                stats = jnp.where(head == h, lse[rows], stats)
            if not own:
                a_, b_, c_ = split_three(stats)
                which = lanes % STATS
                stats = jnp.where(which == 0, a_, jnp.where(which == 1, b_, c_))
            out_ref[:, HEADS * CW :] = stats.astype(out_ref.dtype)
        return 0

    lax.fori_loop(0, 2, attempt, 0)


def attend(flags, q, pieces, own_parts=None, first=0, early=None):
    own = own_parts is not None
    args = [flags, q, *pieces, *(own_parts or ())]
    vmem = pl.BlockSpec(memory_space=pltpu.VMEM)
    keys = SHARES * SHARE + BLOCK * own
    return pl.pallas_call(
        functools.partial(attend_kernel, own, first, early is not None),
        out_shape=pltpu.VMEM((TILE, HEADS * CW + CW), jnp.float32 if own else jnp.bfloat16),
        in_specs=[pl.BlockSpec(memory_space=pltpu.SMEM)]
        + [vmem] * (len(args) - 1)
        + [pl.BlockSpec(memory_space=pl.ANY)] * (early is not None),
        out_specs=vmem,
        scratch_shapes=[
            pltpu.VMEM((keys, 3 * CW), jnp.bfloat16),
            pltpu.VMEM((QROWS, CW), jnp.bfloat16),
            pltpu.VMEM((QROWS, TILE), jnp.float32),
            pltpu.VMEM((QROWS, 2 * CW), jnp.float32),
            pltpu.SMEM((keys // BLOCK + 1,), jnp.int32),
            pltpu.SMEM((1,), jnp.int32),
        ],
        compiler_params=pltpu.CompilerParams(vmem_limit_bytes=24 << 20),
        cost_estimate=pl.CostEstimate(flops=1, bytes_accessed=1, transcendentals=0),
        name="attend_own" if own else "attend_other",
    )(*args, *([] if early is None else [early]))


def combine(refs, att_s):
    stats = [r[:, HEADS * CW :].astype(jnp.float32) for r in refs]
    for h in range(HEADS):
        cols = slice(h * CW, (h + 1) * CW)
        i = STATS * h
        lses = [stats[0][:, i : i + 1]]
        for st in stats[1:]:
            lses.append(st[:, i : i + 1] + st[:, i + 1 : i + 2] + st[:, i + 2 : i + 3])
        top = functools.reduce(jnp.maximum, lses)
        weights = [jnp.exp2(v - top) for v in lses]
        inverse = 1.0 / sum(weights)
        mixed = sum(r[:, cols].astype(jnp.float32) * (w * inverse) for r, w in zip(refs, weights))
        att_s[:, cols] = mixed.astype(jnp.bfloat16)


def project_kernel(first, idx_ref, *refs):
    if first:
        own_ref, a_ref, b_ref, c_ref, w_ref, one_ref, two_ref, att_ref, w_s, sems = refs
    else:
        att_ref, w_ref, out_ref, w_s, sems = refs
    copies = []
    for j in range(4):
        start = pl.multiple_of(idx_ref[j if first else j + 4] * OUT_BLOCK, CW)
        copies.append(
            pltpu.make_async_copy(w_ref.at[:, pl.ds(start, OUT_BLOCK)], w_s.at[j], sems.at[j])
        )
        copies[-1].start()
    if first:
        combine((own_ref, a_ref, b_ref, c_ref), att_ref)
    for j in range(4):
        copies[j].wait()
        term = jnp.dot(att_ref[...], w_s[j], preferred_element_type=jnp.float32)
        if first:
            (one_ref, two_ref)[j // 2][j % 2] = term.astype(jnp.bfloat16)
        else:
            out_ref[j] = term


def project(idx, parts, weight):
    first = len(parts) > 1
    rows, width = TILE, HEADS * CW
    vmem = pl.BlockSpec(memory_space=pltpu.VMEM)
    pair = jax.ShapeDtypeStruct((2, rows, OUT_BLOCK), jnp.bfloat16)
    if first:
        out_shape = [pair, pair, jax.ShapeDtypeStruct((rows, width), jnp.bfloat16)]
    else:
        out_shape = [jax.ShapeDtypeStruct((4, rows, OUT_BLOCK), jnp.float32)]
    return pl.pallas_call(
        functools.partial(project_kernel, first),
        out_shape=out_shape,
        in_specs=[pl.BlockSpec(memory_space=pltpu.SMEM)]
        + [vmem] * len(parts)
        + [pl.BlockSpec(memory_space=pltpu.HBM)],
        out_specs=[vmem] * len(out_shape),
        scratch_shapes=[
            pltpu.VMEM((4, width, OUT_BLOCK), jnp.bfloat16),
            pltpu.SemaphoreType.DMA((4,)),
        ],
        compiler_params=pltpu.CompilerParams(vmem_limit_bytes=20 << 20),
        cost_estimate=pl.CostEstimate(
            flops=2 * rows * width * OUT_BLOCK * 4, bytes_accessed=6 << 20, transcendentals=0
        ),
        name="project_first" if first else "project_second",
    )(idx, *parts, pltpu.with_memory_space_constraint(weight, pltpu.HBM))


def along_z(block, step):
    route = [
        (c * ZS + z, c * ZS + (z + (step if c == 0 else -step)) % ZS)
        for c in range(CORES)
        for z in range(ZS)
    ]
    return lax.ppermute(block, ("core", "z"), route)


def body(q, rkeys, rvalues, pkeys, pvalues, weight, segment_ids, block_mask):
    core, z = lax.axis_index("core"), lax.axis_index("z")
    kv, rkv, bias, q, *seen = prepare(
        block_mask, segment_ids, pkeys, pvalues, rkeys, rvalues, q
    )
    far, far_q = shifted(kv, "x", 2), shifted(q, "y", 2)
    chip, chip_q = paired(kv, shifted(kv, "core", 1), q, shifted(q, "core", 1))
    near, near_q = opposite(chip, "x", 1), opposite(chip_q, "y", 1)
    pieces = [chip, far, shifted(far, "core", 1), near, shifted(near, "core", 1)]
    route = [(seq, seq + 1) for seq in range(XS * YS * CORES - 1)]
    prev = lax.ppermute(rkv, ("x", "y", "core"), route)

    others = [
        shifted(attend(seen[1], far_q, pieces), "y", 2),
        opposite(attend(seen[2], near_q, pieces), "y", -1),
        opposite(
            attend(seen[3], shifted(near_q, "core", 1), pieces, first=QROWS // 2, early=prev), "y", 1
        ),
    ]
    own = attend(seen[0], q, pieces, (prev, rkv, bias))

    sign = 1 - 2 * core
    idx = jnp.stack([(z + sign * o) % ZS for o in (-4, -2, 3, 1, -3, -1, 2, 0)]).astype(jnp.int32)
    one, two, att = project(idx, [own, *others], weight)
    got_one = along_z(one, -1)
    got_two = along_z(two, 1)
    (rest,) = project(idx, [att], weight)
    back3 = along_z((rest[0] + got_one[0].astype(jnp.float32)).astype(jnp.bfloat16), -3)
    on2 = along_z((rest[2] + got_two[0].astype(jnp.float32)).astype(jnp.bfloat16), 2)
    back1 = along_z((rest[1] + got_one[1].astype(jnp.float32)).astype(jnp.bfloat16), -1)
    total = rest[3] + got_two[1].astype(jnp.float32)
    for part in (back1, on2, back3):
        total = total + part.astype(jnp.float32)
    return total.astype(jnp.bfloat16)


def solution(mesh):
    split = Mesh(mesh.devices.reshape(XS, YS, CORES, ZS), ("x", "y", "core", "z"))
    seq = ("x", "y", "core")
    placed = (P(seq, "z"),) * 5 + (P("z", None), P(), P())
    return jax.shard_map(
        body, mesh=split, in_specs=placed, out_specs=P(seq, "z"), check_vma=False
    )
```

```python
import functools
import math

import jax
import jax.numpy as jnp
from jax import lax
from jax.experimental import pallas as pl
from jax.experimental.pallas import tpu as pltpu
from jax.sharding import Mesh, PartitionSpec as P

H = 64
KVH = 8
CW = 128
TILE = 128
HEADS = H // KVH
XS, YS, CORES, ZS = 4, 4, 2, 8
SHARE = 512
SHARES = XS * CORES
BLOCK = 256
NEG_FILL = -1e30
SCALE2 = math.log2(math.e) / math.sqrt(CW)
STATS = 3
QUIET = 64.0
QROWS = HEADS * TILE
OUT_BLOCK = 640


def seq_index(x, y, c):
    return (lax.rem(x, XS) * YS + lax.rem(y, YS)) * CORES + c


def shifted(block, axis, step):
    n = lax.axis_size(axis)
    return lax.ppermute(block, axis, [((i + step) % n, i) for i in range(n)])


def prepare_kernel(
    mask_hbm, seg_hbm, pk_ref, pv_ref, rk_ref, rv_ref, q_hbm, kv_ref, rkv_ref, bias_ref, q_ref, *refs
):
    flag_refs, (mask_ref, seg_ref, sems) = refs[:4], refs[4:]
    x, y, core = (lax.axis_index(a) for a in ("x", "y", "core"))
    copies = [
        pltpu.make_async_copy(source, target, sems.at[i])
        for i, (source, target) in enumerate(
            (
                (mask_hbm, mask_ref),
                (seg_hbm, seg_ref),
                (pk_ref, kv_ref.at[:, :CW]),
                (pv_ref, kv_ref.at[:, CW:]),
                (rk_ref, rkv_ref.at[:, :CW]),
                (rv_ref, rkv_ref.at[:, CW:]),
            )
            + tuple(
                (q_hbm.at[:, i : i + 2 * CW], q_ref.at[i // 2 : i // 2 + TILE])
                for i in range(0, HEADS * CW, 2 * CW)
            )
        )
    ]
    for copy in copies:
        copy.start()
    for copy in copies:
        copy.wait()
    tiles = SHARE // TILE
    step = XS + 1 - 2 * core
    back = XS - 1 + 2 * core
    other = 1 - core
    shares = (
        (0, core), (0, other), (2, core), (2, other),
        (step, core), (step, other), (back, other), (back, core),
    )
    for flags, dy in zip(flag_refs, (0, 2, 1 - 2 * core, 2 * core - 1)):
        row = seq_index(x, y + dy + YS, core)
        for p, (dx, c) in enumerate(shares):
            first = seq_index(x + dx, y, c) * tiles
            for t in range(tiles):
                flags[p * tiles + t] = mask_ref[row, first + t]
    device = seq_index(x, y, core)
    mine = seg_ref[pl.ds(device, 1), :]
    before = seg_ref[pl.ds(jnp.maximum(device - 1, 0), 1), :]
    before = jnp.where(device > 0, before, -1)
    rows = jnp.broadcast_to(mine, (TILE, TILE)).T
    r = lax.broadcasted_iota(jnp.int32, (TILE, TILE), 0)
    c = lax.broadcasted_iota(jnp.int32, (TILE, TILE), 1)
    bias_ref[:, :TILE] = jnp.where(rows == before, 0.0, NEG_FILL)
    bias_ref[:, TILE:] = jnp.where((rows == mine) & (c <= r), 0.0, NEG_FILL)


def prepare(block_mask, segment_ids, pkeys, pvalues, rkeys, rvalues, q):
    vmem = pl.BlockSpec(memory_space=pltpu.VMEM)
    smem = pl.BlockSpec(memory_space=pltpu.SMEM)
    flags = jax.ShapeDtypeStruct((SHARES * SHARE // TILE,), jnp.int32)
    return pl.pallas_call(
        prepare_kernel,
        out_shape=[
            jax.ShapeDtypeStruct((pkeys.shape[0], 2 * CW), jnp.bfloat16),
            jax.ShapeDtypeStruct((TILE, 2 * CW), jnp.bfloat16),
            jax.ShapeDtypeStruct((TILE, 2 * TILE), jnp.float32),
            jax.ShapeDtypeStruct((QROWS // 2, 2 * CW), q.dtype),
        ]
        + [flags] * 4,
        in_specs=[pl.BlockSpec(memory_space=pltpu.HBM)] * 7,
        out_specs=[vmem] * 4 + [smem] * 4,
        scratch_shapes=[
            pltpu.SMEM(block_mask.shape, jnp.int32),
            pltpu.VMEM((segment_ids.shape[0] // TILE, TILE), jnp.int32),
            pltpu.SemaphoreType.DMA((10,)),
        ],
        compiler_params=pltpu.CompilerParams(vmem_limit_bytes=8 << 20),
        cost_estimate=pl.CostEstimate(flops=1, bytes_accessed=1, transcendentals=0),
        name="prepare",
    )(
        *(
            pltpu.with_memory_space_constraint(a, pltpu.HBM)
            for a in (block_mask, segment_ids.reshape(-1, TILE), pkeys, pvalues, rkeys, rvalues, q)
        )
    )


def pair_kernel(*refs):
    for i in range(2):
        a_ref, b_ref, out_ref = refs[2 * i], refs[2 * i + 1], refs[4 + i]
        rows = a_ref.shape[0]
        out_ref[:rows] = a_ref[...]
        out_ref[rows:] = b_ref[...]


def paired(*arrays):
    vmem = pl.BlockSpec(memory_space=pltpu.VMEM)
    return pl.pallas_call(
        pair_kernel,
        out_shape=[pltpu.VMEM((2 * a.shape[0], a.shape[1]), a.dtype) for a in arrays[::2]],
        in_specs=[vmem] * 4,
        out_specs=[vmem] * 2,
        compiler_params=pltpu.CompilerParams(vmem_limit_bytes=4 << 20),
        cost_estimate=pl.CostEstimate(flops=1, bytes_accessed=1, transcendentals=0),
        name="paired",
    )(*arrays)


def split_three(value):
    parts = []
    for _ in range(STATS):
        parts.append(value.astype(jnp.bfloat16).astype(jnp.float32))
        value = value - parts[-1]
    return parts


def opposite(block, axis, step):
    n = lax.axis_size(axis)
    route = [
        (((i + (step if c == 0 else -step)) % n) * CORES + c, i * CORES + c)
        for i in range(n)
        for c in range(CORES)
    ]
    return lax.ppermute(block, (axis, "core"), route)


def attend_kernel(own, first, early, flags_ref, q_ref, *refs):
    kv_refs, refs = refs[:5], refs[5:]
    if own:
        (prev_ref, mine_ref, bias_ref), refs = refs[:3], refs[3:]
    refs = refs[early:]
    out_ref, kv_s, q_s, m_s, acc_s, list_s, again_s = refs[:7]
    last = SHARES * SHARE
    copies = []
    if own:
        bias_s, sems = refs[7:]
        targets = (
            kv_s.at[last : last + TILE, : 2 * CW],
            kv_s.at[last + TILE : last + BLOCK, : 2 * CW],
            bias_s,
        )
        for i, (source, target) in enumerate(zip((prev_ref, mine_ref, bias_ref), targets)):
            copies.append(pltpu.make_async_copy(source, target, sems.at[i]))
            copies[-1].start()
    lanes = lax.broadcasted_iota(jnp.int32, (TILE, CW), 1)

    count = 0
    block = 0
    for ref in kv_refs:
        for b in range(ref.shape[0] // BLOCK):
            seen = flags_ref[2 * block] + flags_ref[2 * block + 1] > 0
            list_s[count] = block

            @pl.when(seen)
            def _():
                rows = slice(block * BLOCK, (block + 1) * BLOCK)
                kv_s[rows, : 2 * CW] = ref[b * BLOCK : (b + 1) * BLOCK]
                kv_s[rows, 2 * CW :] = jnp.ones((BLOCK, CW), jnp.bfloat16)

            count = count + jnp.where(seen, 1, 0)
            block += 1
    if own:
        kv_s[last:, 2 * CW :] = jnp.ones((BLOCK, CW), jnp.bfloat16)
    for h in range(HEADS):
        at = first + h // 2 * TILE
        q_s[h * TILE : (h + 1) * TILE, :] = q_ref[at : at + TILE, h % 2 * CW : (h % 2 + 1) * CW]

    def rows_of(i):
        return pl.ds(pl.multiple_of(list_s[i] * BLOCK, BLOCK), BLOCK)

    def joined(parts, axis):
        return parts[0] if len(parts) == 1 else jnp.concatenate(parts, axis=axis)

    def scores(first, size):
        k = joined([kv_s[rows_of(first + i), :CW] for i in range(size)], 0)
        s = lax.dot_general(q_s[...], k, (((1,), (1,)), ((), ())), preferred_element_type=jnp.float32)
        halves = []
        for i in range(size):
            b = list_s[first + i]
            for t in range(2):
                bias = jnp.where(flags_ref[2 * b + t] > 0, 0.0, NEG_FILL)
                at = 2 * i + t
                halves.append(s[:, at * TILE : (at + 1) * TILE] * SCALE2 + bias)
        return halves

    def own_scores():
        s = lax.dot_general(q_s[...], kv_s[last:, :CW], (((1,), (1,)), ((), ())), preferred_element_type=jnp.float32)
        s = (s.reshape(HEADS, TILE, BLOCK) * SCALE2 + bias_s[...][None]).reshape(QROWS, BLOCK)
        return [s[:, :TILE], s[:, TILE:]]

    def top_of(halves):
        m = jnp.max(functools.reduce(jnp.maximum, halves), axis=1, keepdims=True)
        return jnp.broadcast_to(m, (QROWS, TILE))

    def weigh(halves, v):
        m = m_s[...]
        p = jnp.concatenate([jnp.exp2(s - m).astype(jnp.bfloat16) for s in halves], axis=1)
        return jnp.dot(p, v, preferred_element_type=jnp.float32)

    def absorb(first, size):
        v = joined([kv_s[rows_of(first + i), CW:] for i in range(size)], 0)
        acc_s[...] += weigh(scores(first, size), v)

    def attempt(a, _):
        @pl.when(jnp.logical_or(a == 0, again_s[0] == 1))
        def _():
            @pl.when(a == 0)
            def _():
                m_s[...] = jnp.zeros_like(m_s)

            @pl.when(a == 1)
            def _():
                m_s[...] = top_of(own_scores()) if own else jnp.full_like(m_s, NEG_FILL)

                def top(i, _):
                    m_s[...] = jnp.maximum(m_s[...], top_of(scores(i, 1)))
                    return 0

                lax.fori_loop(0, count, top, 0)

            acc_s[...] = jnp.zeros_like(acc_s)
            done = 0
            for size in (4, 2, 1):

                def group(j, _, size=size, done=done):
                    absorb(done + j * size, size)
                    return 0

                loops = (count - done) // size
                lax.fori_loop(0, loops, group, 0)
                done = done + loops * size
            if own:
                acc_s[...] += weigh(own_scores(), kv_s[last:, CW:])
            raw = acc_s[:, CW:]
            total = jnp.maximum(raw, 1e-30)
            inverse = 1.0 / total
            log_total = jnp.log2(total)
            loud = jnp.max(jnp.abs(log_total)) > QUIET
            if not own:
                loud = jnp.logical_and(loud, count > 0)
            again_s[0] = jnp.where(loud, 1, 0)
            lse = m_s[...] + log_total
            if not own:
                lse = jnp.where(raw > 0, lse, NEG_FILL)
            head = lanes // STATS
            stats = lse[:TILE]
            for h in range(HEADS):
                rows = slice(h * TILE, (h + 1) * TILE)
                out_ref[:, h * CW : (h + 1) * CW] = (acc_s[rows, :CW] * inverse[rows]).astype(out_ref.dtype)
                stats = jnp.where(head == h, lse[rows], stats)
            if not own:
                a_, b_, c_ = split_three(stats)
                which = lanes % STATS
                stats = jnp.where(which == 0, a_, jnp.where(which == 1, b_, c_))
            out_ref[:, HEADS * CW :] = stats.astype(out_ref.dtype)
        return 0

    again_s[0] = 0
    for copy in copies:
        copy.wait()
    lax.fori_loop(0, 2, attempt, 0)


def attend(flags, q, pieces, own_parts=None, first=0, early=None):
    own = own_parts is not None
    args = [flags, q, *pieces]
    vmem = pl.BlockSpec(memory_space=pltpu.VMEM)
    keys = SHARES * SHARE + BLOCK * own
    return pl.pallas_call(
        functools.partial(attend_kernel, own, first, early is not None),
        out_shape=pltpu.VMEM((TILE, HEADS * CW + CW), jnp.float32 if own else jnp.bfloat16),
        in_specs=[pl.BlockSpec(memory_space=pltpu.SMEM)]
        + [vmem] * (len(args) - 1)
        + [pl.BlockSpec(memory_space=pl.ANY)] * ((early is not None) + 3 * own),
        out_specs=vmem,
        scratch_shapes=[
            pltpu.VMEM((keys, 3 * CW), jnp.bfloat16),
            pltpu.VMEM((QROWS, CW), jnp.bfloat16),
            pltpu.VMEM((QROWS, TILE), jnp.float32),
            pltpu.VMEM((QROWS, 2 * CW), jnp.float32),
            pltpu.SMEM((keys // BLOCK + 1,), jnp.int32),
            pltpu.SMEM((1,), jnp.int32),
        ]
        + [pltpu.VMEM((TILE, BLOCK), jnp.float32), pltpu.SemaphoreType.DMA((3,))] * own,
        compiler_params=pltpu.CompilerParams(vmem_limit_bytes=14 << 20),
        cost_estimate=pl.CostEstimate(flops=1, bytes_accessed=1, transcendentals=0),
        name="attend_own" if own else "attend_other",
    )(*args, *(own_parts or ()), *([] if early is None else [early]))


def combine(refs, att_s):
    stats = [r[:, HEADS * CW :].astype(jnp.float32) for r in refs]
    for h in range(HEADS):
        cols = slice(h * CW, (h + 1) * CW)
        i = STATS * h
        lses = [stats[0][:, i : i + 1]]
        for st in stats[1:]:
            lses.append(st[:, i : i + 1] + st[:, i + 1 : i + 2] + st[:, i + 2 : i + 3])
        top = functools.reduce(jnp.maximum, lses)
        weights = [jnp.exp2(v - top) for v in lses]
        inverse = 1.0 / sum(weights)
        mixed = sum(r[:, cols].astype(jnp.float32) * (w * inverse) for r, w in zip(refs, weights))
        att_s[:, cols] = mixed.astype(jnp.bfloat16)


def project_kernel(first, idx_ref, *refs):
    if first:
        own_ref, a_ref, b_ref, c_ref, w_ref, one_ref, two_ref, att_ref, w_s, sems = refs
    else:
        att_ref, w_ref, out_ref, w_s, sems = refs
    copies = []
    for j in range(4):
        start = pl.multiple_of(idx_ref[j if first else j + 4] * OUT_BLOCK, CW)
        copies.append(
            pltpu.make_async_copy(w_ref.at[:, pl.ds(start, OUT_BLOCK)], w_s.at[j], sems.at[j])
        )
        copies[-1].start()
    if first:
        combine((own_ref, a_ref, b_ref, c_ref), att_ref)
    for j in range(4):
        copies[j].wait()
        term = jnp.dot(att_ref[...], w_s[j], preferred_element_type=jnp.float32)
        if first:
            (one_ref, two_ref)[j // 2][j % 2] = term.astype(jnp.bfloat16)
        else:
            out_ref[j] = term


def project(idx, parts, weight):
    first = len(parts) > 1
    rows, width = TILE, HEADS * CW
    vmem = pl.BlockSpec(memory_space=pltpu.VMEM)
    pair = jax.ShapeDtypeStruct((2, rows, OUT_BLOCK), jnp.bfloat16)
    if first:
        out_shape = [pair, pair, jax.ShapeDtypeStruct((rows, width), jnp.bfloat16)]
    else:
        out_shape = [jax.ShapeDtypeStruct((4, rows, OUT_BLOCK), jnp.float32)]
    return pl.pallas_call(
        functools.partial(project_kernel, first),
        out_shape=out_shape,
        in_specs=[pl.BlockSpec(memory_space=pltpu.SMEM)]
        + [vmem] * len(parts)
        + [pl.BlockSpec(memory_space=pltpu.HBM)],
        out_specs=[vmem] * len(out_shape),
        scratch_shapes=[
            pltpu.VMEM((4, width, OUT_BLOCK), jnp.bfloat16),
            pltpu.SemaphoreType.DMA((4,)),
        ],
        compiler_params=pltpu.CompilerParams(vmem_limit_bytes=20 << 20),
        cost_estimate=pl.CostEstimate(
            flops=2 * rows * width * OUT_BLOCK * 4, bytes_accessed=6 << 20, transcendentals=0
        ),
        name="project_first" if first else "project_second",
    )(idx, *parts, pltpu.with_memory_space_constraint(weight, pltpu.HBM))


def along_z(block, step):
    route = [
        (c * ZS + z, c * ZS + (z + (step if c == 0 else -step)) % ZS)
        for c in range(CORES)
        for z in range(ZS)
    ]
    return lax.ppermute(block, ("core", "z"), route)


def body(q, rkeys, rvalues, pkeys, pvalues, weight, segment_ids, block_mask):
    core, z = lax.axis_index("core"), lax.axis_index("z")
    kv, rkv, bias, q, *seen = prepare(
        block_mask, segment_ids, pkeys, pvalues, rkeys, rvalues, q
    )
    far, far_q = shifted(kv, "x", 2), shifted(q, "y", 2)
    chip, chip_q = paired(kv, shifted(kv, "core", 1), q, shifted(q, "core", 1))
    near, near_q = opposite(chip, "x", 1), opposite(chip_q, "y", 1)
    prev = shifted(rkv, ("x", "y", "core"), -1)
    far, far_q, near, near_q, prev = lax.optimization_barrier(
        (far, far_q, near, near_q, prev)
    )
    pieces = [chip, far, shifted(far, "core", 1), near, shifted(near, "core", 1)]

    part = attend(seen[1], far_q, pieces)
    two = shifted(part, "y", 2)
    next_one = opposite(attend(seen[2], near_q, pieces), "y", -1)
    swapped = shifted(near_q, "core", 1)
    last_one = opposite(attend(seen[3], swapped, pieces, first=QROWS // 2, early=part), "y", 1)
    own = attend(seen[0], q, pieces, (prev, rkv, bias))

    sign = 1 - 2 * core
    idx = jnp.stack([(z + sign * o) % ZS for o in (-4, -2, 3, 1, -3, -1, 2, 0)]).astype(jnp.int32)
    one, two, att = project(idx, [own, two, next_one, last_one], weight)
    got_one = along_z(one, -1)
    got_two = along_z(two, 1)
    (rest,) = project(idx, [att], weight)
    back3 = along_z((rest[0] + got_one[0].astype(jnp.float32)).astype(jnp.bfloat16), -3)
    on2 = along_z((rest[2] + got_two[0].astype(jnp.float32)).astype(jnp.bfloat16), 2)
    back1 = along_z((rest[1] + got_one[1].astype(jnp.float32)).astype(jnp.bfloat16), -1)
    total = rest[3] + got_two[1].astype(jnp.float32)
    for part in (back1, on2, back3):
        total = total + part.astype(jnp.float32)
    return total.astype(jnp.bfloat16)


def solution(mesh):
    split = Mesh(mesh.devices.reshape(XS, YS, CORES, ZS), ("x", "y", "core", "z"))
    seq = ("x", "y", "core")
    placed = (P(seq, "z"),) * 5 + (P("z", None), P(), P())
    return jax.shard_map(
        body, mesh=split, in_specs=placed, out_specs=P(seq, "z"), check_vma=False
    )
```

```python
import functools
import math

import jax
import jax.numpy as jnp
from jax import lax
from jax.experimental import pallas as pl
from jax.experimental.pallas import tpu as pltpu
from jax.sharding import Mesh, PartitionSpec as P

H = 64
KVH = 8
CW = 128
TILE = 128
HEADS = H // KVH
XS, YS, CORES, ZS = 4, 4, 2, 8
SHARE = 512
SHARES = XS * CORES
BLOCK = 256
NEG_FILL = -1e30
SCALE2 = math.log2(math.e) / math.sqrt(CW)
STATS = 3
QUIET = 64.0
QROWS = HEADS * TILE
OUT_BLOCK = 640


def seq_index(x, y, c):
    return (lax.rem(x, XS) * YS + lax.rem(y, YS)) * CORES + c


def shifted(block, axis, step):
    n = lax.axis_size(axis)
    return lax.ppermute(block, axis, [((i + step) % n, i) for i in range(n)])


def prepare_kernel(
    mask_hbm, seg_hbm, pk_ref, pv_ref, rk_ref, rv_ref, q_hbm, kv_ref, rkv_ref, bias_ref, q_ref, *refs
):
    flag_refs, (mask_ref, seg_ref, sems) = refs[:4], refs[4:]
    x, y, core = (lax.axis_index(a) for a in ("x", "y", "core"))
    copies = [
        pltpu.make_async_copy(source, target, sems.at[i])
        for i, (source, target) in enumerate(
            (
                (mask_hbm, mask_ref),
                (seg_hbm, seg_ref),
                (pk_ref, kv_ref.at[:, :CW]),
                (pv_ref, kv_ref.at[:, CW:]),
                (rk_ref, rkv_ref.at[:, :CW]),
                (rv_ref, rkv_ref.at[:, CW:]),
            )
            + tuple(
                (q_hbm.at[:, i : i + 2 * CW], q_ref.at[i // 2 : i // 2 + TILE])
                for i in range(0, HEADS * CW, 2 * CW)
            )
        )
    ]
    for copy in copies:
        copy.start()
    for copy in copies:
        copy.wait()
    tiles = SHARE // TILE
    step = XS + 1 - 2 * core
    back = XS - 1 + 2 * core
    other = 1 - core
    shares = (
        (0, core), (0, other), (2, core), (2, other),
        (step, core), (step, other), (back, other), (back, core),
    )
    for flags, dy in zip(flag_refs, (0, 2, 1 - 2 * core, 2 * core - 1)):
        row = seq_index(x, y + dy + YS, core)
        for p, (dx, c) in enumerate(shares):
            first = seq_index(x + dx, y, c) * tiles
            for t in range(tiles):
                flags[p * tiles + t] = mask_ref[row, first + t]
    device = seq_index(x, y, core)
    mine = seg_ref[pl.ds(device, 1), :]
    before = seg_ref[pl.ds(jnp.maximum(device - 1, 0), 1), :]
    before = jnp.where(device > 0, before, -1)
    rows = jnp.broadcast_to(mine, (TILE, TILE)).T
    r = lax.broadcasted_iota(jnp.int32, (TILE, TILE), 0)
    c = lax.broadcasted_iota(jnp.int32, (TILE, TILE), 1)
    bias_ref[:, :TILE] = jnp.where(rows == before, 0.0, NEG_FILL)
    bias_ref[:, TILE:] = jnp.where((rows == mine) & (c <= r), 0.0, NEG_FILL)


def prepare(block_mask, segment_ids, pkeys, pvalues, rkeys, rvalues, q):
    vmem = pl.BlockSpec(memory_space=pltpu.VMEM)
    smem = pl.BlockSpec(memory_space=pltpu.SMEM)
    flags = jax.ShapeDtypeStruct((SHARES * SHARE // TILE,), jnp.int32)
    return pl.pallas_call(
        prepare_kernel,
        out_shape=[
            pltpu.VMEM((pkeys.shape[0], 2 * CW), jnp.bfloat16),
            pltpu.VMEM((TILE, 2 * CW), jnp.bfloat16),
            pltpu.VMEM((TILE, 2 * TILE), jnp.float32),
            pltpu.VMEM((QROWS // 2, 2 * CW), q.dtype),
        ]
        + [flags] * 4,
        in_specs=[pl.BlockSpec(memory_space=pltpu.HBM)] * 7,
        out_specs=[vmem] * 4 + [smem] * 4,
        scratch_shapes=[
            pltpu.SMEM(block_mask.shape, jnp.int32),
            pltpu.VMEM((segment_ids.shape[0] // TILE, TILE), jnp.int32),
            pltpu.SemaphoreType.DMA((10,)),
        ],
        compiler_params=pltpu.CompilerParams(vmem_limit_bytes=8 << 20),
        cost_estimate=pl.CostEstimate(flops=1, bytes_accessed=1, transcendentals=0),
        name="prepare",
    )(
        *(
            pltpu.with_memory_space_constraint(a, pltpu.HBM)
            for a in (block_mask, segment_ids.reshape(-1, TILE), pkeys, pvalues, rkeys, rvalues, q)
        )
    )


def pair_kernel(*refs):
    for i in range(2):
        a_ref, b_ref, out_ref = refs[2 * i], refs[2 * i + 1], refs[4 + i]
        rows = a_ref.shape[0]
        out_ref[:rows] = a_ref[...]
        out_ref[rows:] = b_ref[...]


def paired(*arrays):
    vmem = pl.BlockSpec(memory_space=pltpu.VMEM)
    return pl.pallas_call(
        pair_kernel,
        out_shape=[pltpu.VMEM((2 * a.shape[0], a.shape[1]), a.dtype) for a in arrays[::2]],
        in_specs=[vmem] * 4,
        out_specs=[vmem] * 2,
        compiler_params=pltpu.CompilerParams(vmem_limit_bytes=4 << 20),
        cost_estimate=pl.CostEstimate(flops=1, bytes_accessed=1, transcendentals=0),
        name="paired",
    )(*arrays)


def split_three(value):
    parts = []
    for _ in range(STATS):
        parts.append(value.astype(jnp.bfloat16).astype(jnp.float32))
        value = value - parts[-1]
    return parts


def opposite(block, axis, step):
    n = lax.axis_size(axis)
    route = [
        (((i + (step if c == 0 else -step)) % n) * CORES + c, i * CORES + c)
        for i in range(n)
        for c in range(CORES)
    ]
    return lax.ppermute(block, (axis, "core"), route)


def attend_kernel(own, first, early, flags_ref, q_ref, *refs):
    kv_refs, refs = refs[:5], refs[5:]
    if own:
        (prev_ref, mine_ref, bias_ref), refs = refs[:3], refs[3:]
    refs = refs[early:]
    out_ref, kv_s, q_s, m_s, acc_s, list_s, again_s = refs[:7]
    last = SHARES * SHARE
    copies = []
    if own:
        bias_s, sems = refs[7:]
        targets = (
            kv_s.at[last : last + TILE, : 2 * CW],
            kv_s.at[last + TILE : last + BLOCK, : 2 * CW],
            bias_s,
        )
        for i, (source, target) in enumerate(zip((prev_ref, mine_ref, bias_ref), targets)):
            copies.append(pltpu.make_async_copy(source, target, sems.at[i]))
            copies[-1].start()
    lanes = lax.broadcasted_iota(jnp.int32, (TILE, CW), 1)

    count = 0
    block = 0
    for ref in kv_refs:
        for b in range(ref.shape[0] // BLOCK):
            seen = flags_ref[2 * block] + flags_ref[2 * block + 1] > 0
            list_s[count] = block

            @pl.when(seen)
            def _():
                rows = slice(block * BLOCK, (block + 1) * BLOCK)
                kv_s[rows, : 2 * CW] = ref[b * BLOCK : (b + 1) * BLOCK]
                kv_s[rows, 2 * CW :] = jnp.ones((BLOCK, CW), jnp.bfloat16)

            count = count + jnp.where(seen, 1, 0)
            block += 1
    if own:
        kv_s[last:, 2 * CW :] = jnp.ones((BLOCK, CW), jnp.bfloat16)
    for h in range(HEADS):
        at = first + h // 2 * TILE
        q_s[h * TILE : (h + 1) * TILE, :] = q_ref[at : at + TILE, h % 2 * CW : (h % 2 + 1) * CW]

    def rows_of(i):
        return pl.ds(pl.multiple_of(list_s[i] * BLOCK, BLOCK), BLOCK)

    def joined(parts, axis):
        return parts[0] if len(parts) == 1 else jnp.concatenate(parts, axis=axis)

    def scores(first, size):
        k = joined([kv_s[rows_of(first + i), :CW] for i in range(size)], 0)
        s = lax.dot_general(q_s[...], k, (((1,), (1,)), ((), ())), preferred_element_type=jnp.float32)
        halves = []
        for i in range(size):
            b = list_s[first + i]
            for t in range(2):
                bias = jnp.where(flags_ref[2 * b + t] > 0, 0.0, NEG_FILL)
                at = 2 * i + t
                halves.append(s[:, at * TILE : (at + 1) * TILE] * SCALE2 + bias)
        return halves

    def own_scores():
        s = lax.dot_general(q_s[...], kv_s[last:, :CW], (((1,), (1,)), ((), ())), preferred_element_type=jnp.float32)
        s = (s.reshape(HEADS, TILE, BLOCK) * SCALE2 + bias_s[...][None]).reshape(QROWS, BLOCK)
        return [s[:, :TILE], s[:, TILE:]]

    def top_of(halves):
        m = jnp.max(functools.reduce(jnp.maximum, halves), axis=1, keepdims=True)
        return jnp.broadcast_to(m, (QROWS, TILE))

    def weigh(halves, v):
        m = m_s[...]
        p = jnp.concatenate([jnp.exp2(s - m).astype(jnp.bfloat16) for s in halves], axis=1)
        return jnp.dot(p, v, preferred_element_type=jnp.float32)

    def absorb(first, size):
        v = joined([kv_s[rows_of(first + i), CW:] for i in range(size)], 0)
        acc_s[...] += weigh(scores(first, size), v)

    def attempt(a, _):
        @pl.when(jnp.logical_or(a == 0, again_s[0] == 1))
        def _():
            @pl.when(a == 0)
            def _():
                m_s[...] = jnp.zeros_like(m_s)

            @pl.when(a == 1)
            def _():
                m_s[...] = top_of(own_scores()) if own else jnp.full_like(m_s, NEG_FILL)

                def top(i, _):
                    m_s[...] = jnp.maximum(m_s[...], top_of(scores(i, 1)))
                    return 0

                lax.fori_loop(0, count, top, 0)

            acc_s[...] = jnp.zeros_like(acc_s)
            done = 0
            for size in (4, 2, 1):

                def group(j, _, size=size, done=done):
                    absorb(done + j * size, size)
                    return 0

                loops = (count - done) // size
                lax.fori_loop(0, loops, group, 0)
                done = done + loops * size
            if own:
                acc_s[...] += weigh(own_scores(), kv_s[last:, CW:])
            raw = acc_s[:, CW:]
            total = jnp.maximum(raw, 1e-30)
            inverse = 1.0 / total
            log_total = jnp.log2(total)
            loud = jnp.max(jnp.abs(log_total)) > QUIET
            if not own:
                loud = jnp.logical_and(loud, count > 0)
            again_s[0] = jnp.where(loud, 1, 0)
            lse = m_s[...] + log_total
            if not own:
                lse = jnp.where(raw > 0, lse, NEG_FILL)
            head = lanes // STATS
            stats = lse[:TILE]
            for h in range(HEADS):
                rows = slice(h * TILE, (h + 1) * TILE)
                out_ref[:, h * CW : (h + 1) * CW] = (acc_s[rows, :CW] * inverse[rows]).astype(out_ref.dtype)
                stats = jnp.where(head == h, lse[rows], stats)
            if not own:
                a_, b_, c_ = split_three(stats)
                which = lanes % STATS
                stats = jnp.where(which == 0, a_, jnp.where(which == 1, b_, c_))
            out_ref[:, HEADS * CW :] = stats.astype(out_ref.dtype)
        return 0

    again_s[0] = 0
    for copy in copies:
        copy.wait()
    lax.fori_loop(0, 2, attempt, 0)


def attend(flags, q, pieces, own_parts=None, first=0, early=None):
    own = own_parts is not None
    args = [flags, q, *pieces]
    vmem = pl.BlockSpec(memory_space=pltpu.VMEM)
    keys = SHARES * SHARE + BLOCK * own
    return pl.pallas_call(
        functools.partial(attend_kernel, own, first, early is not None),
        out_shape=pltpu.VMEM((TILE, HEADS * CW + CW), jnp.float32 if own else jnp.bfloat16),
        in_specs=[pl.BlockSpec(memory_space=pltpu.SMEM)]
        + [vmem] * (len(args) - 1)
        + [pl.BlockSpec(memory_space=pl.ANY)] * ((early is not None) + 3 * own),
        out_specs=vmem,
        scratch_shapes=[
            pltpu.VMEM((keys, 3 * CW), jnp.bfloat16),
            pltpu.VMEM((QROWS, CW), jnp.bfloat16),
            pltpu.VMEM((QROWS, TILE), jnp.float32),
            pltpu.VMEM((QROWS, 2 * CW), jnp.float32),
            pltpu.SMEM((keys // BLOCK + 1,), jnp.int32),
            pltpu.SMEM((1,), jnp.int32),
        ]
        + [pltpu.VMEM((TILE, BLOCK), jnp.float32), pltpu.SemaphoreType.DMA((3,))] * own,
        compiler_params=pltpu.CompilerParams(vmem_limit_bytes=14 << 20),
        cost_estimate=pl.CostEstimate(flops=1, bytes_accessed=1, transcendentals=0),
        name="attend_own" if own else "attend_other",
    )(*args, *(own_parts or ()), *([] if early is None else [early]))


def combine(refs, att_s):
    stats = [r[:, HEADS * CW :].astype(jnp.float32) for r in refs]
    for h in range(HEADS):
        cols = slice(h * CW, (h + 1) * CW)
        i = STATS * h
        lses = [stats[0][:, i : i + 1]]
        for st in stats[1:]:
            lses.append(st[:, i : i + 1] + st[:, i + 1 : i + 2] + st[:, i + 2 : i + 3])
        top = functools.reduce(jnp.maximum, lses)
        weights = [jnp.exp2(v - top) for v in lses]
        inverse = 1.0 / sum(weights)
        mixed = sum(r[:, cols].astype(jnp.float32) * (w * inverse) for r, w in zip(refs, weights))
        att_s[:, cols] = mixed.astype(jnp.bfloat16)


def project_kernel(first, idx_ref, *refs):
    if first:
        own_ref, a_ref, b_ref, c_ref, w_ref, one_ref, two_ref, att_ref, w_s, sems = refs
    else:
        att_ref, w_ref, out_ref, w_s, sems = refs
    copies = []
    for j in range(4):
        start = pl.multiple_of(idx_ref[j if first else j + 4] * OUT_BLOCK, CW)
        copies.append(
            pltpu.make_async_copy(w_ref.at[:, pl.ds(start, OUT_BLOCK)], w_s.at[j], sems.at[j])
        )
        copies[-1].start()
    if first:
        combine((own_ref, a_ref, b_ref, c_ref), att_ref)
    for j in range(4):
        copies[j].wait()
        term = jnp.dot(att_ref[...], w_s[j], preferred_element_type=jnp.float32)
        if first:
            (one_ref, two_ref)[j // 2][j % 2] = term.astype(jnp.bfloat16)
        else:
            out_ref[j] = term


def project(idx, parts, weight):
    first = len(parts) > 1
    rows, width = TILE, HEADS * CW
    vmem = pl.BlockSpec(memory_space=pltpu.VMEM)
    pair = jax.ShapeDtypeStruct((2, rows, OUT_BLOCK), jnp.bfloat16)
    if first:
        out_shape = [pair, pair, jax.ShapeDtypeStruct((rows, width), jnp.bfloat16)]
    else:
        out_shape = [jax.ShapeDtypeStruct((4, rows, OUT_BLOCK), jnp.float32)]
    return pl.pallas_call(
        functools.partial(project_kernel, first),
        out_shape=out_shape,
        in_specs=[pl.BlockSpec(memory_space=pltpu.SMEM)]
        + [vmem] * len(parts)
        + [pl.BlockSpec(memory_space=pltpu.HBM)],
        out_specs=[vmem] * len(out_shape),
        scratch_shapes=[
            pltpu.VMEM((4, width, OUT_BLOCK), jnp.bfloat16),
            pltpu.SemaphoreType.DMA((4,)),
        ],
        compiler_params=pltpu.CompilerParams(vmem_limit_bytes=20 << 20),
        cost_estimate=pl.CostEstimate(
            flops=2 * rows * width * OUT_BLOCK * 4, bytes_accessed=6 << 20, transcendentals=0
        ),
        name="project_first" if first else "project_second",
    )(idx, *parts, pltpu.with_memory_space_constraint(weight, pltpu.HBM))


def along_z(block, step):
    route = [
        (c * ZS + z, c * ZS + (z + (step if c == 0 else -step)) % ZS)
        for c in range(CORES)
        for z in range(ZS)
    ]
    return lax.ppermute(block, ("core", "z"), route)


def body(q, rkeys, rvalues, pkeys, pvalues, weight, segment_ids, block_mask):
    core, z = lax.axis_index("core"), lax.axis_index("z")
    kv, rkv, bias, q, *seen = prepare(
        block_mask, segment_ids, pkeys, pvalues, rkeys, rvalues, q
    )
    chip, chip_q = paired(kv, shifted(kv, "core", 1), q, shifted(q, "core", 1))
    near, near_q = opposite(chip, "x", 1), opposite(chip_q, "y", 1)
    prev = shifted(rkv, ("x", "y", "core"), -1)
    near, near_q, prev = lax.optimization_barrier((near, near_q, prev))
    far = opposite(near[:SHARE], "x", 1)
    far_q = opposite(near_q[: QROWS // 2], "y", 1)
    near_other, swapped = shifted(near, "core", 1), shifted(near_q, "core", 1)
    far, far_q = lax.optimization_barrier((far, far_q))
    pieces = [chip, far, shifted(far, "core", 1), near, near_other]

    part = attend(seen[1], far_q, pieces)
    two = shifted(part, "y", 2)
    next_one = opposite(attend(seen[2], near_q, pieces), "y", -1)
    last_one = opposite(attend(seen[3], swapped, pieces, first=QROWS // 2, early=part), "y", 1)
    own = attend(seen[0], q, pieces, (prev, rkv, bias))

    sign = 1 - 2 * core
    idx = jnp.stack([(z + sign * o) % ZS for o in (-4, -2, 3, 1, -3, -1, 2, 0)]).astype(jnp.int32)
    one, two, att = project(idx, [own, two, next_one, last_one], weight)
    got_one = along_z(one, -1)
    got_two = along_z(two, 1)
    (rest,) = project(idx, [att], weight)
    back3 = along_z((rest[0] + got_one[0].astype(jnp.float32)).astype(jnp.bfloat16), -3)
    on2 = along_z((rest[2] + got_two[0].astype(jnp.float32)).astype(jnp.bfloat16), 2)
    back1 = along_z((rest[1] + got_one[1].astype(jnp.float32)).astype(jnp.bfloat16), -1)
    total = rest[3] + got_two[1].astype(jnp.float32)
    for part in (back1, on2, back3):
        total = total + part.astype(jnp.float32)
    return total.astype(jnp.bfloat16)


def solution(mesh):
    split = Mesh(mesh.devices.reshape(XS, YS, CORES, ZS), ("x", "y", "core", "z"))
    seq = ("x", "y", "core")
    placed = (P(seq, "z"),) * 5 + (P("z", None), P(), P())
    return jax.shard_map(
        body, mesh=split, in_specs=placed, out_specs=P(seq, "z"), check_vma=False
    )
```

```python
import functools
import math

import jax
import jax.numpy as jnp
from jax import lax
from jax.experimental import pallas as pl
from jax.experimental.pallas import tpu as pltpu
from jax.sharding import Mesh, PartitionSpec as P

H = 64
KVH = 8
CW = 128
TILE = 128
HEADS = H // KVH
XS, YS, CORES, ZS = 4, 4, 2, 8
SHARE = 512
SHARES = XS * CORES
BLOCK = 256
NEG_FILL = -1e30
SCALE2 = math.log2(math.e) / math.sqrt(CW)
STATS = 3
QUIET = 64.0
QROWS = HEADS * TILE
OUT_BLOCK = 640


def seq_index(x, y, c):
    return (lax.rem(x, XS) * YS + lax.rem(y, YS)) * CORES + c


def shifted(block, axis, step):
    n = lax.axis_size(axis)
    return lax.ppermute(block, axis, [((i + step) % n, i) for i in range(n)])


def prepare_kernel(
    mask_hbm, seg_hbm, pk_ref, pv_ref, rk_ref, rv_ref, q_hbm, kv_ref, rkv_ref, bias_ref, q_ref, *refs
):
    flag_refs, (mask_ref, seg_ref, sems) = refs[:4], refs[4:]
    x, y, core = (lax.axis_index(a) for a in ("x", "y", "core"))
    copies = [
        pltpu.make_async_copy(source, target, sems.at[i])
        for i, (source, target) in enumerate(
            (
                (mask_hbm, mask_ref),
                (seg_hbm, seg_ref),
                (pk_ref, kv_ref.at[:, :CW]),
                (pv_ref, kv_ref.at[:, CW:]),
                (rk_ref, rkv_ref.at[:, :CW]),
                (rv_ref, rkv_ref.at[:, CW:]),
            )
            + tuple(
                (q_hbm.at[:, i : i + 2 * CW], q_ref.at[i // 2 : i // 2 + TILE])
                for i in range(0, HEADS * CW, 2 * CW)
            )
        )
    ]
    for copy in copies:
        copy.start()
    for copy in copies:
        copy.wait()
    tiles = SHARE // TILE
    step = XS + 1 - 2 * core
    back = XS - 1 + 2 * core
    other = 1 - core
    shares = (
        (0, core), (step, core), (back, core), (2, core),
        (0, other), (back, other), (step, other), (2, other),
    )
    for flags, dy in zip(flag_refs, (0, 2, 1 - 2 * core, 2 * core - 1)):
        row = seq_index(x, y + dy + YS, core)
        for p, (dx, c) in enumerate(shares):
            first = seq_index(x + dx, y, c) * tiles
            for t in range(tiles):
                flags[p * tiles + t] = mask_ref[row, first + t]
    device = seq_index(x, y, core)
    mine = seg_ref[pl.ds(device, 1), :]
    before = seg_ref[pl.ds(jnp.maximum(device - 1, 0), 1), :]
    before = jnp.where(device > 0, before, -1)
    rows = jnp.broadcast_to(mine, (TILE, TILE)).T
    r = lax.broadcasted_iota(jnp.int32, (TILE, TILE), 0)
    c = lax.broadcasted_iota(jnp.int32, (TILE, TILE), 1)
    bias_ref[:, :TILE] = jnp.where(rows == before, 0.0, NEG_FILL)
    bias_ref[:, TILE:] = jnp.where((rows == mine) & (c <= r), 0.0, NEG_FILL)


def prepare(block_mask, segment_ids, pkeys, pvalues, rkeys, rvalues, q):
    vmem = pl.BlockSpec(memory_space=pltpu.VMEM)
    smem = pl.BlockSpec(memory_space=pltpu.SMEM)
    flags = jax.ShapeDtypeStruct((SHARES * SHARE // TILE,), jnp.int32)
    return pl.pallas_call(
        prepare_kernel,
        out_shape=[
            pltpu.VMEM((pkeys.shape[0], 2 * CW), jnp.bfloat16),
            pltpu.VMEM((TILE, 2 * CW), jnp.bfloat16),
            pltpu.VMEM((TILE, 2 * TILE), jnp.float32),
            pltpu.VMEM((QROWS // 2, 2 * CW), q.dtype),
        ]
        + [flags] * 4,
        in_specs=[pl.BlockSpec(memory_space=pltpu.HBM)] * 7,
        out_specs=[vmem] * 4 + [smem] * 4,
        scratch_shapes=[
            pltpu.SMEM(block_mask.shape, jnp.int32),
            pltpu.VMEM((segment_ids.shape[0] // TILE, TILE), jnp.int32),
            pltpu.SemaphoreType.DMA((10,)),
        ],
        compiler_params=pltpu.CompilerParams(vmem_limit_bytes=8 << 20),
        cost_estimate=pl.CostEstimate(flops=1, bytes_accessed=1, transcendentals=0),
        name="prepare",
    )(
        *(
            pltpu.with_memory_space_constraint(a, pltpu.HBM)
            for a in (block_mask, segment_ids.reshape(-1, TILE), pkeys, pvalues, rkeys, rvalues, q)
        )
    )


def split_three(value):
    parts = []
    for _ in range(STATS):
        parts.append(value.astype(jnp.bfloat16).astype(jnp.float32))
        value = value - parts[-1]
    return parts


def opposite(block, axis, step):
    n = lax.axis_size(axis)
    route = [
        (((i + (step if c == 0 else -step)) % n) * CORES + c, i * CORES + c)
        for i in range(n)
        for c in range(CORES)
    ]
    return lax.ppermute(block, (axis, "core"), route)


def attend_kernel(own, early, flags_ref, q_ref, *refs):
    kv_refs, refs = refs[:SHARES], refs[SHARES:]
    if own:
        (prev_ref, mine_ref, bias_ref), refs = refs[:3], refs[3:]
    refs = refs[early:]
    out_ref, kv_s, q_s, m_s, acc_s, list_s, again_s = refs[:7]
    last = SHARES * SHARE
    copies = []
    if own:
        bias_s, sems = refs[7:]
        targets = (
            kv_s.at[last : last + TILE, : 2 * CW],
            kv_s.at[last + TILE : last + BLOCK, : 2 * CW],
            bias_s,
        )
        for i, (source, target) in enumerate(zip((prev_ref, mine_ref, bias_ref), targets)):
            copies.append(pltpu.make_async_copy(source, target, sems.at[i]))
            copies[-1].start()
    lanes = lax.broadcasted_iota(jnp.int32, (TILE, CW), 1)

    count = 0
    block = 0
    for ref in kv_refs:
        for b in range(ref.shape[0] // BLOCK):
            seen = flags_ref[2 * block] + flags_ref[2 * block + 1] > 0
            list_s[count] = block

            @pl.when(seen)
            def _():
                rows = slice(block * BLOCK, (block + 1) * BLOCK)
                kv_s[rows, : 2 * CW] = ref[b * BLOCK : (b + 1) * BLOCK]
                kv_s[rows, 2 * CW :] = jnp.ones((BLOCK, CW), jnp.bfloat16)

            count = count + jnp.where(seen, 1, 0)
            block += 1
    if own:
        kv_s[last:, 2 * CW :] = jnp.ones((BLOCK, CW), jnp.bfloat16)
    for h in range(HEADS):
        at = h // 2 * TILE
        q_s[h * TILE : (h + 1) * TILE, :] = q_ref[at : at + TILE, h % 2 * CW : (h % 2 + 1) * CW]

    def rows_of(i):
        return pl.ds(pl.multiple_of(list_s[i] * BLOCK, BLOCK), BLOCK)

    def joined(parts, axis):
        return parts[0] if len(parts) == 1 else jnp.concatenate(parts, axis=axis)

    def scores(first, size):
        k = joined([kv_s[rows_of(first + i), :CW] for i in range(size)], 0)
        s = lax.dot_general(q_s[...], k, (((1,), (1,)), ((), ())), preferred_element_type=jnp.float32)
        halves = []
        for i in range(size):
            b = list_s[first + i]
            for t in range(2):
                bias = jnp.where(flags_ref[2 * b + t] > 0, 0.0, NEG_FILL)
                at = 2 * i + t
                halves.append(s[:, at * TILE : (at + 1) * TILE] * SCALE2 + bias)
        return halves

    def own_scores():
        s = lax.dot_general(q_s[...], kv_s[last:, :CW], (((1,), (1,)), ((), ())), preferred_element_type=jnp.float32)
        s = (s.reshape(HEADS, TILE, BLOCK) * SCALE2 + bias_s[...][None]).reshape(QROWS, BLOCK)
        return [s[:, :TILE], s[:, TILE:]]

    def top_of(halves):
        m = jnp.max(functools.reduce(jnp.maximum, halves), axis=1, keepdims=True)
        return jnp.broadcast_to(m, (QROWS, TILE))

    def weigh(halves, v):
        m = m_s[...]
        p = jnp.concatenate([jnp.exp2(s - m).astype(jnp.bfloat16) for s in halves], axis=1)
        return jnp.dot(p, v, preferred_element_type=jnp.float32)

    def absorb(first, size):
        v = joined([kv_s[rows_of(first + i), CW:] for i in range(size)], 0)
        acc_s[...] += weigh(scores(first, size), v)

    def attempt(a, _):
        @pl.when(jnp.logical_or(a == 0, again_s[0] == 1))
        def _():
            @pl.when(a == 0)
            def _():
                m_s[...] = jnp.zeros_like(m_s)

            @pl.when(a == 1)
            def _():
                m_s[...] = top_of(own_scores()) if own else jnp.full_like(m_s, NEG_FILL)

                def top(i, _):
                    m_s[...] = jnp.maximum(m_s[...], top_of(scores(i, 1)))
                    return 0

                lax.fori_loop(0, count, top, 0)

            acc_s[...] = jnp.zeros_like(acc_s)
            done = 0
            for size in (4, 2, 1):

                def group(j, _, size=size, done=done):
                    absorb(done + j * size, size)
                    return 0

                loops = (count - done) // size
                lax.fori_loop(0, loops, group, 0)
                done = done + loops * size
            if own:
                acc_s[...] += weigh(own_scores(), kv_s[last:, CW:])
            raw = acc_s[:, CW:]
            total = jnp.maximum(raw, 1e-30)
            inverse = 1.0 / total
            log_total = jnp.log2(total)
            loud = jnp.max(jnp.abs(log_total)) > QUIET
            if not own:
                loud = jnp.logical_and(loud, count > 0)
            again_s[0] = jnp.where(loud, 1, 0)
            lse = m_s[...] + log_total
            if not own:
                lse = jnp.where(raw > 0, lse, NEG_FILL)
            head = lanes // STATS
            stats = lse[:TILE]
            for h in range(HEADS):
                rows = slice(h * TILE, (h + 1) * TILE)
                out_ref[:, h * CW : (h + 1) * CW] = (acc_s[rows, :CW] * inverse[rows]).astype(out_ref.dtype)
                stats = jnp.where(head == h, lse[rows], stats)
            if not own:
                a_, b_, c_ = split_three(stats)
                which = lanes % STATS
                stats = jnp.where(which == 0, a_, jnp.where(which == 1, b_, c_))
            out_ref[:, HEADS * CW :] = stats.astype(out_ref.dtype)
        return 0

    again_s[0] = 0
    for copy in copies:
        copy.wait()
    lax.fori_loop(0, 2, attempt, 0)


def attend(flags, q, pieces, own_parts=None, early=None):
    own = own_parts is not None
    args = [flags, q, *pieces]
    vmem = pl.BlockSpec(memory_space=pltpu.VMEM)
    keys = SHARES * SHARE + BLOCK * own
    return pl.pallas_call(
        functools.partial(attend_kernel, own, early is not None),
        out_shape=pltpu.VMEM((TILE, HEADS * CW + CW), jnp.float32 if own else jnp.bfloat16),
        in_specs=[pl.BlockSpec(memory_space=pltpu.SMEM)]
        + [vmem] * (len(args) - 1)
        + [pl.BlockSpec(memory_space=pltpu.HBM)] * (3 * own)
        + [pl.BlockSpec(memory_space=pl.ANY)] * (early is not None),
        out_specs=vmem,
        scratch_shapes=[
            pltpu.VMEM((keys, 3 * CW), jnp.bfloat16),
            pltpu.VMEM((QROWS, CW), jnp.bfloat16),
            pltpu.VMEM((QROWS, TILE), jnp.float32),
            pltpu.VMEM((QROWS, 2 * CW), jnp.float32),
            pltpu.SMEM((keys // BLOCK + 1,), jnp.int32),
            pltpu.SMEM((1,), jnp.int32),
        ]
        + [pltpu.VMEM((TILE, BLOCK), jnp.float32), pltpu.SemaphoreType.DMA((3,))] * own,
        compiler_params=pltpu.CompilerParams(vmem_limit_bytes=14 << 20),
        cost_estimate=pl.CostEstimate(flops=1, bytes_accessed=1, transcendentals=0),
        name="attend_own" if own else "attend_other",
    )(*args, *(own_parts or ()), *([] if early is None else [early]))


def combine(refs, att_s):
    stats = [r[:, HEADS * CW :].astype(jnp.float32) for r in refs]
    for h in range(HEADS):
        cols = slice(h * CW, (h + 1) * CW)
        i = STATS * h
        lses = [stats[0][:, i : i + 1]]
        for st in stats[1:]:
            lses.append(st[:, i : i + 1] + st[:, i + 1 : i + 2] + st[:, i + 2 : i + 3])
        top = functools.reduce(jnp.maximum, lses)
        weights = [jnp.exp2(v - top) for v in lses]
        inverse = 1.0 / sum(weights)
        mixed = sum(r[:, cols].astype(jnp.float32) * (w * inverse) for r, w in zip(refs, weights))
        att_s[:, cols] = mixed.astype(jnp.bfloat16)


def project_kernel(first, idx_ref, *refs):
    if first:
        own_ref, a_ref, b_ref, c_ref, w_ref, one_ref, two_ref, att_ref, w_s, sems = refs
    else:
        att_ref, w_ref, out_ref, w_s, sems = refs
    copies = []
    for j in range(4):
        start = pl.multiple_of(idx_ref[j if first else j + 4] * OUT_BLOCK, CW)
        copies.append(
            pltpu.make_async_copy(w_ref.at[:, pl.ds(start, OUT_BLOCK)], w_s.at[j], sems.at[j])
        )
        copies[-1].start()
    if first:
        combine((own_ref, a_ref, b_ref, c_ref), att_ref)
    for j in range(4):
        copies[j].wait()
        term = jnp.dot(att_ref[...], w_s[j], preferred_element_type=jnp.float32)
        if first:
            (one_ref, two_ref)[j // 2][j % 2] = term.astype(jnp.bfloat16)
        else:
            out_ref[j] = term


def project(idx, parts, weight):
    first = len(parts) > 1
    rows, width = TILE, HEADS * CW
    vmem = pl.BlockSpec(memory_space=pltpu.VMEM)
    pair = jax.ShapeDtypeStruct((2, rows, OUT_BLOCK), jnp.bfloat16)
    if first:
        out_shape = [pair, pair, jax.ShapeDtypeStruct((rows, width), jnp.bfloat16)]
    else:
        out_shape = [jax.ShapeDtypeStruct((4, rows, OUT_BLOCK), jnp.float32)]
    return pl.pallas_call(
        functools.partial(project_kernel, first),
        out_shape=out_shape,
        in_specs=[pl.BlockSpec(memory_space=pltpu.SMEM)]
        + [vmem] * len(parts)
        + [pl.BlockSpec(memory_space=pltpu.HBM)],
        out_specs=[vmem] * len(out_shape),
        scratch_shapes=[
            pltpu.VMEM((4, width, OUT_BLOCK), jnp.bfloat16),
            pltpu.SemaphoreType.DMA((4,)),
        ],
        compiler_params=pltpu.CompilerParams(vmem_limit_bytes=20 << 20),
        cost_estimate=pl.CostEstimate(
            flops=2 * rows * width * OUT_BLOCK * 4, bytes_accessed=6 << 20, transcendentals=0
        ),
        name="project_first" if first else "project_second",
    )(idx, *parts, pltpu.with_memory_space_constraint(weight, pltpu.HBM))


def along_z(block, step):
    route = [
        (c * ZS + z, c * ZS + (z + (step if c == 0 else -step)) % ZS)
        for c in range(CORES)
        for z in range(ZS)
    ]
    return lax.ppermute(block, ("core", "z"), route)


def body(q, rkeys, rvalues, pkeys, pvalues, weight, segment_ids, block_mask):
    core, z = lax.axis_index("core"), lax.axis_index("z")
    kv, rkv, bias, q, *seen = prepare(
        block_mask, segment_ids, pkeys, pvalues, rkeys, rvalues, q
    )
    first, first_q = opposite(kv, "x", 1), opposite(q, "y", 1)
    second, second_q = opposite(kv, "x", -1), opposite(q, "y", -1)
    prev = shifted(rkv, ("x", "y", "core"), -1)
    first, first_q = lax.optimization_barrier((first, first_q))
    far, far_q = opposite(first, "x", 1), opposite(first_q, "y", 1)
    far, far_q, second, second_q, prev = lax.optimization_barrier(
        (far, far_q, second, second_q, prev)
    )
    mine = [kv, first, second, far]
    pieces = mine + [shifted(p, "core", 1) for p in mine]

    part = attend(seen[1], far_q, pieces)
    two = shifted(part, "y", 2)
    next_one = opposite(attend(seen[2], first_q, pieces), "y", -1)
    last_one = opposite(attend(seen[3], second_q, pieces), "y", 1)
    own_parts = [pltpu.with_memory_space_constraint(a, pltpu.HBM) for a in (prev, rkv, bias)]
    own = attend(seen[0], q, pieces, own_parts)

    sign = 1 - 2 * core
    idx = jnp.stack([(z + sign * o) % ZS for o in (-4, -2, 3, 1, -3, -1, 2, 0)]).astype(jnp.int32)
    one, two, att = project(idx, [own, two, next_one, last_one], weight)
    got_one = along_z(one, -1)
    got_two = along_z(two, 1)
    (rest,) = project(idx, [att], weight)
    back3 = along_z((rest[0] + got_one[0].astype(jnp.float32)).astype(jnp.bfloat16), -3)
    on2 = along_z((rest[2] + got_two[0].astype(jnp.float32)).astype(jnp.bfloat16), 2)
    back1 = along_z((rest[1] + got_one[1].astype(jnp.float32)).astype(jnp.bfloat16), -1)
    total = rest[3] + got_two[1].astype(jnp.float32)
    for part in (back1, on2, back3):
        total = total + part.astype(jnp.float32)
    return total.astype(jnp.bfloat16)


def solution(mesh):
    split = Mesh(mesh.devices.reshape(XS, YS, CORES, ZS), ("x", "y", "core", "z"))
    seq = ("x", "y", "core")
    placed = (P(seq, "z"),) * 5 + (P("z", None), P(), P())
    return jax.shard_map(
        body, mesh=split, in_specs=placed, out_specs=P(seq, "z"), check_vma=False
    )
```

```python
import functools
import math

import jax
import jax.numpy as jnp
from jax import lax
from jax.experimental import pallas as pl
from jax.experimental.pallas import tpu as pltpu
from jax.sharding import Mesh, PartitionSpec as P

H = 64
KVH = 8
CW = 128
TILE = 128
HEADS = H // KVH
XS, YS, CORES, ZS = 4, 4, 2, 8
ROWS = XS * YS * CORES * TILE
SHARE = 512
SHARES = XS * CORES
BLOCK = 256
NEG_FILL = -1e30
SCALE2 = math.log2(math.e) / math.sqrt(CW)
STATS = 3
QUIET = 64.0
QROWS = HEADS * TILE
OUT_BLOCK = 640


def seq_index(x, y, c):
    return (lax.rem(x, XS) * YS + lax.rem(y, YS)) * CORES + c


def shifted(block, axis, step):
    n = lax.axis_size(axis)
    return lax.ppermute(block, axis, [((i + step) % n, i) for i in range(n)])


def prepare_kernel(
    mask_hbm, pk_ref, pv_ref, rk_ref, rv_ref, q_hbm, kv_ref, rkv_ref, q_ref, *refs
):
    flag_refs, (mask_ref, sems) = refs[:4], refs[4:]
    x, y, core = (lax.axis_index(a) for a in ("x", "y", "core"))
    copies = [
        pltpu.make_async_copy(source, target, sems.at[i])
        for i, (source, target) in enumerate(
            (
                (mask_hbm, mask_ref),
                (pk_ref, kv_ref.at[:, :CW]),
                (pv_ref, kv_ref.at[:, CW:]),
                (rk_ref, rkv_ref.at[:, :CW]),
                (rv_ref, rkv_ref.at[:, CW:]),
            )
            + tuple(
                (q_hbm.at[:, i : i + 2 * CW], q_ref.at[i // 2 : i // 2 + TILE])
                for i in range(0, HEADS * CW, 2 * CW)
            )
        )
    ]
    for copy in copies:
        copy.start()
    for copy in copies:
        copy.wait()
    tiles = SHARE // TILE
    step = XS + 1 - 2 * core
    back = XS - 1 + 2 * core
    other = 1 - core
    shares = (
        (0, core), (step, core), (back, core), (2, core),
        (0, other), (back, other), (step, other), (2, other),
    )
    for flags, dy in zip(flag_refs, (0, 2, 1 - 2 * core, 2 * core - 1)):
        row = seq_index(x, y + dy + YS, core)
        for p, (dx, c) in enumerate(shares):
            first = seq_index(x + dx, y, c) * tiles
            for t in range(tiles):
                flags[p * tiles + t] = mask_ref[row, first + t]


def own_bias(seg_ref, bias_s):
    device = seq_index(*(lax.axis_index(a) for a in ("x", "y", "core")))
    mine = seg_ref[pl.ds(device, 1), :]
    before = seg_ref[pl.ds(jnp.maximum(device - 1, 0), 1), :]
    before = jnp.where(device > 0, before, -1)
    rows = jnp.broadcast_to(mine, (TILE, TILE)).T
    r = lax.broadcasted_iota(jnp.int32, (TILE, TILE), 0)
    c = lax.broadcasted_iota(jnp.int32, (TILE, TILE), 1)
    bias_s[:, :TILE] = jnp.where(rows == before, 0.0, NEG_FILL)
    bias_s[:, TILE:] = jnp.where((rows == mine) & (c <= r), 0.0, NEG_FILL)


def prepare(block_mask, pkeys, pvalues, rkeys, rvalues, q):
    vmem = pl.BlockSpec(memory_space=pltpu.VMEM)
    smem = pl.BlockSpec(memory_space=pltpu.SMEM)
    flags = jax.ShapeDtypeStruct((SHARES * SHARE // TILE,), jnp.int32)
    return pl.pallas_call(
        prepare_kernel,
        out_shape=[
            pltpu.VMEM((pkeys.shape[0], 2 * CW), jnp.bfloat16),
            pltpu.VMEM((TILE, 2 * CW), jnp.bfloat16),
            pltpu.VMEM((QROWS // 2, 2 * CW), q.dtype),
        ]
        + [flags] * 4,
        in_specs=[pl.BlockSpec(memory_space=pltpu.HBM)] * 6,
        out_specs=[vmem] * 3 + [smem] * 4,
        scratch_shapes=[
            pltpu.SMEM(block_mask.shape, jnp.int32),
            pltpu.SemaphoreType.DMA((9,)),
        ],
        compiler_params=pltpu.CompilerParams(vmem_limit_bytes=8 << 20),
        cost_estimate=pl.CostEstimate(flops=1, bytes_accessed=1, transcendentals=0),
        name="prepare",
    )(
        *(
            pltpu.with_memory_space_constraint(a, pltpu.HBM)
            for a in (block_mask, pkeys, pvalues, rkeys, rvalues, q)
        )
    )


def split_three(value):
    parts = []
    for _ in range(STATS):
        parts.append(value.astype(jnp.bfloat16).astype(jnp.float32))
        value = value - parts[-1]
    return parts


def opposite(block, axis, step):
    n = lax.axis_size(axis)
    route = [
        (((i + (step if c == 0 else -step)) % n) * CORES + c, i * CORES + c)
        for i in range(n)
        for c in range(CORES)
    ]
    return lax.ppermute(block, (axis, "core"), route)


def attend_kernel(own, flags_ref, q_ref, *refs):
    kv_refs, refs = refs[:SHARES], refs[SHARES:]
    if own:
        (prev_ref, mine_ref, seg_hbm), refs = refs[:3], refs[3:]
    out_ref, kv_s, q_s, m_s, acc_s, list_s, again_s = refs[:7]
    last = SHARES * SHARE
    copies = []
    if own:
        bias_s, seg_ref, sems = refs[7:]
        targets = (
            kv_s.at[last : last + TILE, : 2 * CW],
            kv_s.at[last + TILE : last + BLOCK, : 2 * CW],
            seg_ref,
        )
        for i, (source, target) in enumerate(zip((prev_ref, mine_ref, seg_hbm), targets)):
            copies.append(pltpu.make_async_copy(source, target, sems.at[i]))
            copies[-1].start()
    lanes = lax.broadcasted_iota(jnp.int32, (TILE, CW), 1)

    count = 0
    block = 0
    for ref in kv_refs:
        for b in range(ref.shape[0] // BLOCK):
            seen = flags_ref[2 * block] + flags_ref[2 * block + 1] > 0
            list_s[count] = block

            @pl.when(seen)
            def _():
                rows = slice(block * BLOCK, (block + 1) * BLOCK)
                kv_s[rows, : 2 * CW] = ref[b * BLOCK : (b + 1) * BLOCK]
                kv_s[rows, 2 * CW :] = jnp.ones((BLOCK, CW), jnp.bfloat16)

            count = count + jnp.where(seen, 1, 0)
            block += 1
    if own:
        kv_s[last:, 2 * CW :] = jnp.ones((BLOCK, CW), jnp.bfloat16)
    for h in range(HEADS):
        at = h // 2 * TILE
        q_s[h * TILE : (h + 1) * TILE, :] = q_ref[at : at + TILE, h % 2 * CW : (h % 2 + 1) * CW]

    def rows_of(i):
        return pl.ds(pl.multiple_of(list_s[i] * BLOCK, BLOCK), BLOCK)

    def joined(parts, axis):
        return parts[0] if len(parts) == 1 else jnp.concatenate(parts, axis=axis)

    def scores(first, size):
        k = joined([kv_s[rows_of(first + i), :CW] for i in range(size)], 0)
        s = lax.dot_general(q_s[...], k, (((1,), (1,)), ((), ())), preferred_element_type=jnp.float32)
        halves = []
        for i in range(size):
            b = list_s[first + i]
            for t in range(2):
                bias = jnp.where(flags_ref[2 * b + t] > 0, 0.0, NEG_FILL)
                at = 2 * i + t
                halves.append(s[:, at * TILE : (at + 1) * TILE] * SCALE2 + bias)
        return halves

    def own_scores():
        s = lax.dot_general(q_s[...], kv_s[last:, :CW], (((1,), (1,)), ((), ())), preferred_element_type=jnp.float32)
        s = (s.reshape(HEADS, TILE, BLOCK) * SCALE2 + bias_s[...][None]).reshape(QROWS, BLOCK)
        return [s[:, :TILE], s[:, TILE:]]

    def top_of(halves):
        m = jnp.max(functools.reduce(jnp.maximum, halves), axis=1, keepdims=True)
        return jnp.broadcast_to(m, (QROWS, TILE))

    def weigh(halves, v):
        m = m_s[...]
        p = jnp.concatenate([jnp.exp2(s - m).astype(jnp.bfloat16) for s in halves], axis=1)
        return jnp.dot(p, v, preferred_element_type=jnp.float32)

    def absorb(first, size):
        v = joined([kv_s[rows_of(first + i), CW:] for i in range(size)], 0)
        acc_s[...] += weigh(scores(first, size), v)

    def attempt(a, _):
        @pl.when(jnp.logical_or(a == 0, again_s[0] == 1))
        def _():
            @pl.when(a == 0)
            def _():
                m_s[...] = jnp.zeros_like(m_s)

            @pl.when(a == 1)
            def _():
                m_s[...] = top_of(own_scores()) if own else jnp.full_like(m_s, NEG_FILL)

                def top(i, _):
                    m_s[...] = jnp.maximum(m_s[...], top_of(scores(i, 1)))
                    return 0

                lax.fori_loop(0, count, top, 0)

            acc_s[...] = jnp.zeros_like(acc_s)
            done = 0
            for size in (4, 2, 1):

                def group(j, _, size=size, done=done):
                    absorb(done + j * size, size)
                    return 0

                loops = (count - done) // size
                lax.fori_loop(0, loops, group, 0)
                done = done + loops * size
            if own:
                acc_s[...] += weigh(own_scores(), kv_s[last:, CW:])
            raw = acc_s[:, CW:]
            total = jnp.maximum(raw, 1e-30)
            inverse = 1.0 / total
            log_total = jnp.log2(total)
            loud = jnp.max(jnp.abs(log_total)) > QUIET
            if not own:
                loud = jnp.logical_and(loud, count > 0)
            again_s[0] = jnp.where(loud, 1, 0)
            lse = m_s[...] + log_total
            if not own:
                lse = jnp.where(raw > 0, lse, NEG_FILL)
            head = lanes // STATS
            stats = lse[:TILE]
            for h in range(HEADS):
                rows = slice(h * TILE, (h + 1) * TILE)
                out_ref[:, h * CW : (h + 1) * CW] = (acc_s[rows, :CW] * inverse[rows]).astype(out_ref.dtype)
                stats = jnp.where(head == h, lse[rows], stats)
            if not own:
                a_, b_, c_ = split_three(stats)
                which = lanes % STATS
                stats = jnp.where(which == 0, a_, jnp.where(which == 1, b_, c_))
            out_ref[:, HEADS * CW :] = stats.astype(out_ref.dtype)
        return 0

    again_s[0] = 0
    for copy in copies:
        copy.wait()
    if own:
        own_bias(seg_ref, bias_s)
    lax.fori_loop(0, 2, attempt, 0)


def attend(flags, q, pieces, own_parts=None):
    own = own_parts is not None
    args = [flags, q, *pieces]
    vmem = pl.BlockSpec(memory_space=pltpu.VMEM)
    keys = SHARES * SHARE + BLOCK * own
    return pl.pallas_call(
        functools.partial(attend_kernel, own),
        out_shape=pltpu.VMEM((TILE, HEADS * CW + CW), jnp.float32 if own else jnp.bfloat16),
        in_specs=[pl.BlockSpec(memory_space=pltpu.SMEM)]
        + [vmem] * (len(args) - 1)
        + [pl.BlockSpec(memory_space=m) for m in (pl.ANY, pl.ANY, pltpu.HBM)] * own,
        out_specs=vmem,
        scratch_shapes=[
            pltpu.VMEM((keys, 3 * CW), jnp.bfloat16),
            pltpu.VMEM((QROWS, CW), jnp.bfloat16),
            pltpu.VMEM((QROWS, TILE), jnp.float32),
            pltpu.VMEM((QROWS, 2 * CW), jnp.float32),
            pltpu.SMEM((keys // BLOCK + 1,), jnp.int32),
            pltpu.SMEM((1,), jnp.int32),
        ]
        + [
            pltpu.VMEM((TILE, BLOCK), jnp.float32),
            pltpu.VMEM((ROWS // TILE, TILE), jnp.int32),
            pltpu.SemaphoreType.DMA((3,)),
        ]
        * own,
        compiler_params=pltpu.CompilerParams(vmem_limit_bytes=10 << 20),
        cost_estimate=pl.CostEstimate(
            flops=QROWS * 1024 * CW * 4, bytes_accessed=8388608, transcendentals=0
        ),
        name="attend_own" if own else "attend_other",
    )(*args, *(own_parts or ()))


def combine(refs, att_s):
    stats = [r[:, HEADS * CW :].astype(jnp.float32) for r in refs]
    for h in range(HEADS):
        cols = slice(h * CW, (h + 1) * CW)
        i = STATS * h
        lses = [stats[0][:, i : i + 1]]
        for st in stats[1:]:
            lses.append(st[:, i : i + 1] + st[:, i + 1 : i + 2] + st[:, i + 2 : i + 3])
        top = functools.reduce(jnp.maximum, lses)
        weights = [jnp.exp2(v - top) for v in lses]
        inverse = 1.0 / sum(weights)
        mixed = sum(r[:, cols].astype(jnp.float32) * (w * inverse) for r, w in zip(refs, weights))
        att_s[:, cols] = mixed.astype(jnp.bfloat16)


def project_kernel(first, *refs):
    if first:
        own_ref, a_ref, b_ref, c_ref, w_ref, one_ref, two_ref, att_ref, w_s, sems = refs
    else:
        att_ref, w_ref, out_ref, w_s, sems = refs
    z, sign = lax.axis_index("z"), 1 - 2 * lax.axis_index("core")
    copies = []
    for j, offset in enumerate((-4, -2, 3, 1) if first else (-3, -1, 2, 0)):
        block = lax.rem(z + sign * offset + ZS, ZS)
        start = pl.multiple_of(block * OUT_BLOCK, CW)
        copies.append(
            pltpu.make_async_copy(w_ref.at[:, pl.ds(start, OUT_BLOCK)], w_s.at[j], sems.at[j])
        )
        copies[-1].start()
    if first:
        combine((own_ref, a_ref, b_ref, c_ref), att_ref)
    for j in range(4):
        copies[j].wait()
        term = jnp.dot(att_ref[...], w_s[j], preferred_element_type=jnp.float32)
        if first:
            (one_ref, two_ref)[j // 2][j % 2] = term.astype(jnp.bfloat16)
        else:
            out_ref[j] = term


def project(parts, weight):
    first = len(parts) > 1
    rows, width = TILE, HEADS * CW
    vmem = pl.BlockSpec(memory_space=pltpu.VMEM)
    pair = jax.ShapeDtypeStruct((2, rows, OUT_BLOCK), jnp.bfloat16)
    if first:
        out_shape = [pair, pair, jax.ShapeDtypeStruct((rows, width), jnp.bfloat16)]
    else:
        out_shape = [jax.ShapeDtypeStruct((4, rows, OUT_BLOCK), jnp.float32)]
    return pl.pallas_call(
        functools.partial(project_kernel, first),
        out_shape=out_shape,
        in_specs=[vmem] * len(parts)
        + [pl.BlockSpec(memory_space=pltpu.HBM)],
        out_specs=[vmem] * len(out_shape),
        scratch_shapes=[
            pltpu.VMEM((4, width, OUT_BLOCK), jnp.bfloat16),
            pltpu.SemaphoreType.DMA((4,)),
        ],
        compiler_params=pltpu.CompilerParams(vmem_limit_bytes=9 << 20),
        cost_estimate=pl.CostEstimate(
            flops=2 * rows * width * OUT_BLOCK * 4, bytes_accessed=6 << 20, transcendentals=0
        ),
        name="project_first" if first else "project_second",
    )(*parts, pltpu.with_memory_space_constraint(weight, pltpu.HBM))


def along_z(block, step):
    route = [
        (c * ZS + z, c * ZS + (z + (step if c == 0 else -step)) % ZS)
        for c in range(CORES)
        for z in range(ZS)
    ]
    return lax.ppermute(block, ("core", "z"), route)


def body(q, rkeys, rvalues, pkeys, pvalues, weight, segment_ids, block_mask):
    kv, rkv, q, *seen = prepare(block_mask, pkeys, pvalues, rkeys, rvalues, q)
    first, first_q = opposite(kv, "x", 1), opposite(q, "y", 1)
    second, second_q = opposite(kv, "x", -1), opposite(q, "y", -1)
    prev = shifted(rkv, ("x", "y", "core"), -1)
    first, first_q, prev = lax.optimization_barrier((first, first_q, prev))
    far, far_q = opposite(first, "x", 1), opposite(first_q, "y", 1)
    far, far_q, second, second_q = lax.optimization_barrier((far, far_q, second, second_q))
    mine = [kv, first, second, far]
    pieces = mine + [shifted(p, "core", 1) for p in mine]

    part = attend(seen[1], far_q, pieces)
    two = shifted(part, "y", 2)
    next_one = opposite(attend(seen[2], first_q, pieces), "y", -1)
    last_one = opposite(attend(seen[3], second_q, pieces), "y", 1)
    segments = pltpu.with_memory_space_constraint(segment_ids.reshape(-1, TILE), pltpu.HBM)
    own = attend(seen[0], q, pieces, (prev, rkv, segments))

    one, two, att = project([own, two, next_one, last_one], weight)
    got_one = along_z(one, -1)
    got_two = along_z(two, 1)
    (rest,) = project([att], weight)
    back3 = along_z((rest[0] + got_one[0].astype(jnp.float32)).astype(jnp.bfloat16), -3)
    on2 = along_z((rest[2] + got_two[0].astype(jnp.float32)).astype(jnp.bfloat16), 2)
    back1 = along_z((rest[1] + got_one[1].astype(jnp.float32)).astype(jnp.bfloat16), -1)
    total = rest[3] + got_two[1].astype(jnp.float32)
    for part in (back1, on2, back3):
        total = total + part.astype(jnp.float32)
    return total.astype(jnp.bfloat16)


def solution(mesh):
    split = Mesh(mesh.devices.reshape(XS, YS, CORES, ZS), ("x", "y", "core", "z"))
    seq = ("x", "y", "core")
    placed = (P(seq, "z"),) * 5 + (P("z", None), P(), P())
    return jax.shard_map(
        body, mesh=split, in_specs=placed, out_specs=P(seq, "z"), check_vma=False
    )
```

```python
import functools
import math

import jax
import jax.numpy as jnp
from jax import lax
from jax.experimental import pallas as pl
from jax.experimental.pallas import tpu as pltpu
from jax.sharding import Mesh, PartitionSpec as P

H = 64
KVH = 8
CW = 128
TILE = 128
HEADS = H // KVH
XS, YS, CORES, ZS = 4, 4, 2, 8
ROWS = XS * YS * CORES * TILE
SHARE = 512
SHARES = XS * CORES
BLOCK = 256
NEG_FILL = -1e30
SCALE2 = math.log2(math.e) / math.sqrt(CW)
STATS = 3
QUIET = 64.0
QROWS = HEADS * TILE
OUT_BLOCK = 640


def seq_index(x, y, c):
    return (lax.rem(x, XS) * YS + lax.rem(y, YS)) * CORES + c


def shifted(block, axis, step):
    n = lax.axis_size(axis)
    return lax.ppermute(block, axis, [((i + step) % n, i) for i in range(n)])


def prepare_kernel(
    mask_hbm, pk_ref, pv_ref, rk_ref, rv_ref, q_hbm, kv_ref, rkv_ref, q_ref, *refs
):
    flag_refs, (mask_ref, sems) = refs[:4], refs[4:]
    x, y, core = (lax.axis_index(a) for a in ("x", "y", "core"))
    copies = [
        pltpu.make_async_copy(source, target, sems.at[i])
        for i, (source, target) in enumerate(
            (
                (mask_hbm, mask_ref),
                (pk_ref, kv_ref.at[:, :CW]),
                (pv_ref, kv_ref.at[:, CW:]),
                (rk_ref, rkv_ref.at[:, :CW]),
                (rv_ref, rkv_ref.at[:, CW:]),
            )
            + tuple(
                (q_hbm.at[:, i : i + 2 * CW], q_ref.at[i // 2 : i // 2 + TILE])
                for i in range(0, HEADS * CW, 2 * CW)
            )
        )
    ]
    for copy in copies:
        copy.start()
    copies[0].wait()
    tiles = SHARE // TILE
    step = XS + 1 - 2 * core
    back = XS - 1 + 2 * core
    other = 1 - core
    shares = (
        (0, core), (step, core), (back, core), (2, core),
        (0, other), (back, other), (step, other), (2, other),
    )
    for flags, dy in zip(flag_refs, (0, 2, 1 - 2 * core, 2 * core - 1)):
        row = seq_index(x, y + dy + YS, core)
        for p, (dx, c) in enumerate(shares):
            first = seq_index(x + dx, y, c) * tiles
            for t in range(tiles):
                flags[p * tiles + t] = mask_ref[row, first + t]
    for copy in copies[1:]:
        copy.wait()


def own_bias(seg_ref, bias_s):
    device = seq_index(*(lax.axis_index(a) for a in ("x", "y", "core")))
    mine = seg_ref[pl.ds(device, 1), :]
    before = seg_ref[pl.ds(jnp.maximum(device - 1, 0), 1), :]
    before = jnp.where(device > 0, before, -1)
    rows = jnp.broadcast_to(mine, (TILE, TILE)).T
    r = lax.broadcasted_iota(jnp.int32, (TILE, TILE), 0)
    c = lax.broadcasted_iota(jnp.int32, (TILE, TILE), 1)
    bias_s[:, :TILE] = jnp.where(rows == before, 0.0, NEG_FILL)
    bias_s[:, TILE:] = jnp.where((rows == mine) & (c <= r), 0.0, NEG_FILL)


def prepare(block_mask, pkeys, pvalues, rkeys, rvalues, q):
    vmem = pl.BlockSpec(memory_space=pltpu.VMEM)
    smem = pl.BlockSpec(memory_space=pltpu.SMEM)
    flags = jax.ShapeDtypeStruct((SHARES * SHARE // TILE,), jnp.int32)
    return pl.pallas_call(
        prepare_kernel,
        out_shape=[
            pltpu.VMEM((pkeys.shape[0], 2 * CW), jnp.bfloat16),
            pltpu.VMEM((TILE, 2 * CW), jnp.bfloat16),
            pltpu.VMEM((QROWS // 2, 2 * CW), q.dtype),
        ]
        + [flags] * 4,
        in_specs=[pl.BlockSpec(memory_space=pltpu.HBM)] * 6,
        out_specs=[vmem] * 3 + [smem] * 4,
        scratch_shapes=[
            pltpu.SMEM(block_mask.shape, jnp.int32),
            pltpu.SemaphoreType.DMA((9,)),
        ],
        compiler_params=pltpu.CompilerParams(vmem_limit_bytes=8 << 20),
        cost_estimate=pl.CostEstimate(flops=1, bytes_accessed=1, transcendentals=0),
        name="prepare",
    )(
        *(
            pltpu.with_memory_space_constraint(a, pltpu.HBM)
            for a in (block_mask, pkeys, pvalues, rkeys, rvalues, q)
        )
    )


def split_three(value):
    parts = []
    for _ in range(STATS):
        parts.append(value.astype(jnp.bfloat16).astype(jnp.float32))
        value = value - parts[-1]
    return parts


def opposite(block, axis, step):
    n = lax.axis_size(axis)
    route = [
        (((i + (step if c == 0 else -step)) % n) * CORES + c, i * CORES + c)
        for i in range(n)
        for c in range(CORES)
    ]
    return lax.ppermute(block, (axis, "core"), route)


def attend_kernel(own, flags_ref, q_ref, *refs):
    kv_refs, refs = refs[:SHARES], refs[SHARES:]
    if own:
        (prev_ref, mine_ref, seg_hbm), refs = refs[:3], refs[3:]
    out_ref, kv_s, q_s, m_s, acc_s, list_s, again_s = refs[:7]
    last = SHARES * SHARE
    copies = []
    if own:
        bias_s, seg_ref, sems = refs[7:]
        targets = (
            kv_s.at[last : last + TILE, : 2 * CW],
            kv_s.at[last + TILE : last + BLOCK, : 2 * CW],
            seg_ref,
        )
        for i, (source, target) in enumerate(zip((prev_ref, mine_ref, seg_hbm), targets)):
            copies.append(pltpu.make_async_copy(source, target, sems.at[i]))
            copies[-1].start()
    lanes = lax.broadcasted_iota(jnp.int32, (TILE, CW), 1)

    count = 0
    block = 0
    for ref in kv_refs:
        for b in range(ref.shape[0] // BLOCK):
            seen = flags_ref[2 * block] + flags_ref[2 * block + 1] > 0
            list_s[count] = block

            @pl.when(seen)
            def _():
                rows = slice(block * BLOCK, (block + 1) * BLOCK)
                kv_s[rows, : 2 * CW] = ref[b * BLOCK : (b + 1) * BLOCK]
                kv_s[rows, 2 * CW :] = jnp.ones((BLOCK, CW), jnp.bfloat16)

            count = count + jnp.where(seen, 1, 0)
            block += 1
    if own:
        kv_s[last:, 2 * CW :] = jnp.ones((BLOCK, CW), jnp.bfloat16)
    for h in range(HEADS):
        at = h // 2 * TILE
        q_s[h * TILE : (h + 1) * TILE, :] = q_ref[at : at + TILE, h % 2 * CW : (h % 2 + 1) * CW]

    def rows_of(i):
        return pl.ds(pl.multiple_of(list_s[i] * BLOCK, BLOCK), BLOCK)

    def joined(parts, axis):
        return parts[0] if len(parts) == 1 else jnp.concatenate(parts, axis=axis)

    def scores(first, size):
        k = joined([kv_s[rows_of(first + i), :CW] for i in range(size)], 0)
        s = lax.dot_general(q_s[...], k, (((1,), (1,)), ((), ())), preferred_element_type=jnp.float32)
        halves = []
        for i in range(size):
            b = list_s[first + i]
            for t in range(2):
                bias = jnp.where(flags_ref[2 * b + t] > 0, 0.0, NEG_FILL)
                at = 2 * i + t
                halves.append(s[:, at * TILE : (at + 1) * TILE] * SCALE2 + bias)
        return halves

    def own_scores():
        s = lax.dot_general(q_s[...], kv_s[last:, :CW], (((1,), (1,)), ((), ())), preferred_element_type=jnp.float32)
        s = (s.reshape(HEADS, TILE, BLOCK) * SCALE2 + bias_s[...][None]).reshape(QROWS, BLOCK)
        return [s[:, :TILE], s[:, TILE:]]

    def top_of(halves):
        m = jnp.max(functools.reduce(jnp.maximum, halves), axis=1, keepdims=True)
        return jnp.broadcast_to(m, (QROWS, TILE))

    def weigh(halves, v):
        m = m_s[...]
        p = jnp.concatenate([jnp.exp2(s - m).astype(jnp.bfloat16) for s in halves], axis=1)
        return jnp.dot(p, v, preferred_element_type=jnp.float32)

    def absorb(first, size):
        v = joined([kv_s[rows_of(first + i), CW:] for i in range(size)], 0)
        acc_s[...] += weigh(scores(first, size), v)

    def attempt(a, _):
        @pl.when(jnp.logical_or(a == 0, again_s[0] == 1))
        def _():
            @pl.when(a == 0)
            def _():
                m_s[...] = jnp.zeros_like(m_s)

            @pl.when(a == 1)
            def _():
                m_s[...] = top_of(own_scores()) if own else jnp.full_like(m_s, NEG_FILL)

                def top(i, _):
                    m_s[...] = jnp.maximum(m_s[...], top_of(scores(i, 1)))
                    return 0

                lax.fori_loop(0, count, top, 0)

            acc_s[...] = jnp.zeros_like(acc_s)
            done = 0
            for size in (4, 2, 1):

                def group(j, _, size=size, done=done):
                    absorb(done + j * size, size)
                    return 0

                loops = (count - done) // size
                lax.fori_loop(0, loops, group, 0)
                done = done + loops * size
            if own:
                acc_s[...] += weigh(own_scores(), kv_s[last:, CW:])
            raw = acc_s[:, CW:]
            total = jnp.maximum(raw, 1e-30)
            inverse = 1.0 / total
            log_total = jnp.log2(total)
            loud = jnp.max(jnp.abs(log_total)) > QUIET
            if not own:
                loud = jnp.logical_and(loud, count > 0)
            again_s[0] = jnp.where(loud, 1, 0)
            lse = m_s[...] + log_total
            if not own:
                lse = jnp.where(raw > 0, lse, NEG_FILL)
            head = lanes // STATS
            stats = lse[:TILE]
            for h in range(HEADS):
                rows = slice(h * TILE, (h + 1) * TILE)
                out_ref[:, h * CW : (h + 1) * CW] = (acc_s[rows, :CW] * inverse[rows]).astype(out_ref.dtype)
                stats = jnp.where(head == h, lse[rows], stats)
            if not own:
                a_, b_, c_ = split_three(stats)
                which = lanes % STATS
                stats = jnp.where(which == 0, a_, jnp.where(which == 1, b_, c_))
            out_ref[:, HEADS * CW :] = stats.astype(out_ref.dtype)
        return 0

    again_s[0] = 0
    for copy in copies:
        copy.wait()
    if own:
        own_bias(seg_ref, bias_s)
    lax.fori_loop(0, 2, attempt, 0)


def attend(flags, q, pieces, own_parts=None):
    own = own_parts is not None
    args = [flags, q, *pieces]
    vmem = pl.BlockSpec(memory_space=pltpu.VMEM)
    keys = SHARES * SHARE + BLOCK * own
    return pl.pallas_call(
        functools.partial(attend_kernel, own),
        out_shape=pltpu.VMEM((TILE, HEADS * CW + CW), jnp.float32 if own else jnp.bfloat16),
        in_specs=[pl.BlockSpec(memory_space=pltpu.SMEM)]
        + [vmem] * (len(args) - 1)
        + [pl.BlockSpec(memory_space=m) for m in (pl.ANY, pl.ANY, pltpu.HBM)] * own,
        out_specs=vmem,
        scratch_shapes=[
            pltpu.VMEM((keys, 3 * CW), jnp.bfloat16),
            pltpu.VMEM((QROWS, CW), jnp.bfloat16),
            pltpu.VMEM((QROWS, TILE), jnp.float32),
            pltpu.VMEM((QROWS, 2 * CW), jnp.float32),
            pltpu.SMEM((keys // BLOCK + 1,), jnp.int32),
            pltpu.SMEM((1,), jnp.int32),
        ]
        + [
            pltpu.VMEM((TILE, BLOCK), jnp.float32),
            pltpu.VMEM((ROWS // TILE, TILE), jnp.int32),
            pltpu.SemaphoreType.DMA((3,)),
        ]
        * own,
        compiler_params=pltpu.CompilerParams(vmem_limit_bytes=10 << 20),
        cost_estimate=pl.CostEstimate(
            flops=QROWS * 1024 * CW * 4, bytes_accessed=8388608, transcendentals=0
        ),
        name="attend_own" if own else "attend_other",
    )(*args, *(own_parts or ()))


def combine(refs, att_s):
    stats = [r[:, HEADS * CW :].astype(jnp.float32) for r in refs]
    for h in range(HEADS):
        cols = slice(h * CW, (h + 1) * CW)
        i = STATS * h
        lses = [stats[0][:, i : i + 1]]
        for st in stats[1:]:
            lses.append(st[:, i : i + 1] + st[:, i + 1 : i + 2] + st[:, i + 2 : i + 3])
        top = functools.reduce(jnp.maximum, lses)
        weights = [jnp.exp2(v - top) for v in lses]
        inverse = 1.0 / sum(weights)
        mixed = sum(r[:, cols].astype(jnp.float32) * (w * inverse) for r, w in zip(refs, weights))
        att_s[:, cols] = mixed.astype(jnp.bfloat16)


def project_kernel(first, *refs):
    if first:
        own_ref, a_ref, b_ref, c_ref, w_ref, one_ref, two_ref, att_ref, w_s, sems = refs
        offsets, targets = (-4, -2, 3), (one_ref.at[0], one_ref.at[1], two_ref)
    else:
        att_ref, w_ref, direct_ref, rest_ref, w_s, sems = refs
        offsets, targets = (1, -3, -1, 2, 0), (direct_ref, *(rest_ref.at[j] for j in range(4)))
    z, sign = lax.axis_index("z"), 1 - 2 * lax.axis_index("core")
    copies = []
    for j, offset in enumerate(offsets):
        block = lax.rem(z + sign * offset + ZS, ZS)
        start = pl.multiple_of(block * OUT_BLOCK, CW)
        copies.append(
            pltpu.make_async_copy(w_ref.at[:, pl.ds(start, OUT_BLOCK)], w_s.at[j], sems.at[j])
        )
        copies[-1].start()
    if first:
        combine((own_ref, a_ref, b_ref, c_ref), att_ref)
    for j, target in enumerate(targets):
        copies[j].wait()
        term = jnp.dot(att_ref[...], w_s[j], preferred_element_type=jnp.float32)
        target[...] = term.astype(target.dtype)


def project(parts, weight):
    first = len(parts) > 1
    rows, width = TILE, HEADS * CW
    vmem = pl.BlockSpec(memory_space=pltpu.VMEM)
    one = jax.ShapeDtypeStruct((rows, OUT_BLOCK), jnp.bfloat16)
    if first:
        pair = jax.ShapeDtypeStruct((2, rows, OUT_BLOCK), jnp.bfloat16)
        out_shape = [pair, one, jax.ShapeDtypeStruct((rows, width), jnp.bfloat16)]
    else:
        out_shape = [one, jax.ShapeDtypeStruct((4, rows, OUT_BLOCK), jnp.float32)]
    blocks = 3 if first else 5
    return pl.pallas_call(
        functools.partial(project_kernel, first),
        out_shape=out_shape,
        in_specs=[vmem] * len(parts) + [pl.BlockSpec(memory_space=pltpu.HBM)],
        out_specs=[vmem] * len(out_shape),
        scratch_shapes=[
            pltpu.VMEM((blocks, width, OUT_BLOCK), jnp.bfloat16),
            pltpu.SemaphoreType.DMA((blocks,)),
        ],
        compiler_params=pltpu.CompilerParams(vmem_limit_bytes=12 << 20),
        cost_estimate=pl.CostEstimate(
            flops=2 * rows * width * OUT_BLOCK * 4, bytes_accessed=6 << 20, transcendentals=0
        ),
        name="project_first" if first else "project_second",
    )(*parts, pltpu.with_memory_space_constraint(weight, pltpu.HBM))


def along_z(block, step):
    route = [
        (c * ZS + z, c * ZS + (z + (step if c == 0 else -step)) % ZS)
        for c in range(CORES)
        for z in range(ZS)
    ]
    return lax.ppermute(block, ("core", "z"), route)


def body(q, rkeys, rvalues, pkeys, pvalues, weight, segment_ids, block_mask):
    kv, rkv, q, *seen = prepare(block_mask, pkeys, pvalues, rkeys, rvalues, q)
    first, first_q = opposite(kv, "x", 1), opposite(q, "y", 1)
    second, second_q = opposite(kv, "x", -1), opposite(q, "y", -1)
    prev = shifted(rkv, ("x", "y", "core"), -1)
    first, first_q = lax.optimization_barrier((first, first_q))
    far = opposite(first, "x", 1)
    first_q, prev = lax.optimization_barrier((first_q, prev))
    far_q = opposite(first_q, "y", 1)
    far, far_q, second, second_q = lax.optimization_barrier((far, far_q, second, second_q))
    mine = [kv, first, second, far]
    pieces = mine + [shifted(p, "core", 1) for p in mine]

    part = attend(seen[1], far_q, pieces)
    two = shifted(part, "y", 2)
    next_one = opposite(attend(seen[2], first_q, pieces), "y", -1)
    last_one = opposite(attend(seen[3], second_q, pieces), "y", 1)
    segments = pltpu.with_memory_space_constraint(segment_ids.reshape(-1, TILE), pltpu.HBM)
    own = attend(seen[0], q, pieces, (prev, rkv, segments))

    one, two, att = project([own, two, next_one, last_one], weight)
    got_one, got_two = along_z(one, -1), along_z(two, 1)
    direct, rest = project([att], weight)
    got_direct = along_z(direct, 1)
    back3 = along_z((rest[0] + got_one[0].astype(jnp.float32)).astype(jnp.bfloat16), -3)
    on2 = along_z((rest[2] + got_two.astype(jnp.float32)).astype(jnp.bfloat16), 2)
    back1 = (rest[1] + got_one[1].astype(jnp.float32)).astype(jnp.bfloat16)
    back1, got_direct = lax.optimization_barrier((back1, got_direct))
    back1 = along_z(back1, -1)
    total = rest[3] + got_direct.astype(jnp.float32)
    for part in (back1, on2, back3):
        total = total + part.astype(jnp.float32)
    return total.astype(jnp.bfloat16)


def solution(mesh):
    split = Mesh(mesh.devices.reshape(XS, YS, CORES, ZS), ("x", "y", "core", "z"))
    seq = ("x", "y", "core")
    placed = (P(seq, "z"),) * 5 + (P("z", None), P(), P())
    return jax.shard_map(
        body, mesh=split, in_specs=placed, out_specs=P(seq, "z"), check_vma=False
    )
```

```python
import functools
import math

import jax
import jax.numpy as jnp
from jax import lax
from jax.experimental import pallas as pl
from jax.experimental.pallas import tpu as pltpu
from jax.sharding import Mesh, PartitionSpec as P

H = 64
KVH = 8
CW = 128
TILE = 128
HEADS = H // KVH
XS, YS, CORES, ZS = 4, 4, 2, 8
ROWS = XS * YS * CORES * TILE
SHARE = 512
SHARES = XS * CORES
BLOCK = 256
NEG_FILL = -1e30
SCALE2 = math.log2(math.e) / math.sqrt(CW)
STATS = 3
QUIET = 64.0
QROWS = HEADS * TILE
OUT_BLOCK = 640


def seq_index(x, y, c):
    return (lax.rem(x, XS) * YS + lax.rem(y, YS)) * CORES + c


def shifted(block, axis, step):
    n = lax.axis_size(axis)
    return lax.ppermute(block, axis, [((i + step) % n, i) for i in range(n)])


def own_bias(seg_ref, bias_s):
    device = seq_index(*(lax.axis_index(a) for a in ("x", "y", "core")))
    mine = seg_ref[pl.ds(device, 1), :]
    before = seg_ref[pl.ds(jnp.maximum(device - 1, 0), 1), :]
    before = jnp.where(device > 0, before, -1)
    rows = jnp.broadcast_to(mine, (TILE, TILE)).T
    r = lax.broadcasted_iota(jnp.int32, (TILE, TILE), 0)
    c = lax.broadcasted_iota(jnp.int32, (TILE, TILE), 1)
    bias_s[:, :TILE] = jnp.where(rows == before, 0.0, NEG_FILL)
    bias_s[:, TILE:] = jnp.where((rows == mine) & (c <= r), 0.0, NEG_FILL)


def prepare_kernel(pk_ref, pv_ref, rk_ref, rv_ref, q_hbm, kv_ref, rkv_ref, q_ref, sems):
    moves = (
        (pk_ref, kv_ref.at[:, :CW]),
        (pv_ref, kv_ref.at[:, CW:]),
        (rk_ref, rkv_ref.at[:, :CW]),
        (rv_ref, rkv_ref.at[:, CW:]),
    ) + tuple(
        (q_hbm.at[:, i : i + 2 * CW], q_ref.at[i // 2 : i // 2 + TILE])
        for i in range(0, HEADS * CW, 2 * CW)
    )
    copies = [pltpu.make_async_copy(a, b, sems.at[i]) for i, (a, b) in enumerate(moves)]
    for copy in copies:
        copy.start()
    for copy in copies:
        copy.wait()


def prepare(pkeys, pvalues, rkeys, rvalues, q):
    return pl.pallas_call(
        prepare_kernel,
        out_shape=[
            pltpu.VMEM((pkeys.shape[0], 2 * CW), jnp.bfloat16),
            pltpu.VMEM((TILE, 2 * CW), jnp.bfloat16),
            pltpu.VMEM((QROWS // 2, 2 * CW), q.dtype),
        ],
        in_specs=[pl.BlockSpec(memory_space=pltpu.HBM)] * 5,
        out_specs=[pl.BlockSpec(memory_space=pltpu.VMEM)] * 3,
        scratch_shapes=[pltpu.SemaphoreType.DMA((8,))],
        compiler_params=pltpu.CompilerParams(vmem_limit_bytes=8 << 20),
        cost_estimate=pl.CostEstimate(flops=1, bytes_accessed=1, transcendentals=0),
        name="prepare",
    )(
        *(
            pltpu.with_memory_space_constraint(a, pltpu.HBM)
            for a in (pkeys, pvalues, rkeys, rvalues, q)
        )
    )


def visibility_kernel(mask_hbm, *refs):
    flag_refs, (mask_ref, sem) = refs[:4], refs[4:]
    copy = pltpu.make_async_copy(mask_hbm, mask_ref, sem)
    copy.start()
    copy.wait()
    x, y, core = (lax.axis_index(a) for a in ("x", "y", "core"))
    tiles = SHARE // TILE
    step = XS + 1 - 2 * core
    back = XS - 1 + 2 * core
    other = 1 - core
    shares = (
        (0, core), (step, core), (back, core), (2, core),
        (0, other), (back, other), (step, other), (2, other),
    )
    for flags, dy in zip(flag_refs, (0, 2, 1 - 2 * core, 2 * core - 1)):
        row = seq_index(x, y + dy + YS, core)
        for p, (dx, c) in enumerate(shares):
            first = seq_index(x + dx, y, c) * tiles
            for t in range(tiles):
                flags[p * tiles + t] = mask_ref[row, first + t]


def visibility(block_mask):
    return pl.pallas_call(
        visibility_kernel,
        out_shape=[jax.ShapeDtypeStruct((SHARES * SHARE // TILE,), jnp.int32)] * 4,
        in_specs=[pl.BlockSpec(memory_space=pltpu.HBM)],
        out_specs=[pl.BlockSpec(memory_space=pltpu.SMEM)] * 4,
        scratch_shapes=[pltpu.SMEM(block_mask.shape, jnp.int32), pltpu.SemaphoreType.DMA(())],
        compiler_params=pltpu.CompilerParams(vmem_limit_bytes=4 << 20),
        cost_estimate=pl.CostEstimate(flops=1, bytes_accessed=1, transcendentals=0),
        name="visibility",
    )(pltpu.with_memory_space_constraint(block_mask, pltpu.HBM))


def split_three(value):
    parts = []
    for _ in range(STATS):
        parts.append(value.astype(jnp.bfloat16).astype(jnp.float32))
        value = value - parts[-1]
    return parts


def opposite(block, axis, step):
    n = lax.axis_size(axis)
    route = [
        (((i + (step if c == 0 else -step)) % n) * CORES + c, i * CORES + c)
        for i in range(n)
        for c in range(CORES)
    ]
    return lax.ppermute(block, (axis, "core"), route)


def attend_kernel(own, flags_ref, q_ref, *refs):
    kv_refs, refs = refs[:SHARES], refs[SHARES:]
    if own:
        (prev_ref, mine_ref, seg_hbm), refs = refs[:3], refs[3:]
    out_ref, kv_s, q_s, m_s, acc_s, list_s, again_s = refs[:7]
    last = SHARES * SHARE
    copies = []
    if own:
        bias_s, seg_ref, sems = refs[7:]
        targets = (
            kv_s.at[last : last + TILE, : 2 * CW],
            kv_s.at[last + TILE : last + BLOCK, : 2 * CW],
            seg_ref,
        )
        for i, (source, target) in enumerate(zip((prev_ref, mine_ref, seg_hbm), targets)):
            copies.append(pltpu.make_async_copy(source, target, sems.at[i]))
            copies[-1].start()
    lanes = lax.broadcasted_iota(jnp.int32, (TILE, CW), 1)

    count = 0
    block = 0
    for ref in kv_refs:
        for b in range(ref.shape[0] // BLOCK):
            seen = flags_ref[2 * block] + flags_ref[2 * block + 1] > 0
            list_s[count] = block

            @pl.when(seen)
            def _():
                rows = slice(block * BLOCK, (block + 1) * BLOCK)
                kv_s[rows, : 2 * CW] = ref[b * BLOCK : (b + 1) * BLOCK]
                kv_s[rows, 2 * CW :] = jnp.ones((BLOCK, CW), jnp.bfloat16)

            count = count + jnp.where(seen, 1, 0)
            block += 1
    if own:
        kv_s[last:, 2 * CW :] = jnp.ones((BLOCK, CW), jnp.bfloat16)
    for h in range(HEADS):
        at = h // 2 * TILE
        q_s[h * TILE : (h + 1) * TILE, :] = q_ref[at : at + TILE, h % 2 * CW : (h % 2 + 1) * CW]

    def rows_of(i):
        return pl.ds(pl.multiple_of(list_s[i] * BLOCK, BLOCK), BLOCK)

    def joined(parts, axis):
        return parts[0] if len(parts) == 1 else jnp.concatenate(parts, axis=axis)

    def scores(first, size):
        k = joined([kv_s[rows_of(first + i), :CW] for i in range(size)], 0)
        s = lax.dot_general(q_s[...], k, (((1,), (1,)), ((), ())), preferred_element_type=jnp.float32)
        halves = []
        for i in range(size):
            b = list_s[first + i]
            for t in range(2):
                bias = jnp.where(flags_ref[2 * b + t] > 0, 0.0, NEG_FILL)
                at = 2 * i + t
                halves.append(s[:, at * TILE : (at + 1) * TILE] * SCALE2 + bias)
        return halves

    def own_scores():
        s = lax.dot_general(q_s[...], kv_s[last:, :CW], (((1,), (1,)), ((), ())), preferred_element_type=jnp.float32)
        s = (s.reshape(HEADS, TILE, BLOCK) * SCALE2 + bias_s[...][None]).reshape(QROWS, BLOCK)
        return [s[:, :TILE], s[:, TILE:]]

    def top_of(halves):
        m = jnp.max(functools.reduce(jnp.maximum, halves), axis=1, keepdims=True)
        return jnp.broadcast_to(m, (QROWS, TILE))

    def weigh(halves, v):
        m = m_s[...]
        p = jnp.concatenate([jnp.exp2(s - m).astype(jnp.bfloat16) for s in halves], axis=1)
        return jnp.dot(p, v, preferred_element_type=jnp.float32)

    def absorb(first, size):
        v = joined([kv_s[rows_of(first + i), CW:] for i in range(size)], 0)
        acc_s[...] += weigh(scores(first, size), v)

    def attempt(a, _):
        @pl.when(jnp.logical_or(a == 0, again_s[0] == 1))
        def _():
            @pl.when(a == 0)
            def _():
                m_s[...] = jnp.zeros_like(m_s)

            @pl.when(a == 1)
            def _():
                m_s[...] = top_of(own_scores()) if own else jnp.full_like(m_s, NEG_FILL)

                def top(i, _):
                    m_s[...] = jnp.maximum(m_s[...], top_of(scores(i, 1)))
                    return 0

                lax.fori_loop(0, count, top, 0)

            acc_s[...] = jnp.zeros_like(acc_s)
            done = 0
            for size in (4, 2, 1):

                def group(j, _, size=size, done=done):
                    absorb(done + j * size, size)
                    return 0

                loops = (count - done) // size
                lax.fori_loop(0, loops, group, 0)
                done = done + loops * size
            if own:
                acc_s[...] += weigh(own_scores(), kv_s[last:, CW:])
            raw = acc_s[:, CW:]
            total = jnp.maximum(raw, 1e-30)
            inverse = 1.0 / total
            log_total = jnp.log2(total)
            loud = jnp.max(jnp.abs(log_total)) > QUIET
            if not own:
                loud = jnp.logical_and(loud, count > 0)
            again_s[0] = jnp.where(loud, 1, 0)
            lse = m_s[...] + log_total
            if not own:
                lse = jnp.where(raw > 0, lse, NEG_FILL)
            head = lanes // STATS
            stats = lse[:TILE]
            for h in range(HEADS):
                rows = slice(h * TILE, (h + 1) * TILE)
                out_ref[:, h * CW : (h + 1) * CW] = (acc_s[rows, :CW] * inverse[rows]).astype(out_ref.dtype)
                stats = jnp.where(head == h, lse[rows], stats)
            if not own:
                a_, b_, c_ = split_three(stats)
                which = lanes % STATS
                stats = jnp.where(which == 0, a_, jnp.where(which == 1, b_, c_))
            out_ref[:, HEADS * CW :] = stats.astype(out_ref.dtype)
        return 0

    again_s[0] = 0
    for copy in copies:
        copy.wait()
    if own:
        own_bias(seg_ref, bias_s)
    lax.fori_loop(0, 2, attempt, 0)


def attend(flags, q, pieces, own_parts=None):
    own = own_parts is not None
    args = [flags, q, *pieces]
    vmem = pl.BlockSpec(memory_space=pltpu.VMEM)
    keys = SHARES * SHARE + BLOCK * own
    return pl.pallas_call(
        functools.partial(attend_kernel, own),
        out_shape=pltpu.VMEM((TILE, HEADS * CW + CW), jnp.float32 if own else jnp.bfloat16),
        in_specs=[pl.BlockSpec(memory_space=pltpu.SMEM)]
        + [vmem] * (len(args) - 1)
        + [pl.BlockSpec(memory_space=m) for m in (pl.ANY, pl.ANY, pltpu.HBM)] * own,
        out_specs=vmem,
        scratch_shapes=[
            pltpu.VMEM((keys, 3 * CW), jnp.bfloat16),
            pltpu.VMEM((QROWS, CW), jnp.bfloat16),
            pltpu.VMEM((QROWS, TILE), jnp.float32),
            pltpu.VMEM((QROWS, 2 * CW), jnp.float32),
            pltpu.SMEM((keys // BLOCK + 1,), jnp.int32),
            pltpu.SMEM((1,), jnp.int32),
        ]
        + [
            pltpu.VMEM((TILE, BLOCK), jnp.float32),
            pltpu.VMEM((ROWS // TILE, TILE), jnp.int32),
            pltpu.SemaphoreType.DMA((3,)),
        ]
        * own,
        compiler_params=pltpu.CompilerParams(vmem_limit_bytes=10 << 20),
        cost_estimate=pl.CostEstimate(
            flops=QROWS * 1024 * CW * 4, bytes_accessed=8388608, transcendentals=0
        ),
        name="attend_own" if own else "attend_other",
    )(*args, *(own_parts or ()))


def combine(refs, att_s):
    stats = [r[:, HEADS * CW :].astype(jnp.float32) for r in refs]
    for h in range(HEADS):
        cols = slice(h * CW, (h + 1) * CW)
        i = STATS * h
        lses = [stats[0][:, i : i + 1]]
        for st in stats[1:]:
            lses.append(st[:, i : i + 1] + st[:, i + 1 : i + 2] + st[:, i + 2 : i + 3])
        top = functools.reduce(jnp.maximum, lses)
        weights = [jnp.exp2(v - top) for v in lses]
        inverse = 1.0 / sum(weights)
        mixed = sum(r[:, cols].astype(jnp.float32) * (w * inverse) for r, w in zip(refs, weights))
        att_s[:, cols] = mixed.astype(jnp.bfloat16)


def project_kernel(first, *refs):
    if first:
        own_ref, a_ref, b_ref, c_ref, w_ref, *targets, att_ref, w_s, sems = refs
        offsets = (-4, 3, -2)
    else:
        att_ref, w_ref, *targets, w_s, sems = refs
        offsets = (1, -3, 2, -1, 0)
    z, sign = lax.axis_index("z"), 1 - 2 * lax.axis_index("core")
    copies = []
    for j, offset in enumerate(offsets):
        block = lax.rem(z + sign * offset + ZS, ZS)
        start = pl.multiple_of(block * OUT_BLOCK, CW)
        copies.append(
            pltpu.make_async_copy(w_ref.at[:, pl.ds(start, OUT_BLOCK)], w_s.at[j], sems.at[j])
        )
        copies[-1].start()
    if first:
        combine((own_ref, a_ref, b_ref, c_ref), att_ref)
    for j, target in enumerate(targets):
        copies[j].wait()
        term = jnp.dot(att_ref[...], w_s[j], preferred_element_type=jnp.float32)
        target[...] = term.astype(target.dtype)


def project(parts, weight):
    first = len(parts) > 1
    rows, width = TILE, HEADS * CW
    vmem = pl.BlockSpec(memory_space=pltpu.VMEM)
    one = jax.ShapeDtypeStruct((rows, OUT_BLOCK), jnp.bfloat16)
    if first:
        out_shape = [one] * 3 + [jax.ShapeDtypeStruct((rows, width), jnp.bfloat16)]
    else:
        out_shape = [one] + [jax.ShapeDtypeStruct(one.shape, jnp.float32)] * 4
    blocks = 3 if first else 5
    return pl.pallas_call(
        functools.partial(project_kernel, first),
        out_shape=out_shape,
        in_specs=[vmem] * len(parts) + [pl.BlockSpec(memory_space=pltpu.HBM)],
        out_specs=[vmem] * len(out_shape),
        scratch_shapes=[
            pltpu.VMEM((blocks, width, OUT_BLOCK), jnp.bfloat16),
            pltpu.SemaphoreType.DMA((blocks,)),
        ],
        compiler_params=pltpu.CompilerParams(vmem_limit_bytes=12 << 20),
        cost_estimate=pl.CostEstimate(
            flops=2 * rows * width * OUT_BLOCK * 4, bytes_accessed=6 << 20, transcendentals=0
        ),
        name="project_first" if first else "project_second",
    )(*parts, pltpu.with_memory_space_constraint(weight, pltpu.HBM))


def along_z(block, step):
    route = [
        (c * ZS + z, c * ZS + (z + (step if c == 0 else -step)) % ZS)
        for c in range(CORES)
        for z in range(ZS)
    ]
    return lax.ppermute(block, ("core", "z"), route)


def body(q, rkeys, rvalues, pkeys, pvalues, weight, segment_ids, block_mask):
    kv, rkv, q = prepare(pkeys, pvalues, rkeys, rvalues, q)
    first, first_q = opposite(kv, "x", 1), opposite(q, "y", 1)
    second, second_q = opposite(kv, "x", -1), opposite(q, "y", -1)
    prev = shifted(rkv, ("x", "y", "core"), -1)
    first, first_q, seen = lax.optimization_barrier((first, first_q, visibility(block_mask)))
    far = opposite(first, "x", 1)
    first_q, prev = lax.optimization_barrier((first_q, prev))
    far_q = opposite(first_q, "y", 1)
    far, far_q, second, second_q = lax.optimization_barrier((far, far_q, second, second_q))
    mine = [kv, first, second, far]
    pieces = mine + [shifted(p, "core", 1) for p in mine]

    part = attend(seen[1], far_q, pieces)
    two = shifted(part, "y", 2)
    next_one = opposite(attend(seen[2], first_q, pieces), "y", -1)
    last_one = opposite(attend(seen[3], second_q, pieces), "y", 1)
    segments = pltpu.with_memory_space_constraint(segment_ids.reshape(-1, TILE), pltpu.HBM)
    own = attend(seen[0], q, pieces, (prev, rkv, segments))

    *sent, att = project([own, two, next_one, last_one], weight)
    for3, for2, for1 = (along_z(b, step) for b, step in zip(sent, (-1, 1, -1)))
    direct, rest3, rest2, rest1, total = project([att], weight)
    got_direct = along_z(direct, 1)
    back3 = along_z((rest3 + for3.astype(jnp.float32)).astype(jnp.bfloat16), -3)
    on2 = along_z((rest2 + for2.astype(jnp.float32)).astype(jnp.bfloat16), 2)
    back1 = along_z((rest1 + for1.astype(jnp.float32)).astype(jnp.bfloat16), -1)
    total = total + got_direct.astype(jnp.float32)
    for part in (back1, on2, back3):
        total = total + part.astype(jnp.float32)
    return total.astype(jnp.bfloat16)


def solution(mesh):
    split = Mesh(mesh.devices.reshape(XS, YS, CORES, ZS), ("x", "y", "core", "z"))
    seq = ("x", "y", "core")
    placed = (P(seq, "z"),) * 5 + (P("z", None), P(), P())
    return jax.shard_map(
        body, mesh=split, in_specs=placed, out_specs=P(seq, "z"), check_vma=False
    )
```

```python
import functools
import math

import jax
import jax.numpy as jnp
from jax import lax
from jax.experimental import pallas as pl
from jax.experimental.pallas import tpu as pltpu
from jax.sharding import Mesh, PartitionSpec as P

H = 64
KVH = 8
CW = 128
TILE = 128
HEADS = H // KVH
XS, YS, CORES, ZS = 4, 4, 2, 8
ROWS = XS * YS * CORES * TILE
SHARE = 512
SHARES = XS * CORES
BLOCK = 256
NEG_FILL = -1e30
SCALE2 = math.log2(math.e) / math.sqrt(CW)
STATS = 3
QUIET = 64.0
QROWS = HEADS * TILE
OUT_BLOCK = 640


def seq_index(x, y, c):
    return (lax.rem(x, XS) * YS + lax.rem(y, YS)) * CORES + c


def shifted(block, axis, step):
    n = lax.axis_size(axis)
    return lax.ppermute(block, axis, [((i + step) % n, i) for i in range(n)])


def own_bias(seg_ref, bias_s):
    device = seq_index(*(lax.axis_index(a) for a in ("x", "y", "core")))
    mine = seg_ref[pl.ds(device, 1), :]
    before = seg_ref[pl.ds(jnp.maximum(device - 1, 0), 1), :]
    before = jnp.where(device > 0, before, -1)
    rows = jnp.broadcast_to(mine, (TILE, TILE)).T
    r = lax.broadcasted_iota(jnp.int32, (TILE, TILE), 0)
    c = lax.broadcasted_iota(jnp.int32, (TILE, TILE), 1)
    bias_s[:, :TILE] = jnp.where(rows == before, 0.0, NEG_FILL)
    bias_s[:, TILE:] = jnp.where((rows == mine) & (c <= r), 0.0, NEG_FILL)


def prepare_kernel(pk_ref, pv_ref, rk_ref, rv_ref, q_hbm, kv_ref, rkv_ref, q_ref, sems):
    moves = (
        (pk_ref, kv_ref.at[:, :CW]),
        (pv_ref, kv_ref.at[:, CW:]),
        (rk_ref, rkv_ref.at[:, :CW]),
        (rv_ref, rkv_ref.at[:, CW:]),
    ) + tuple(
        (q_hbm.at[:, i : i + 2 * CW], q_ref.at[i // 2 : i // 2 + TILE])
        for i in range(0, HEADS * CW, 2 * CW)
    )
    copies = [pltpu.make_async_copy(a, b, sems.at[i]) for i, (a, b) in enumerate(moves)]
    for copy in copies:
        copy.start()
    for copy in copies:
        copy.wait()


def prepare(pkeys, pvalues, rkeys, rvalues, q):
    return pl.pallas_call(
        prepare_kernel,
        out_shape=[
            pltpu.VMEM((pkeys.shape[0], 2 * CW), jnp.bfloat16),
            pltpu.VMEM((TILE, 2 * CW), jnp.bfloat16),
            pltpu.VMEM((QROWS // 2, 2 * CW), q.dtype),
        ],
        in_specs=[pl.BlockSpec(memory_space=pltpu.HBM)] * 5,
        out_specs=[pl.BlockSpec(memory_space=pltpu.VMEM)] * 3,
        scratch_shapes=[pltpu.SemaphoreType.DMA((8,))],
        compiler_params=pltpu.CompilerParams(vmem_limit_bytes=8 << 20),
        cost_estimate=pl.CostEstimate(flops=1, bytes_accessed=1, transcendentals=0),
        name="prepare",
    )(
        *(
            pltpu.with_memory_space_constraint(a, pltpu.HBM)
            for a in (pkeys, pvalues, rkeys, rvalues, q)
        )
    )


def visibility_kernel(mask_hbm, *refs):
    flag_refs, (mask_ref, sem) = refs[:4], refs[4:]
    copy = pltpu.make_async_copy(mask_hbm, mask_ref, sem)
    copy.start()
    copy.wait()
    x, y, core = (lax.axis_index(a) for a in ("x", "y", "core"))
    tiles = SHARE // TILE
    step = XS + 1 - 2 * core
    back = XS - 1 + 2 * core
    other = 1 - core
    shares = (
        (0, core), (step, core), (back, core), (2, core),
        (0, other), (back, other), (step, other), (2, other),
    )
    for flags, dy in zip(flag_refs, (0, 2, 1 - 2 * core, 2 * core - 1)):
        row = seq_index(x, y + dy + YS, core)
        for p, (dx, c) in enumerate(shares):
            first = seq_index(x + dx, y, c) * tiles
            for t in range(tiles):
                flags[p * tiles + t] = mask_ref[row, first + t]


def visibility(block_mask):
    return pl.pallas_call(
        visibility_kernel,
        out_shape=[jax.ShapeDtypeStruct((SHARES * SHARE // TILE,), jnp.int32)] * 4,
        in_specs=[pl.BlockSpec(memory_space=pltpu.HBM)],
        out_specs=[pl.BlockSpec(memory_space=pltpu.SMEM)] * 4,
        scratch_shapes=[pltpu.SMEM(block_mask.shape, jnp.int32), pltpu.SemaphoreType.DMA(())],
        compiler_params=pltpu.CompilerParams(vmem_limit_bytes=4 << 20),
        cost_estimate=pl.CostEstimate(flops=1, bytes_accessed=1, transcendentals=0),
        name="visibility",
    )(pltpu.with_memory_space_constraint(block_mask, pltpu.HBM))


def split_three(value):
    parts = []
    for _ in range(STATS):
        parts.append(value.astype(jnp.bfloat16).astype(jnp.float32))
        value = value - parts[-1]
    return parts


def opposite(block, axis, step):
    n = lax.axis_size(axis)
    route = [
        (((i + (step if c == 0 else -step)) % n) * CORES + c, i * CORES + c)
        for i in range(n)
        for c in range(CORES)
    ]
    return lax.ppermute(block, (axis, "core"), route)


def attend_kernel(own, flags_ref, q_ref, *refs):
    kv_refs, refs = refs[:SHARES], refs[SHARES:]
    if own:
        (prev_ref, mine_ref, seg_hbm), refs = refs[:3], refs[3:]
    out_ref, kv_s, q_s, m_s, acc_s, list_s, again_s = refs[:7]
    last = SHARES * SHARE
    copies = []
    if own:
        bias_s, seg_ref, sems = refs[7:]
        targets = (
            kv_s.at[last : last + TILE, : 2 * CW],
            kv_s.at[last + TILE : last + BLOCK, : 2 * CW],
            seg_ref,
        )
        for i, (source, target) in enumerate(zip((prev_ref, mine_ref, seg_hbm), targets)):
            copies.append(pltpu.make_async_copy(source, target, sems.at[i]))
            copies[-1].start()
    lanes = lax.broadcasted_iota(jnp.int32, (TILE, CW), 1)

    count = 0
    block = 0
    for ref in kv_refs:
        for b in range(ref.shape[0] // BLOCK):
            seen = flags_ref[2 * block] + flags_ref[2 * block + 1] > 0
            list_s[count] = block

            @pl.when(seen)
            def _():
                rows = slice(block * BLOCK, (block + 1) * BLOCK)
                kv_s[rows, : 2 * CW] = ref[b * BLOCK : (b + 1) * BLOCK]
                kv_s[rows, 2 * CW :] = jnp.ones((BLOCK, CW), jnp.bfloat16)

            count = count + jnp.where(seen, 1, 0)
            block += 1
    if own:
        kv_s[last:, 2 * CW :] = jnp.ones((BLOCK, CW), jnp.bfloat16)
    for h in range(HEADS):
        at = h // 2 * TILE
        q_s[h * TILE : (h + 1) * TILE, :] = q_ref[at : at + TILE, h % 2 * CW : (h % 2 + 1) * CW]

    def rows_of(i):
        return pl.ds(pl.multiple_of(list_s[i] * BLOCK, BLOCK), BLOCK)

    def joined(parts, axis):
        return parts[0] if len(parts) == 1 else jnp.concatenate(parts, axis=axis)

    def scores(first, size):
        k = joined([kv_s[rows_of(first + i), :CW] for i in range(size)], 0)
        s = lax.dot_general(q_s[...], k, (((1,), (1,)), ((), ())), preferred_element_type=jnp.float32)
        halves = []
        for i in range(size):
            b = list_s[first + i]
            for t in range(2):
                bias = jnp.where(flags_ref[2 * b + t] > 0, 0.0, NEG_FILL)
                at = 2 * i + t
                halves.append(s[:, at * TILE : (at + 1) * TILE] * SCALE2 + bias)
        return halves

    def own_scores():
        s = lax.dot_general(q_s[...], kv_s[last:, :CW], (((1,), (1,)), ((), ())), preferred_element_type=jnp.float32)
        s = (s.reshape(HEADS, TILE, BLOCK) * SCALE2 + bias_s[...][None]).reshape(QROWS, BLOCK)
        return [s[:, :TILE], s[:, TILE:]]

    def top_of(halves):
        m = jnp.max(functools.reduce(jnp.maximum, halves), axis=1, keepdims=True)
        return jnp.broadcast_to(m, (QROWS, TILE))

    def weigh(halves, v):
        m = m_s[...]
        p = jnp.concatenate([jnp.exp2(s - m).astype(jnp.bfloat16) for s in halves], axis=1)
        return jnp.dot(p, v, preferred_element_type=jnp.float32)

    def absorb(first, size):
        v = joined([kv_s[rows_of(first + i), CW:] for i in range(size)], 0)
        acc_s[...] += weigh(scores(first, size), v)

    def attempt(a, _):
        @pl.when(jnp.logical_or(a == 0, again_s[0] == 1))
        def _():
            @pl.when(a == 0)
            def _():
                m_s[...] = jnp.zeros_like(m_s)

            @pl.when(a == 1)
            def _():
                m_s[...] = top_of(own_scores()) if own else jnp.full_like(m_s, NEG_FILL)

                def top(i, _):
                    m_s[...] = jnp.maximum(m_s[...], top_of(scores(i, 1)))
                    return 0

                lax.fori_loop(0, count, top, 0)

            acc_s[...] = jnp.zeros_like(acc_s)
            done = 0
            for size in (4, 2, 1):

                def group(j, _, size=size, done=done):
                    absorb(done + j * size, size)
                    return 0

                loops = (count - done) // size
                lax.fori_loop(0, loops, group, 0)
                done = done + loops * size
            if own:
                acc_s[...] += weigh(own_scores(), kv_s[last:, CW:])
            raw = acc_s[:, CW:]
            total = jnp.maximum(raw, 1e-30)
            inverse = 1.0 / total
            log_total = jnp.log2(total)
            loud = jnp.max(jnp.abs(log_total)) > QUIET
            if not own:
                loud = jnp.logical_and(loud, count > 0)
            again_s[0] = jnp.where(loud, 1, 0)
            lse = m_s[...] + log_total
            if not own:
                lse = jnp.where(raw > 0, lse, NEG_FILL)
            head = lanes // STATS
            stats = lse[:TILE]
            for h in range(HEADS):
                rows = slice(h * TILE, (h + 1) * TILE)
                out_ref[:, h * CW : (h + 1) * CW] = (acc_s[rows, :CW] * inverse[rows]).astype(out_ref.dtype)
                stats = jnp.where(head == h, lse[rows], stats)
            if not own:
                a_, b_, c_ = split_three(stats)
                which = lanes % STATS
                stats = jnp.where(which == 0, a_, jnp.where(which == 1, b_, c_))
            out_ref[:, HEADS * CW :] = stats.astype(out_ref.dtype)
        return 0

    again_s[0] = 0
    for copy in copies:
        copy.wait()
    if own:
        own_bias(seg_ref, bias_s)
    lax.fori_loop(0, 2, attempt, 0)


def attend(flags, q, pieces, own_parts=None):
    own = own_parts is not None
    args = [flags, q, *pieces]
    vmem = pl.BlockSpec(memory_space=pltpu.VMEM)
    keys = SHARES * SHARE + BLOCK * own
    return pl.pallas_call(
        functools.partial(attend_kernel, own),
        out_shape=pltpu.VMEM((TILE, HEADS * CW + CW), jnp.float32 if own else jnp.bfloat16),
        in_specs=[pl.BlockSpec(memory_space=pltpu.SMEM)]
        + [vmem] * (len(args) - 1)
        + [pl.BlockSpec(memory_space=m) for m in (pl.ANY, pl.ANY, pltpu.HBM)] * own,
        out_specs=vmem,
        scratch_shapes=[
            pltpu.VMEM((keys, 3 * CW), jnp.bfloat16),
            pltpu.VMEM((QROWS, CW), jnp.bfloat16),
            pltpu.VMEM((QROWS, TILE), jnp.float32),
            pltpu.VMEM((QROWS, 2 * CW), jnp.float32),
            pltpu.SMEM((keys // BLOCK + 1,), jnp.int32),
            pltpu.SMEM((1,), jnp.int32),
        ]
        + [
            pltpu.VMEM((TILE, BLOCK), jnp.float32),
            pltpu.VMEM((ROWS // TILE, TILE), jnp.int32),
            pltpu.SemaphoreType.DMA((3,)),
        ]
        * own,
        compiler_params=pltpu.CompilerParams(vmem_limit_bytes=10 << 20),
        cost_estimate=pl.CostEstimate(
            flops=QROWS * 1024 * CW * 4, bytes_accessed=8388608, transcendentals=0
        ),
        name="attend_own" if own else "attend_other",
    )(*args, *(own_parts or ()))


def combine(refs, att_s):
    stats = [r[:, HEADS * CW :].astype(jnp.float32) for r in refs]
    for h in range(HEADS):
        cols = slice(h * CW, (h + 1) * CW)
        i = STATS * h
        lses = [stats[0][:, i : i + 1]]
        for st in stats[1:]:
            lses.append(st[:, i : i + 1] + st[:, i + 1 : i + 2] + st[:, i + 2 : i + 3])
        top = functools.reduce(jnp.maximum, lses)
        weights = [jnp.exp2(v - top) for v in lses]
        inverse = 1.0 / sum(weights)
        mixed = sum(r[:, cols].astype(jnp.float32) * (w * inverse) for r, w in zip(refs, weights))
        att_s[:, cols] = mixed.astype(jnp.bfloat16)


def project_kernel(first, *refs):
    if first:
        own_ref, a_ref, b_ref, c_ref, w_ref, *targets, att_ref, w_s, sems = refs
        offsets = (-4, 3)
    else:
        att_ref, w_ref, *targets, w_s, sems = refs
        offsets = (-2, -3, 2, -1, 1, 0)
    z, sign = lax.axis_index("z"), 1 - 2 * lax.axis_index("core")
    copies = []
    for j, offset in enumerate(offsets):
        block = lax.rem(z + sign * offset + ZS, ZS)
        start = pl.multiple_of(block * OUT_BLOCK, CW)
        copies.append(
            pltpu.make_async_copy(w_ref.at[:, pl.ds(start, OUT_BLOCK)], w_s.at[j], sems.at[j])
        )
        copies[-1].start()
    if first:
        combine((own_ref, a_ref, b_ref, c_ref), att_ref)
    for j, target in enumerate(targets):
        copies[j].wait()
        term = jnp.dot(att_ref[...], w_s[j], preferred_element_type=jnp.float32)
        target[...] = term.astype(target.dtype)


def project(parts, weight):
    first = len(parts) > 1
    rows, width = TILE, HEADS * CW
    vmem = pl.BlockSpec(memory_space=pltpu.VMEM)
    one = jax.ShapeDtypeStruct((rows, OUT_BLOCK), jnp.bfloat16)
    if first:
        out_shape = [one] * 2 + [jax.ShapeDtypeStruct((rows, width), jnp.bfloat16)]
    else:
        out_shape = [one] + [jax.ShapeDtypeStruct(one.shape, jnp.float32)] * 5
    blocks = 2 if first else 6
    return pl.pallas_call(
        functools.partial(project_kernel, first),
        out_shape=out_shape,
        in_specs=[vmem] * len(parts) + [pl.BlockSpec(memory_space=pltpu.HBM)],
        out_specs=[vmem] * len(out_shape),
        scratch_shapes=[
            pltpu.VMEM((blocks, width, OUT_BLOCK), jnp.bfloat16),
            pltpu.SemaphoreType.DMA((blocks,)),
        ],
        compiler_params=pltpu.CompilerParams(vmem_limit_bytes=14 << 20),
        cost_estimate=pl.CostEstimate(
            flops=2 * rows * width * OUT_BLOCK * 4, bytes_accessed=6 << 20, transcendentals=0
        ),
        name="project_first" if first else "project_second",
    )(*parts, pltpu.with_memory_space_constraint(weight, pltpu.HBM))


def along_z(block, step):
    route = [
        (c * ZS + z, c * ZS + (z + (step if c == 0 else -step)) % ZS)
        for c in range(CORES)
        for z in range(ZS)
    ]
    return lax.ppermute(block, ("core", "z"), route)


def body(q, rkeys, rvalues, pkeys, pvalues, weight, segment_ids, block_mask):
    kv, rkv, q = prepare(pkeys, pvalues, rkeys, rvalues, q)
    first, first_q = opposite(kv, "x", 1), opposite(q, "y", 1)
    second, second_q = opposite(kv, "x", -1), opposite(q, "y", -1)
    prev = shifted(rkv, ("x", "y", "core"), -1)
    first, first_q, seen = lax.optimization_barrier((first, first_q, visibility(block_mask)))
    far = opposite(first, "x", 1)
    first_q, prev = lax.optimization_barrier((first_q, prev))
    far_q = opposite(first_q, "y", 1)
    far, far_q, second, second_q = lax.optimization_barrier((far, far_q, second, second_q))
    mine = [kv, first, second, far]
    pieces = mine + [shifted(p, "core", 1) for p in mine]

    part = attend(seen[1], far_q, pieces)
    two = shifted(part, "y", 2)
    next_one = opposite(attend(seen[2], first_q, pieces), "y", -1)
    last_one = opposite(attend(seen[3], second_q, pieces), "y", 1)
    segments = pltpu.with_memory_space_constraint(segment_ids.reshape(-1, TILE), pltpu.HBM)
    own = attend(seen[0], q, pieces, (prev, rkv, segments))

    four, three, att = project([own, two, next_one, last_one], weight)
    four, three = along_z(four, -1), along_z(three, 1)
    four, three = lax.optimization_barrier((four, three))
    back2, back3, on2, back1, on1, total = project([att], weight)
    back2 = along_z(back2, -1)
    back3 = along_z((back3 + four.astype(jnp.float32)).astype(jnp.bfloat16), -2)
    on2 = along_z((on2 + three.astype(jnp.float32)).astype(jnp.bfloat16), 1)
    back1 = back1 + back2.astype(jnp.float32) + back3.astype(jnp.float32)
    back1 = along_z(back1.astype(jnp.bfloat16), -1)
    on1 = along_z((on1 + on2.astype(jnp.float32)).astype(jnp.bfloat16), 1)
    total = total + back1.astype(jnp.float32) + on1.astype(jnp.float32)
    return total.astype(jnp.bfloat16)


def solution(mesh):
    split = Mesh(mesh.devices.reshape(XS, YS, CORES, ZS), ("x", "y", "core", "z"))
    seq = ("x", "y", "core")
    placed = (P(seq, "z"),) * 5 + (P("z", None), P(), P())
    return jax.shard_map(
        body, mesh=split, in_specs=placed, out_specs=P(seq, "z"), check_vma=False
    )
```

```python
import functools
import math

import jax
import jax.numpy as jnp
from jax import lax
from jax.experimental import pallas as pl
from jax.experimental.pallas import tpu as pltpu
from jax.sharding import Mesh, PartitionSpec as P

H = 64
KVH = 8
CW = 128
TILE = 128
HEADS = H // KVH
XS, YS, CORES, ZS = 4, 4, 2, 8
ROWS = XS * YS * CORES * TILE
SHARE = 512
SHARES = XS * CORES
BLOCK = 256
NEG_FILL = -1e30
SCALE2 = math.log2(math.e) / math.sqrt(CW)
STATS = 3
QUIET = 64.0
QROWS = HEADS * TILE
OUT_BLOCK = 640


def seq_index(x, y, c):
    return (lax.rem(x, XS) * YS + lax.rem(y, YS)) * CORES + c


def shifted(block, axis, step):
    n = lax.axis_size(axis)
    return lax.ppermute(block, axis, [((i + step) % n, i) for i in range(n)])


def own_bias(seg_ref, bias_s):
    device = seq_index(*(lax.axis_index(a) for a in ("x", "y", "core")))
    mine = seg_ref[pl.ds(device, 1), :]
    before = seg_ref[pl.ds(jnp.maximum(device - 1, 0), 1), :]
    before = jnp.where(device > 0, before, -1)
    rows = jnp.broadcast_to(mine, (TILE, TILE)).T
    r = lax.broadcasted_iota(jnp.int32, (TILE, TILE), 0)
    c = lax.broadcasted_iota(jnp.int32, (TILE, TILE), 1)
    bias_s[:, :TILE] = jnp.where(rows == before, 0.0, NEG_FILL)
    bias_s[:, TILE:] = jnp.where((rows == mine) & (c <= r), 0.0, NEG_FILL)


def prepare_kernel(pk_ref, pv_ref, rk_ref, rv_ref, q_hbm, kv_ref, rkv_ref, q_ref, sems):
    moves = (
        (pk_ref, kv_ref.at[:, :CW]),
        (pv_ref, kv_ref.at[:, CW:]),
        (rk_ref, rkv_ref.at[:, :CW]),
        (rv_ref, rkv_ref.at[:, CW:]),
    ) + tuple(
        (q_hbm.at[:, i : i + 2 * CW], q_ref.at[i // 2 : i // 2 + TILE])
        for i in range(0, HEADS * CW, 2 * CW)
    )
    copies = [pltpu.make_async_copy(a, b, sems.at[i]) for i, (a, b) in enumerate(moves)]
    for copy in copies:
        copy.start()
    for copy in copies:
        copy.wait()


def prepare(pkeys, pvalues, rkeys, rvalues, q):
    return pl.pallas_call(
        prepare_kernel,
        out_shape=[
            pltpu.VMEM((pkeys.shape[0], 2 * CW), jnp.bfloat16),
            pltpu.VMEM((TILE, 2 * CW), jnp.bfloat16),
            pltpu.VMEM((QROWS // 2, 2 * CW), q.dtype),
        ],
        in_specs=[pl.BlockSpec(memory_space=pltpu.HBM)] * 5,
        out_specs=[pl.BlockSpec(memory_space=pltpu.VMEM)] * 3,
        scratch_shapes=[pltpu.SemaphoreType.DMA((8,))],
        compiler_params=pltpu.CompilerParams(vmem_limit_bytes=8 << 20),
        cost_estimate=pl.CostEstimate(flops=1, bytes_accessed=1, transcendentals=0),
        name="prepare",
    )(
        *(
            pltpu.with_memory_space_constraint(a, pltpu.HBM)
            for a in (pkeys, pvalues, rkeys, rvalues, q)
        )
    )


def visibility_kernel(mask_hbm, *refs):
    flag_refs, (mask_ref, sem) = refs[:4], refs[4:]
    copy = pltpu.make_async_copy(mask_hbm, mask_ref, sem)
    copy.start()
    copy.wait()
    x, y, core = (lax.axis_index(a) for a in ("x", "y", "core"))
    tiles = SHARE // TILE
    step = XS + 1 - 2 * core
    back = XS - 1 + 2 * core
    other = 1 - core
    shares = (
        (0, core), (step, core), (back, core), (2, core),
        (0, other), (back, other), (step, other), (2, other),
    )
    for flags, dy in zip(flag_refs, (0, 2, 1 - 2 * core, 2 * core - 1)):
        row = seq_index(x, y + dy + YS, core)
        for p, (dx, c) in enumerate(shares):
            first = seq_index(x + dx, y, c) * tiles
            for t in range(tiles):
                flags[p * tiles + t] = mask_ref[row, first + t]


def visibility(block_mask):
    return pl.pallas_call(
        visibility_kernel,
        out_shape=[jax.ShapeDtypeStruct((SHARES * SHARE // TILE,), jnp.int32)] * 4,
        in_specs=[pl.BlockSpec(memory_space=pltpu.HBM)],
        out_specs=[pl.BlockSpec(memory_space=pltpu.SMEM)] * 4,
        scratch_shapes=[pltpu.SMEM(block_mask.shape, jnp.int32), pltpu.SemaphoreType.DMA(())],
        compiler_params=pltpu.CompilerParams(vmem_limit_bytes=4 << 20),
        cost_estimate=pl.CostEstimate(flops=1, bytes_accessed=1, transcendentals=0),
        name="visibility",
    )(pltpu.with_memory_space_constraint(block_mask, pltpu.HBM))


def split_three(value):
    parts = []
    for _ in range(STATS):
        parts.append(value.astype(jnp.bfloat16).astype(jnp.float32))
        value = value - parts[-1]
    return parts


def opposite(block, axis, step):
    n = lax.axis_size(axis)
    route = [
        (((i + (step if c == 0 else -step)) % n) * CORES + c, i * CORES + c)
        for i in range(n)
        for c in range(CORES)
    ]
    return lax.ppermute(block, (axis, "core"), route)


def attend_kernel(own, flags_ref, q_ref, *refs):
    kv_refs, refs = refs[:SHARES], refs[SHARES:]
    if own:
        (prev_ref, mine_ref, seg_hbm, w_hbm), refs = refs[:4], refs[4:]
        w_ref, refs = refs[1], refs[:1] + refs[2:]
    out_ref, kv_s, q_s, m_s, acc_s, list_s, again_s = refs[:7]
    last = SHARES * SHARE
    copies = []
    if own:
        bias_s, seg_ref, sems = refs[7:]
        targets = (
            kv_s.at[last : last + TILE, : 2 * CW],
            kv_s.at[last + TILE : last + BLOCK, : 2 * CW],
            seg_ref,
        )
        for i, (source, target) in enumerate(zip((prev_ref, mine_ref, seg_hbm), targets)):
            copies.append(pltpu.make_async_copy(source, target, sems.at[i]))
            copies[-1].start()
        weight_copy = pltpu.make_async_copy(w_hbm, w_ref, sems.at[3])
        weight_copy.start()
    lanes = lax.broadcasted_iota(jnp.int32, (TILE, CW), 1)

    count = 0
    block = 0
    for ref in kv_refs:
        for b in range(ref.shape[0] // BLOCK):
            seen = flags_ref[2 * block] + flags_ref[2 * block + 1] > 0
            list_s[count] = block

            @pl.when(seen)
            def _():
                rows = slice(block * BLOCK, (block + 1) * BLOCK)
                kv_s[rows, : 2 * CW] = ref[b * BLOCK : (b + 1) * BLOCK]
                kv_s[rows, 2 * CW :] = jnp.ones((BLOCK, CW), jnp.bfloat16)

            count = count + jnp.where(seen, 1, 0)
            block += 1
    if own:
        kv_s[last:, 2 * CW :] = jnp.ones((BLOCK, CW), jnp.bfloat16)
    for h in range(HEADS):
        at = h // 2 * TILE
        q_s[h * TILE : (h + 1) * TILE, :] = q_ref[at : at + TILE, h % 2 * CW : (h % 2 + 1) * CW]

    def rows_of(i):
        return pl.ds(pl.multiple_of(list_s[i] * BLOCK, BLOCK), BLOCK)

    def joined(parts, axis):
        return parts[0] if len(parts) == 1 else jnp.concatenate(parts, axis=axis)

    def scores(first, size):
        k = joined([kv_s[rows_of(first + i), :CW] for i in range(size)], 0)
        s = lax.dot_general(q_s[...], k, (((1,), (1,)), ((), ())), preferred_element_type=jnp.float32)
        halves = []
        for i in range(size):
            b = list_s[first + i]
            for t in range(2):
                bias = jnp.where(flags_ref[2 * b + t] > 0, 0.0, NEG_FILL)
                at = 2 * i + t
                halves.append(s[:, at * TILE : (at + 1) * TILE] * SCALE2 + bias)
        return halves

    def own_scores():
        s = lax.dot_general(q_s[...], kv_s[last:, :CW], (((1,), (1,)), ((), ())), preferred_element_type=jnp.float32)
        s = (s.reshape(HEADS, TILE, BLOCK) * SCALE2 + bias_s[...][None]).reshape(QROWS, BLOCK)
        return [s[:, :TILE], s[:, TILE:]]

    def top_of(halves):
        m = jnp.max(functools.reduce(jnp.maximum, halves), axis=1, keepdims=True)
        return jnp.broadcast_to(m, (QROWS, TILE))

    def weigh(halves, v):
        m = m_s[...]
        p = jnp.concatenate([jnp.exp2(s - m).astype(jnp.bfloat16) for s in halves], axis=1)
        return jnp.dot(p, v, preferred_element_type=jnp.float32)

    def absorb(first, size):
        v = joined([kv_s[rows_of(first + i), CW:] for i in range(size)], 0)
        acc_s[...] += weigh(scores(first, size), v)

    def attempt(a, _):
        @pl.when(jnp.logical_or(a == 0, again_s[0] == 1))
        def _():
            @pl.when(a == 0)
            def _():
                m_s[...] = jnp.zeros_like(m_s)

            @pl.when(a == 1)
            def _():
                m_s[...] = top_of(own_scores()) if own else jnp.full_like(m_s, NEG_FILL)

                def top(i, _):
                    m_s[...] = jnp.maximum(m_s[...], top_of(scores(i, 1)))
                    return 0

                lax.fori_loop(0, count, top, 0)

            acc_s[...] = jnp.zeros_like(acc_s)
            done = 0
            for size in (4, 2, 1):

                def group(j, _, size=size, done=done):
                    absorb(done + j * size, size)
                    return 0

                loops = (count - done) // size
                lax.fori_loop(0, loops, group, 0)
                done = done + loops * size
            if own:
                acc_s[...] += weigh(own_scores(), kv_s[last:, CW:])
            raw = acc_s[:, CW:]
            total = jnp.maximum(raw, 1e-30)
            inverse = 1.0 / total
            log_total = jnp.log2(total)
            loud = jnp.max(jnp.abs(log_total)) > QUIET
            if not own:
                loud = jnp.logical_and(loud, count > 0)
            again_s[0] = jnp.where(loud, 1, 0)
            lse = m_s[...] + log_total
            if not own:
                lse = jnp.where(raw > 0, lse, NEG_FILL)
            head = lanes // STATS
            stats = lse[:TILE]
            for h in range(HEADS):
                rows = slice(h * TILE, (h + 1) * TILE)
                out_ref[:, h * CW : (h + 1) * CW] = (acc_s[rows, :CW] * inverse[rows]).astype(out_ref.dtype)
                stats = jnp.where(head == h, lse[rows], stats)
            if not own:
                a_, b_, c_ = split_three(stats)
                which = lanes % STATS
                stats = jnp.where(which == 0, a_, jnp.where(which == 1, b_, c_))
            out_ref[:, HEADS * CW :] = stats.astype(out_ref.dtype)
        return 0

    again_s[0] = 0
    for copy in copies:
        copy.wait()
    if own:
        own_bias(seg_ref, bias_s)
    lax.fori_loop(0, 2, attempt, 0)
    if own:
        weight_copy.wait()


def attend(flags, q, pieces, own_parts=None):
    own = own_parts is not None
    args = [flags, q, *pieces]
    vmem = pl.BlockSpec(memory_space=pltpu.VMEM)
    out_shape = [pltpu.VMEM((TILE, HEADS * CW + CW), jnp.float32 if own else jnp.bfloat16)]
    if own:
        out_shape.append(pltpu.VMEM(own_parts[-1].shape, own_parts[-1].dtype))
    keys = SHARES * SHARE + BLOCK * own
    return pl.pallas_call(
        functools.partial(attend_kernel, own),
        out_shape=out_shape,
        in_specs=[pl.BlockSpec(memory_space=pltpu.SMEM)]
        + [vmem] * (len(args) - 1)
        + [pl.BlockSpec(memory_space=m) for m in (pl.ANY, pl.ANY, pltpu.HBM, pltpu.HBM)] * own,
        out_specs=[vmem] * len(out_shape),
        scratch_shapes=[
            pltpu.VMEM((keys, 3 * CW), jnp.bfloat16),
            pltpu.VMEM((QROWS, CW), jnp.bfloat16),
            pltpu.VMEM((QROWS, TILE), jnp.float32),
            pltpu.VMEM((QROWS, 2 * CW), jnp.float32),
            pltpu.SMEM((keys // BLOCK + 1,), jnp.int32),
            pltpu.SMEM((1,), jnp.int32),
        ]
        + [
            pltpu.VMEM((TILE, BLOCK), jnp.float32),
            pltpu.VMEM((ROWS // TILE, TILE), jnp.int32),
            pltpu.SemaphoreType.DMA((4,)),
        ]
        * own,
        compiler_params=pltpu.CompilerParams(vmem_limit_bytes=10 << 20),
        cost_estimate=pl.CostEstimate(
            flops=QROWS * 1024 * CW * 4, bytes_accessed=8388608, transcendentals=0
        ),
        name="attend_own" if own else "attend_other",
    )(*args, *(own_parts or ()))


def combine(refs, att_s):
    stats = [r[:, HEADS * CW :].astype(jnp.float32) for r in refs]
    for h in range(HEADS):
        cols = slice(h * CW, (h + 1) * CW)
        i = STATS * h
        lses = [stats[0][:, i : i + 1]]
        for st in stats[1:]:
            lses.append(st[:, i : i + 1] + st[:, i + 1 : i + 2] + st[:, i + 2 : i + 3])
        top = functools.reduce(jnp.maximum, lses)
        weights = [jnp.exp2(v - top) for v in lses]
        inverse = 1.0 / sum(weights)
        mixed = sum(r[:, cols].astype(jnp.float32) * (w * inverse) for r, w in zip(refs, weights))
        att_s[:, cols] = mixed.astype(jnp.bfloat16)


def project_kernel(first, *refs):
    if first:
        own_ref, a_ref, b_ref, c_ref, w_ref, *targets, att_ref = refs
        offsets = (-4, 3)
        combine((own_ref, a_ref, b_ref, c_ref), att_ref)
    else:
        att_ref, w_ref, *targets = refs
        offsets = (-2, -3, 2, -1, 1, 0)
    z, sign = lax.axis_index("z"), 1 - 2 * lax.axis_index("core")
    for offset, target in zip(offsets, targets):
        block = lax.rem(z + sign * offset + ZS, ZS)
        start = pl.multiple_of(block * OUT_BLOCK, CW)
        weight = w_ref[:, pl.ds(start, OUT_BLOCK)]
        term = jnp.dot(att_ref[...], weight, preferred_element_type=jnp.float32)
        target[...] = term.astype(target.dtype)


def project(parts, weight):
    first = len(parts) > 1
    rows, width = TILE, HEADS * CW
    vmem = pl.BlockSpec(memory_space=pltpu.VMEM)
    one = jax.ShapeDtypeStruct((rows, OUT_BLOCK), jnp.bfloat16)
    if first:
        out_shape = [one] * 2 + [jax.ShapeDtypeStruct((rows, width), jnp.bfloat16)]
    else:
        out_shape = [one] + [jax.ShapeDtypeStruct(one.shape, jnp.float32)] * 5
    return pl.pallas_call(
        functools.partial(project_kernel, first),
        out_shape=out_shape,
        in_specs=[vmem] * (len(parts) + 1),
        out_specs=[vmem] * len(out_shape),
        compiler_params=pltpu.CompilerParams(vmem_limit_bytes=8 << 20),
        cost_estimate=pl.CostEstimate(
            flops=2 * rows * width * OUT_BLOCK * 4, bytes_accessed=6 << 20, transcendentals=0
        ),
        name="project_first" if first else "project_second",
    )(*parts, weight)


def along_z(block, step):
    route = [
        (c * ZS + z, c * ZS + (z + (step if c == 0 else -step)) % ZS)
        for c in range(CORES)
        for z in range(ZS)
    ]
    return lax.ppermute(block, ("core", "z"), route)


def body(q, rkeys, rvalues, pkeys, pvalues, weight, segment_ids, block_mask):
    kv, rkv, q = prepare(pkeys, pvalues, rkeys, rvalues, q)
    first, first_q = opposite(kv, "x", 1), opposite(q, "y", 1)
    second, second_q = opposite(kv, "x", -1), opposite(q, "y", -1)
    prev = shifted(rkv, ("x", "y", "core"), -1)
    first, first_q, seen = lax.optimization_barrier((first, first_q, visibility(block_mask)))
    far = opposite(first, "x", 1)
    first_q, prev = lax.optimization_barrier((first_q, prev))
    far_q = opposite(first_q, "y", 1)
    far, far_q, second, second_q = lax.optimization_barrier((far, far_q, second, second_q))
    mine = [kv, first, second, far]
    pieces = mine + [shifted(p, "core", 1) for p in mine]

    two = shifted(attend(seen[1], far_q, pieces)[0], "y", 2)
    next_one = opposite(attend(seen[2], first_q, pieces)[0], "y", -1)
    last_one = opposite(attend(seen[3], second_q, pieces)[0], "y", 1)
    segments = pltpu.with_memory_space_constraint(segment_ids.reshape(-1, TILE), pltpu.HBM)
    weight = pltpu.with_memory_space_constraint(weight, pltpu.HBM)
    own, weight = attend(seen[0], q, pieces, (prev, rkv, segments, weight))

    four, three, att = project([own, two, next_one, last_one], weight)
    four, three = along_z(four, -1), along_z(three, 1)
    four, three = lax.optimization_barrier((four, three))
    back2, back3, on2, back1, on1, total = project([att], weight)
    back3 = (back3 + four.astype(jnp.float32)).astype(jnp.bfloat16)
    on2 = (on2 + three.astype(jnp.float32)).astype(jnp.bfloat16)
    back3, on2, back2 = lax.optimization_barrier((back3, on2, back2))
    back3, on2, back2 = along_z(back3, -2), along_z(on2, 1), along_z(back2, -1)
    back1 = back1 + back2.astype(jnp.float32) + back3.astype(jnp.float32)
    back1 = along_z(back1.astype(jnp.bfloat16), -1)
    on1 = along_z((on1 + on2.astype(jnp.float32)).astype(jnp.bfloat16), 1)
    total = total + back1.astype(jnp.float32) + on1.astype(jnp.float32)
    return total.astype(jnp.bfloat16)


def solution(mesh):
    split = Mesh(mesh.devices.reshape(XS, YS, CORES, ZS), ("x", "y", "core", "z"))
    seq = ("x", "y", "core")
    placed = (P(seq, "z"),) * 5 + (P("z", None), P(), P())
    return jax.shard_map(
        body, mesh=split, in_specs=placed, out_specs=P(seq, "z"), check_vma=False
    )
```

```python
import functools
import math

import jax
import jax.numpy as jnp
from jax import lax
from jax.experimental import pallas as pl
from jax.experimental.pallas import tpu as pltpu
from jax.sharding import Mesh, PartitionSpec as P

H = 64
KVH = 8
CW = 128
TILE = 128
HEADS = H // KVH
XS, YS, CORES, ZS = 4, 4, 2, 8
ROWS = XS * YS * CORES * TILE
SHARE = 512
SHARES = XS * CORES
BLOCK = 256
NEG_FILL = -1e30
SCALE2 = math.log2(math.e) / math.sqrt(CW)
STATS = 3
QUIET = 64.0
QROWS = HEADS * TILE
OUT_BLOCK = 640


def seq_index(x, y, c):
    return (lax.rem(x, XS) * YS + lax.rem(y, YS)) * CORES + c


def shifted(block, axis, step):
    n = lax.axis_size(axis)
    return lax.ppermute(block, axis, [((i + step) % n, i) for i in range(n)])


def own_bias(seg_ref, bias_s):
    device = seq_index(*(lax.axis_index(a) for a in ("x", "y", "core")))
    mine = seg_ref[pl.ds(device, 1), :]
    before = seg_ref[pl.ds(jnp.maximum(device - 1, 0), 1), :]
    before = jnp.where(device > 0, before, -1)
    rows = jnp.broadcast_to(mine, (TILE, TILE)).T
    r = lax.broadcasted_iota(jnp.int32, (TILE, TILE), 0)
    c = lax.broadcasted_iota(jnp.int32, (TILE, TILE), 1)
    bias_s[:, :TILE] = jnp.where(rows == before, 0.0, NEG_FILL)
    bias_s[:, TILE:] = jnp.where((rows == mine) & (c <= r), 0.0, NEG_FILL)


def prepare_kernel(pk_ref, pv_ref, rk_ref, rv_ref, q_hbm, kv_ref, rkv_ref, q_ref, sems):
    moves = (
        (pk_ref, kv_ref.at[:, :CW]),
        (pv_ref, kv_ref.at[:, CW:]),
        (rk_ref, rkv_ref.at[:, :CW]),
        (rv_ref, rkv_ref.at[:, CW:]),
    ) + tuple(
        (q_hbm.at[:, i : i + 2 * CW], q_ref.at[i // 2 : i // 2 + TILE])
        for i in range(0, HEADS * CW, 2 * CW)
    )
    copies = [pltpu.make_async_copy(a, b, sems.at[i]) for i, (a, b) in enumerate(moves)]
    for copy in copies:
        copy.start()
    for copy in copies:
        copy.wait()


def prepare(pkeys, pvalues, rkeys, rvalues, q):
    return pl.pallas_call(
        prepare_kernel,
        out_shape=[
            pltpu.VMEM((pkeys.shape[0], 2 * CW), jnp.bfloat16),
            pltpu.VMEM((TILE, 2 * CW), jnp.bfloat16),
            pltpu.VMEM((QROWS // 2, 2 * CW), q.dtype),
        ],
        in_specs=[pl.BlockSpec(memory_space=pltpu.HBM)] * 5,
        out_specs=[pl.BlockSpec(memory_space=pltpu.VMEM)] * 3,
        scratch_shapes=[pltpu.SemaphoreType.DMA((8,))],
        compiler_params=pltpu.CompilerParams(vmem_limit_bytes=8 << 20),
        cost_estimate=pl.CostEstimate(flops=1, bytes_accessed=1, transcendentals=0),
        name="prepare",
    )(
        *(
            pltpu.with_memory_space_constraint(a, pltpu.HBM)
            for a in (pkeys, pvalues, rkeys, rvalues, q)
        )
    )


def visibility_kernel(mask_hbm, *refs):
    flag_refs, (mask_ref, sem) = refs[:4], refs[4:]
    copy = pltpu.make_async_copy(mask_hbm, mask_ref, sem)
    copy.start()
    copy.wait()
    x, y, core = (lax.axis_index(a) for a in ("x", "y", "core"))
    tiles = SHARE // TILE
    step = XS + 1 - 2 * core
    back = XS - 1 + 2 * core
    other = 1 - core
    shares = (
        (0, core), (step, core), (back, core), (2, core),
        (0, other), (back, other), (step, other), (2, other),
    )
    for flags, dy in zip(flag_refs, (0, 2, 1 - 2 * core, 2 * core - 1)):
        row = seq_index(x, y + dy + YS, core)
        for p, (dx, c) in enumerate(shares):
            first = seq_index(x + dx, y, c) * tiles
            for t in range(tiles):
                flags[p * tiles + t] = mask_ref[row, first + t]


def visibility(block_mask):
    return pl.pallas_call(
        visibility_kernel,
        out_shape=[jax.ShapeDtypeStruct((SHARES * SHARE // TILE,), jnp.int32)] * 4,
        in_specs=[pl.BlockSpec(memory_space=pltpu.HBM)],
        out_specs=[pl.BlockSpec(memory_space=pltpu.SMEM)] * 4,
        scratch_shapes=[pltpu.SMEM(block_mask.shape, jnp.int32), pltpu.SemaphoreType.DMA(())],
        compiler_params=pltpu.CompilerParams(vmem_limit_bytes=4 << 20),
        cost_estimate=pl.CostEstimate(flops=1, bytes_accessed=1, transcendentals=0),
        name="visibility",
    )(pltpu.with_memory_space_constraint(block_mask, pltpu.HBM))


def split_three(value):
    parts = []
    for _ in range(STATS):
        parts.append(value.astype(jnp.bfloat16).astype(jnp.float32))
        value = value - parts[-1]
    return parts


def opposite(block, axis, step):
    n = lax.axis_size(axis)
    route = [
        (((i + (step if c == 0 else -step)) % n) * CORES + c, i * CORES + c)
        for i in range(n)
        for c in range(CORES)
    ]
    return lax.ppermute(block, (axis, "core"), route)


def attend_kernel(own, flags_ref, q_ref, *refs):
    kv_refs, refs = refs[:SHARES], refs[SHARES:]
    if own:
        (prev_ref, mine_ref, seg_hbm, w_hbm), refs = refs[:4], refs[4:]
        w_ref, refs = refs[1], refs[:1] + refs[2:]
    out_ref, kv_s, q_s, m_s, acc_s, list_s, again_s = refs[:7]
    last = SHARES * SHARE
    copies = []
    if own:
        bias_s, seg_ref, sems = refs[7:]
        targets = (
            kv_s.at[last : last + TILE, : 2 * CW],
            kv_s.at[last + TILE : last + BLOCK, : 2 * CW],
            seg_ref,
        )
        for i, (source, target) in enumerate(zip((prev_ref, mine_ref, seg_hbm), targets)):
            copies.append(pltpu.make_async_copy(source, target, sems.at[i]))
            copies[-1].start()
        weight_copy = pltpu.make_async_copy(w_hbm, w_ref, sems.at[3])
        weight_copy.start()
    lanes = lax.broadcasted_iota(jnp.int32, (TILE, CW), 1)

    count = 0
    block = 0
    for ref in kv_refs:
        for b in range(ref.shape[0] // BLOCK):
            seen = flags_ref[2 * block] + flags_ref[2 * block + 1] > 0
            list_s[count] = block

            @pl.when(seen)
            def _():
                rows = slice(block * BLOCK, (block + 1) * BLOCK)
                kv_s[rows, : 2 * CW] = ref[b * BLOCK : (b + 1) * BLOCK]
                kv_s[rows, 2 * CW :] = jnp.ones((BLOCK, CW), jnp.bfloat16)

            count = count + jnp.where(seen, 1, 0)
            block += 1
    if own:
        kv_s[last:, 2 * CW :] = jnp.ones((BLOCK, CW), jnp.bfloat16)
    for h in range(HEADS):
        at = h // 2 * TILE
        q_s[h * TILE : (h + 1) * TILE, :] = q_ref[at : at + TILE, h % 2 * CW : (h % 2 + 1) * CW]

    def rows_of(i):
        return pl.ds(pl.multiple_of(list_s[i] * BLOCK, BLOCK), BLOCK)

    def joined(parts, axis):
        return parts[0] if len(parts) == 1 else jnp.concatenate(parts, axis=axis)

    def scores(first, size):
        k = joined([kv_s[rows_of(first + i), :CW] for i in range(size)], 0)
        s = lax.dot_general(q_s[...], k, (((1,), (1,)), ((), ())), preferred_element_type=jnp.float32)
        halves = []
        for i in range(size):
            b = list_s[first + i]
            for t in range(2):
                bias = jnp.where(flags_ref[2 * b + t] > 0, 0.0, NEG_FILL)
                at = 2 * i + t
                halves.append(s[:, at * TILE : (at + 1) * TILE] * SCALE2 + bias)
        return halves

    def own_scores():
        s = lax.dot_general(q_s[...], kv_s[last:, :CW], (((1,), (1,)), ((), ())), preferred_element_type=jnp.float32)
        s = (s.reshape(HEADS, TILE, BLOCK) * SCALE2 + bias_s[...][None]).reshape(QROWS, BLOCK)
        return [s[:, :TILE], s[:, TILE:]]

    def top_of(halves):
        m = jnp.max(functools.reduce(jnp.maximum, halves), axis=1, keepdims=True)
        return jnp.broadcast_to(m, (QROWS, TILE))

    def weigh(halves, v):
        m = m_s[...]
        p = jnp.concatenate([jnp.exp2(s - m).astype(jnp.bfloat16) for s in halves], axis=1)
        return jnp.dot(p, v, preferred_element_type=jnp.float32)

    def absorb(first, size):
        v = joined([kv_s[rows_of(first + i), CW:] for i in range(size)], 0)
        acc_s[...] += weigh(scores(first, size), v)

    def attempt(a, _):
        @pl.when(jnp.logical_or(a == 0, again_s[0] == 1))
        def _():
            @pl.when(a == 0)
            def _():
                m_s[...] = jnp.zeros_like(m_s)

            @pl.when(a == 1)
            def _():
                m_s[...] = top_of(own_scores()) if own else jnp.full_like(m_s, NEG_FILL)

                def top(i, _):
                    m_s[...] = jnp.maximum(m_s[...], top_of(scores(i, 1)))
                    return 0

                lax.fori_loop(0, count, top, 0)

            acc_s[...] = jnp.zeros_like(acc_s)
            done = 0
            for size in (4, 2, 1):

                def group(j, _, size=size, done=done):
                    absorb(done + j * size, size)
                    return 0

                loops = (count - done) // size
                lax.fori_loop(0, loops, group, 0)
                done = done + loops * size
            if own:
                acc_s[...] += weigh(own_scores(), kv_s[last:, CW:])
            raw = acc_s[:, CW:]
            total = jnp.maximum(raw, 1e-30)
            inverse = 1.0 / total
            log_total = jnp.log2(total)
            loud = jnp.max(jnp.abs(log_total)) > QUIET
            if not own:
                loud = jnp.logical_and(loud, count > 0)
            again_s[0] = jnp.where(loud, 1, 0)
            lse = m_s[...] + log_total
            if not own:
                lse = jnp.where(raw > 0, lse, NEG_FILL)
            head = lanes // STATS
            stats = lse[:TILE]
            for h in range(HEADS):
                rows = slice(h * TILE, (h + 1) * TILE)
                out_ref[:, h * CW : (h + 1) * CW] = (acc_s[rows, :CW] * inverse[rows]).astype(out_ref.dtype)
                stats = jnp.where(head == h, lse[rows], stats)
            if not own:
                a_, b_, c_ = split_three(stats)
                which = lanes % STATS
                stats = jnp.where(which == 0, a_, jnp.where(which == 1, b_, c_))
            out_ref[:, HEADS * CW :] = stats.astype(out_ref.dtype)
        return 0

    again_s[0] = 0
    for copy in copies:
        copy.wait()
    if own:
        own_bias(seg_ref, bias_s)
    lax.fori_loop(0, 2, attempt, 0)
    if own:
        weight_copy.wait()


def attend(flags, q, pieces, own_parts=None):
    own = own_parts is not None
    args = [flags, q, *pieces]
    vmem = pl.BlockSpec(memory_space=pltpu.VMEM)
    out_shape = [pltpu.VMEM((TILE, HEADS * CW + CW), jnp.float32 if own else jnp.bfloat16)]
    if own:
        out_shape.append(pltpu.VMEM(own_parts[-1].shape, own_parts[-1].dtype))
    keys = SHARES * SHARE + BLOCK * own
    return pl.pallas_call(
        functools.partial(attend_kernel, own),
        out_shape=out_shape,
        in_specs=[pl.BlockSpec(memory_space=pltpu.SMEM)]
        + [vmem] * (len(args) - 1)
        + [pl.BlockSpec(memory_space=m) for m in (pl.ANY, pl.ANY, pltpu.HBM, pltpu.HBM)] * own,
        out_specs=[vmem] * len(out_shape),
        scratch_shapes=[
            pltpu.VMEM((keys, 3 * CW), jnp.bfloat16),
            pltpu.VMEM((QROWS, CW), jnp.bfloat16),
            pltpu.VMEM((QROWS, TILE), jnp.float32),
            pltpu.VMEM((QROWS, 2 * CW), jnp.float32),
            pltpu.SMEM((keys // BLOCK + 1,), jnp.int32),
            pltpu.SMEM((1,), jnp.int32),
        ]
        + [
            pltpu.VMEM((TILE, BLOCK), jnp.float32),
            pltpu.VMEM((ROWS // TILE, TILE), jnp.int32),
            pltpu.SemaphoreType.DMA((4,)),
        ]
        * own,
        compiler_params=pltpu.CompilerParams(vmem_limit_bytes=10 << 20),
        cost_estimate=pl.CostEstimate(
            flops=QROWS * 1024 * CW * 4, bytes_accessed=8388608, transcendentals=0
        ),
        name="attend_own" if own else "attend_other",
    )(*args, *(own_parts or ()))


def combine(refs, att_s):
    stats = [r[:, HEADS * CW :].astype(jnp.float32) for r in refs]
    for h in range(HEADS):
        cols = slice(h * CW, (h + 1) * CW)
        i = STATS * h
        lses = [stats[0][:, i : i + 1]]
        for st in stats[1:]:
            lses.append(st[:, i : i + 1] + st[:, i + 1 : i + 2] + st[:, i + 2 : i + 3])
        top = functools.reduce(jnp.maximum, lses)
        weights = [jnp.exp2(v - top) for v in lses]
        inverse = 1.0 / sum(weights)
        mixed = sum(r[:, cols].astype(jnp.float32) * (w * inverse) for r, w in zip(refs, weights))
        att_s[:, cols] = mixed.astype(jnp.bfloat16)


def project_kernel(first, *refs):
    if first:
        own_ref, a_ref, b_ref, c_ref, w_ref, *targets, att_ref = refs
        offsets = (-4, 3, -2)
        combine((own_ref, a_ref, b_ref, c_ref), att_ref)
    else:
        att_ref, w_ref, *targets = refs
        offsets = (1, -3, 2, -1, 0)
    z, sign = lax.axis_index("z"), 1 - 2 * lax.axis_index("core")
    for offset, target in zip(offsets, targets):
        block = lax.rem(z + sign * offset + ZS, ZS)
        start = pl.multiple_of(block * OUT_BLOCK, CW)
        weight = w_ref[:, pl.ds(start, OUT_BLOCK)]
        term = jnp.dot(att_ref[...], weight, preferred_element_type=jnp.float32)
        target[...] = term.astype(target.dtype)


def project(parts, weight):
    first = len(parts) > 1
    rows, width = TILE, HEADS * CW
    vmem = pl.BlockSpec(memory_space=pltpu.VMEM)
    one = jax.ShapeDtypeStruct((rows, OUT_BLOCK), jnp.bfloat16)
    if first:
        out_shape = [one] * 3 + [jax.ShapeDtypeStruct((rows, width), jnp.bfloat16)]
    else:
        out_shape = [one] + [jax.ShapeDtypeStruct(one.shape, jnp.float32)] * 4
    return pl.pallas_call(
        functools.partial(project_kernel, first),
        out_shape=out_shape,
        in_specs=[vmem] * (len(parts) + 1),
        out_specs=[vmem] * len(out_shape),
        compiler_params=pltpu.CompilerParams(vmem_limit_bytes=8 << 20),
        cost_estimate=pl.CostEstimate(
            flops=2 * rows * width * OUT_BLOCK * 4, bytes_accessed=6 << 20, transcendentals=0
        ),
        name="project_first" if first else "project_second",
    )(*parts, weight)


def along_z(block, step):
    route = [
        (c * ZS + z, c * ZS + (z + (step if c == 0 else -step)) % ZS)
        for c in range(CORES)
        for z in range(ZS)
    ]
    return lax.ppermute(block, ("core", "z"), route)


def body(q, rkeys, rvalues, pkeys, pvalues, weight, segment_ids, block_mask):
    kv, rkv, q = prepare(pkeys, pvalues, rkeys, rvalues, q)
    first, first_q = opposite(kv, "x", 1), opposite(q, "y", 1)
    second, second_q = opposite(kv, "x", -1), opposite(q, "y", -1)
    prev = shifted(rkv, ("x", "y", "core"), -1)
    first, first_q, seen = lax.optimization_barrier((first, first_q, visibility(block_mask)))
    far = opposite(first, "x", 1)
    first_q, prev = lax.optimization_barrier((first_q, prev))
    far_q = opposite(first_q, "y", 1)
    far, far_q, second, second_q = lax.optimization_barrier((far, far_q, second, second_q))
    mine = [kv, first, second, far]
    pieces = mine + [shifted(p, "core", 1) for p in mine]

    two = shifted(attend(seen[1], far_q, pieces)[0], "y", 2)
    next_one = opposite(attend(seen[2], first_q, pieces)[0], "y", -1)
    last_one = opposite(attend(seen[3], second_q, pieces)[0], "y", 1)
    segments = pltpu.with_memory_space_constraint(segment_ids.reshape(-1, TILE), pltpu.HBM)
    weight = pltpu.with_memory_space_constraint(weight, pltpu.HBM)
    own, weight = attend(seen[0], q, pieces, (prev, rkv, segments, weight))

    *sent, att = project([own, two, next_one, last_one], weight)
    for3, for2, for1 = (along_z(b, step) for b, step in zip(sent, (-1, 1, -1)))
    direct, rest3, rest2, rest1, total = project([att], weight)
    back3 = (rest3 + for3.astype(jnp.float32)).astype(jnp.bfloat16)
    back3, direct = lax.optimization_barrier((back3, direct))
    back3, got_direct = along_z(back3, -3), along_z(direct, 1)
    on2 = along_z((rest2 + for2.astype(jnp.float32)).astype(jnp.bfloat16), 2)
    back1 = along_z((rest1 + for1.astype(jnp.float32)).astype(jnp.bfloat16), -1)
    total = total + got_direct.astype(jnp.float32)
    for part in (back1, on2, back3):
        total = total + part.astype(jnp.float32)
    return total.astype(jnp.bfloat16)


def solution(mesh):
    split = Mesh(mesh.devices.reshape(XS, YS, CORES, ZS), ("x", "y", "core", "z"))
    seq = ("x", "y", "core")
    placed = (P(seq, "z"),) * 5 + (P("z", None), P(), P())
    return jax.shard_map(
        body, mesh=split, in_specs=placed, out_specs=P(seq, "z"), check_vma=False
    )
```

```python
import functools
import math

import jax
import jax.numpy as jnp
from jax import lax
from jax.experimental import pallas as pl
from jax.experimental.pallas import tpu as pltpu
from jax.sharding import Mesh, PartitionSpec as P

H = 64
KVH = 8
CW = 128
TILE = 128
HEADS = H // KVH
XS, YS, CORES, ZS = 4, 4, 2, 8
ROWS = XS * YS * CORES * TILE
SHARE = 512
SHARES = XS * CORES
BLOCK = 256
NEG_FILL = -1e30
SCALE2 = math.log2(math.e) / math.sqrt(CW)
STATS = 3
QUIET = 64.0
QROWS = HEADS * TILE
OUT_BLOCK = 640


def seq_index(x, y, c):
    return (lax.rem(x, XS) * YS + lax.rem(y, YS)) * CORES + c


def shifted(block, axis, step):
    n = lax.axis_size(axis)
    return lax.ppermute(block, axis, [((i + step) % n, i) for i in range(n)])


def own_bias(seg_ref, bias_s):
    device = seq_index(*(lax.axis_index(a) for a in ("x", "y", "core")))
    mine = seg_ref[pl.ds(device, 1), :]
    before = seg_ref[pl.ds(jnp.maximum(device - 1, 0), 1), :]
    before = jnp.where(device > 0, before, -1)
    rows = jnp.broadcast_to(mine, (TILE, TILE)).T
    r = lax.broadcasted_iota(jnp.int32, (TILE, TILE), 0)
    c = lax.broadcasted_iota(jnp.int32, (TILE, TILE), 1)
    bias_s[:, :TILE] = jnp.where(rows == before, 0.0, NEG_FILL)
    bias_s[:, TILE:] = jnp.where((rows == mine) & (c <= r), 0.0, NEG_FILL)


def prepare_kernel(pk_ref, pv_ref, rk_ref, rv_ref, q_hbm, kv_ref, rkv_ref, q_ref, sems):
    moves = (
        (pk_ref, kv_ref.at[:, :CW]),
        (pv_ref, kv_ref.at[:, CW:]),
        (rk_ref, rkv_ref.at[:, :CW]),
        (rv_ref, rkv_ref.at[:, CW:]),
    ) + tuple(
        (q_hbm.at[:, i : i + 2 * CW], q_ref.at[i // 2 : i // 2 + TILE])
        for i in range(0, HEADS * CW, 2 * CW)
    )
    copies = [pltpu.make_async_copy(a, b, sems.at[i]) for i, (a, b) in enumerate(moves)]
    for copy in copies:
        copy.start()
    for copy in copies:
        copy.wait()


def prepare(pkeys, pvalues, rkeys, rvalues, q):
    return pl.pallas_call(
        prepare_kernel,
        out_shape=[
            pltpu.VMEM((pkeys.shape[0], 2 * CW), jnp.bfloat16),
            pltpu.VMEM((TILE, 2 * CW), jnp.bfloat16),
            pltpu.VMEM((QROWS // 2, 2 * CW), q.dtype),
        ],
        in_specs=[pl.BlockSpec(memory_space=pltpu.HBM)] * 5,
        out_specs=[pl.BlockSpec(memory_space=pltpu.VMEM)] * 3,
        scratch_shapes=[pltpu.SemaphoreType.DMA((8,))],
        compiler_params=pltpu.CompilerParams(vmem_limit_bytes=8 << 20),
        cost_estimate=pl.CostEstimate(flops=1, bytes_accessed=1, transcendentals=0),
        name="prepare",
    )(
        *(
            pltpu.with_memory_space_constraint(a, pltpu.HBM)
            for a in (pkeys, pvalues, rkeys, rvalues, q)
        )
    )


def visibility_kernel(mask_hbm, *refs):
    flag_refs, (mask_ref, sem) = refs[:4], refs[4:]
    copy = pltpu.make_async_copy(mask_hbm, mask_ref, sem)
    copy.start()
    copy.wait()
    x, y, core = (lax.axis_index(a) for a in ("x", "y", "core"))
    tiles = SHARE // TILE
    step = XS + 1 - 2 * core
    back = XS - 1 + 2 * core
    other = 1 - core
    shares = (
        (0, core), (step, core), (back, core), (2, core),
        (0, other), (back, other), (step, other), (2, other),
    )
    for flags, dy in zip(flag_refs, (0, 2, 1 - 2 * core, 2 * core - 1)):
        row = seq_index(x, y + dy + YS, core)
        for p, (dx, c) in enumerate(shares):
            first = seq_index(x + dx, y, c) * tiles
            for t in range(tiles):
                flags[p * tiles + t] = mask_ref[row, first + t]


def visibility(block_mask):
    return pl.pallas_call(
        visibility_kernel,
        out_shape=[jax.ShapeDtypeStruct((SHARES * SHARE // TILE,), jnp.int32)] * 4,
        in_specs=[pl.BlockSpec(memory_space=pltpu.HBM)],
        out_specs=[pl.BlockSpec(memory_space=pltpu.SMEM)] * 4,
        scratch_shapes=[pltpu.SMEM(block_mask.shape, jnp.int32), pltpu.SemaphoreType.DMA(())],
        compiler_params=pltpu.CompilerParams(vmem_limit_bytes=4 << 20),
        cost_estimate=pl.CostEstimate(flops=1, bytes_accessed=1, transcendentals=0),
        name="visibility",
    )(pltpu.with_memory_space_constraint(block_mask, pltpu.HBM))


def split_three(value):
    parts = []
    for _ in range(STATS):
        parts.append(value.astype(jnp.bfloat16).astype(jnp.float32))
        value = value - parts[-1]
    return parts


def opposite(block, axis, step):
    n = lax.axis_size(axis)
    route = [
        (((i + (step if c == 0 else -step)) % n) * CORES + c, i * CORES + c)
        for i in range(n)
        for c in range(CORES)
    ]
    return lax.ppermute(block, (axis, "core"), route)


def attend_kernel(own, flags_ref, q_ref, *refs):
    kv_refs, refs = refs[:SHARES], refs[SHARES:]
    if own:
        (prev_ref, mine_ref, seg_hbm, w_hbm), refs = refs[:4], refs[4:]
        w_ref, refs = refs[1], refs[:1] + refs[2:]
    out_ref, kv_s, q_s, m_s, acc_s, list_s, again_s = refs[:7]
    last = SHARES * SHARE
    copies = []
    if own:
        bias_s, seg_ref, sems = refs[7:]
        targets = (
            kv_s.at[last : last + TILE, : 2 * CW],
            kv_s.at[last + TILE : last + BLOCK, : 2 * CW],
            seg_ref,
        )
        for i, (source, target) in enumerate(zip((prev_ref, mine_ref, seg_hbm), targets)):
            copies.append(pltpu.make_async_copy(source, target, sems.at[i]))
            copies[-1].start()
        weight_copy = pltpu.make_async_copy(w_hbm, w_ref, sems.at[3])
        weight_copy.start()
    lanes = lax.broadcasted_iota(jnp.int32, (TILE, CW), 1)

    count = 0
    block = 0
    for ref in kv_refs:
        for b in range(ref.shape[0] // BLOCK):
            seen = flags_ref[2 * block] + flags_ref[2 * block + 1] > 0
            list_s[count] = block

            @pl.when(seen)
            def _():
                rows = slice(block * BLOCK, (block + 1) * BLOCK)
                kv_s[rows, : 2 * CW] = ref[b * BLOCK : (b + 1) * BLOCK]
                kv_s[rows, 2 * CW :] = jnp.ones((BLOCK, CW), jnp.bfloat16)

            count = count + jnp.where(seen, 1, 0)
            block += 1
    if own:
        kv_s[last:, 2 * CW :] = jnp.ones((BLOCK, CW), jnp.bfloat16)
    for h in range(HEADS):
        at = h // 2 * TILE
        q_s[h * TILE : (h + 1) * TILE, :] = q_ref[at : at + TILE, h % 2 * CW : (h % 2 + 1) * CW]

    def rows_of(i):
        return pl.ds(pl.multiple_of(list_s[i] * BLOCK, BLOCK), BLOCK)

    def joined(parts, axis):
        return parts[0] if len(parts) == 1 else jnp.concatenate(parts, axis=axis)

    def scores(first, size):
        k = joined([kv_s[rows_of(first + i), :CW] for i in range(size)], 0)
        s = lax.dot_general(q_s[...], k, (((1,), (1,)), ((), ())), preferred_element_type=jnp.float32)
        halves = []
        for i in range(size):
            b = list_s[first + i]
            for t in range(2):
                bias = jnp.where(flags_ref[2 * b + t] > 0, 0.0, NEG_FILL)
                at = 2 * i + t
                halves.append(s[:, at * TILE : (at + 1) * TILE] * SCALE2 + bias)
        return halves

    def own_scores():
        s = lax.dot_general(q_s[...], kv_s[last:, :CW], (((1,), (1,)), ((), ())), preferred_element_type=jnp.float32)
        s = (s.reshape(HEADS, TILE, BLOCK) * SCALE2 + bias_s[...][None]).reshape(QROWS, BLOCK)
        return [s[:, :TILE], s[:, TILE:]]

    def top_of(halves):
        m = jnp.max(functools.reduce(jnp.maximum, halves), axis=1, keepdims=True)
        return jnp.broadcast_to(m, (QROWS, TILE))

    def weigh(halves, v):
        m = m_s[...]
        p = jnp.concatenate([jnp.exp2(s - m).astype(jnp.bfloat16) for s in halves], axis=1)
        return jnp.dot(p, v, preferred_element_type=jnp.float32)

    def absorb(first, size):
        v = joined([kv_s[rows_of(first + i), CW:] for i in range(size)], 0)
        acc_s[...] += weigh(scores(first, size), v)

    def attempt(a, _):
        @pl.when(jnp.logical_or(a == 0, again_s[0] == 1))
        def _():
            @pl.when(a == 0)
            def _():
                m_s[...] = jnp.zeros_like(m_s)

            @pl.when(a == 1)
            def _():
                m_s[...] = top_of(own_scores()) if own else jnp.full_like(m_s, NEG_FILL)

                def top(i, _):
                    m_s[...] = jnp.maximum(m_s[...], top_of(scores(i, 1)))
                    return 0

                lax.fori_loop(0, count, top, 0)

            acc_s[...] = jnp.zeros_like(acc_s)
            done = 0
            for size in (4, 2, 1):

                def group(j, _, size=size, done=done):
                    absorb(done + j * size, size)
                    return 0

                loops = (count - done) // size
                lax.fori_loop(0, loops, group, 0)
                done = done + loops * size
            if own:
                acc_s[...] += weigh(own_scores(), kv_s[last:, CW:])
            raw = acc_s[:, CW:]
            total = jnp.maximum(raw, 1e-30)
            inverse = 1.0 / total
            log_total = jnp.log2(total)
            loud = jnp.max(jnp.abs(log_total)) > QUIET
            if not own:
                loud = jnp.logical_and(loud, count > 0)
            again_s[0] = jnp.where(loud, 1, 0)
            lse = m_s[...] + log_total
            if not own:
                lse = jnp.where(raw > 0, lse, NEG_FILL)
            head = lanes // STATS
            stats = lse[:TILE]
            for h in range(HEADS):
                rows = slice(h * TILE, (h + 1) * TILE)
                out_ref[:, h * CW : (h + 1) * CW] = (acc_s[rows, :CW] * inverse[rows]).astype(out_ref.dtype)
                stats = jnp.where(head == h, lse[rows], stats)
            if not own:
                a_, b_, c_ = split_three(stats)
                which = lanes % STATS
                stats = jnp.where(which == 0, a_, jnp.where(which == 1, b_, c_))
            out_ref[:, HEADS * CW :] = stats.astype(out_ref.dtype)
        return 0

    again_s[0] = 0
    for copy in copies:
        copy.wait()
    if own:
        own_bias(seg_ref, bias_s)
    lax.fori_loop(0, 2, attempt, 0)
    if own:
        weight_copy.wait()


def attend(flags, q, pieces, own_parts=None):
    own = own_parts is not None
    args = [flags, q, *pieces]
    vmem = pl.BlockSpec(memory_space=pltpu.VMEM)
    out_shape = [pltpu.VMEM((TILE, HEADS * CW + CW), jnp.float32 if own else jnp.bfloat16)]
    if own:
        out_shape.append(pltpu.VMEM(own_parts[-1].shape, own_parts[-1].dtype))
    keys = SHARES * SHARE + BLOCK * own
    return pl.pallas_call(
        functools.partial(attend_kernel, own),
        out_shape=out_shape,
        in_specs=[pl.BlockSpec(memory_space=pltpu.SMEM)]
        + [vmem] * (len(args) - 1)
        + [pl.BlockSpec(memory_space=m) for m in (pl.ANY, pl.ANY, pltpu.HBM, pltpu.HBM)] * own,
        out_specs=[vmem] * len(out_shape),
        scratch_shapes=[
            pltpu.VMEM((keys, 3 * CW), jnp.bfloat16),
            pltpu.VMEM((QROWS, CW), jnp.bfloat16),
            pltpu.VMEM((QROWS, TILE), jnp.float32),
            pltpu.VMEM((QROWS, 2 * CW), jnp.float32),
            pltpu.SMEM((keys // BLOCK + 1,), jnp.int32),
            pltpu.SMEM((1,), jnp.int32),
        ]
        + [
            pltpu.VMEM((TILE, BLOCK), jnp.float32),
            pltpu.VMEM((ROWS // TILE, TILE), jnp.int32),
            pltpu.SemaphoreType.DMA((4,)),
        ]
        * own,
        compiler_params=pltpu.CompilerParams(vmem_limit_bytes=10 << 20),
        cost_estimate=pl.CostEstimate(
            flops=QROWS * 1024 * CW * 4, bytes_accessed=8388608, transcendentals=0
        ),
        name="attend_own" if own else "attend_other",
    )(*args, *(own_parts or ()))


def combine(refs, att_s):
    stats = [r[:, HEADS * CW :].astype(jnp.float32) for r in refs]
    for h in range(HEADS):
        cols = slice(h * CW, (h + 1) * CW)
        i = STATS * h
        lses = [stats[0][:, i : i + 1]]
        for st in stats[1:]:
            lses.append(st[:, i : i + 1] + st[:, i + 1 : i + 2] + st[:, i + 2 : i + 3])
        top = functools.reduce(jnp.maximum, lses)
        weights = [jnp.exp2(v - top) for v in lses]
        inverse = 1.0 / sum(weights)
        mixed = sum(r[:, cols].astype(jnp.float32) * (w * inverse) for r, w in zip(refs, weights))
        att_s[:, cols] = mixed.astype(jnp.bfloat16)


def project_kernel(first, *refs):
    if first:
        own_ref, a_ref, b_ref, c_ref, w_ref, *targets, att_ref = refs
        offsets = (-4, 3, -2)
        combine((own_ref, a_ref, b_ref, c_ref), att_ref)
    else:
        att_ref, w_ref, *targets = refs
        offsets = (1, -3, 2, -1, 0)
    z, sign = lax.axis_index("z"), 1 - 2 * lax.axis_index("core")
    for offset, target in zip(offsets, targets):
        block = lax.rem(z + sign * offset + ZS, ZS)
        start = pl.multiple_of(block * OUT_BLOCK, CW)
        weight = w_ref[:, pl.ds(start, OUT_BLOCK)]
        term = jnp.dot(att_ref[...], weight, preferred_element_type=jnp.float32)
        target[...] = term.astype(target.dtype)


def project(parts, weight):
    first = len(parts) > 1
    rows, width = TILE, HEADS * CW
    vmem = pl.BlockSpec(memory_space=pltpu.VMEM)
    one = jax.ShapeDtypeStruct((rows, OUT_BLOCK), jnp.bfloat16)
    if first:
        out_shape = [one] * 3 + [jax.ShapeDtypeStruct((rows, width), jnp.bfloat16)]
    else:
        out_shape = [one] + [jax.ShapeDtypeStruct(one.shape, jnp.float32)] * 4
    return pl.pallas_call(
        functools.partial(project_kernel, first),
        out_shape=out_shape,
        in_specs=[vmem] * (len(parts) + 1),
        out_specs=[vmem] * len(out_shape),
        compiler_params=pltpu.CompilerParams(vmem_limit_bytes=8 << 20),
        cost_estimate=pl.CostEstimate(
            flops=2 * rows * width * OUT_BLOCK * 4, bytes_accessed=6 << 20, transcendentals=0
        ),
        name="project_first" if first else "project_second",
    )(*parts, weight)


def along_z(block, step):
    route = [
        (c * ZS + z, c * ZS + (z + (step if c == 0 else -step)) % ZS)
        for c in range(CORES)
        for z in range(ZS)
    ]
    return lax.ppermute(block, ("core", "z"), route)


def body(q, rkeys, rvalues, pkeys, pvalues, weight, segment_ids, block_mask):
    kv, rkv, q = prepare(pkeys, pvalues, rkeys, rvalues, q)
    first, first_q = opposite(kv, "x", 1), opposite(q, "y", 1)
    second, second_q = opposite(kv, "x", -1), opposite(q, "y", -1)
    prev = shifted(rkv, ("x", "y", "core"), -1)
    first, first_q, prev, seen = lax.optimization_barrier(
        (first, first_q, prev, visibility(block_mask))
    )
    far, far_q = opposite(first, "x", 1), opposite(first_q, "y", 1)
    second, second_q, far_q = lax.optimization_barrier((second, second_q, far_q))
    mine = [kv, first, second, far]
    pieces = mine + [shifted(p, "core", 1) for p in mine]

    two = shifted(attend(seen[1], far_q, pieces)[0], "y", 2)
    next_one = opposite(attend(seen[2], first_q, pieces)[0], "y", -1)
    last_one = opposite(attend(seen[3], second_q, pieces)[0], "y", 1)
    segments = pltpu.with_memory_space_constraint(segment_ids.reshape(-1, TILE), pltpu.HBM)
    weight = pltpu.with_memory_space_constraint(weight, pltpu.HBM)
    own, weight = attend(seen[0], q, pieces, (prev, rkv, segments, weight))

    *sent, att = project([own, two, next_one, last_one], weight)
    for3, for2, for1 = (along_z(b, step) for b, step in zip(sent, (-1, 1, -1)))
    direct, rest3, rest2, rest1, total = project([att], weight)
    back3 = (rest3 + for3.astype(jnp.float32)).astype(jnp.bfloat16)
    back3, direct = lax.optimization_barrier((back3, direct))
    back3, got_direct = along_z(back3, -3), along_z(direct, 1)
    on2 = along_z((rest2 + for2.astype(jnp.float32)).astype(jnp.bfloat16), 2)
    back1 = along_z((rest1 + for1.astype(jnp.float32)).astype(jnp.bfloat16), -1)
    total = total + got_direct.astype(jnp.float32)
    for part in (back1, on2, back3):
        total = total + part.astype(jnp.float32)
    return total.astype(jnp.bfloat16)


def solution(mesh):
    split = Mesh(mesh.devices.reshape(XS, YS, CORES, ZS), ("x", "y", "core", "z"))
    seq = ("x", "y", "core")
    placed = (P(seq, "z"),) * 5 + (P("z", None), P(), P())
    return jax.shard_map(
        body, mesh=split, in_specs=placed, out_specs=P(seq, "z"), check_vma=False
    )
```

```python
import functools
import math

import jax
import jax.numpy as jnp
from jax import lax
from jax.experimental import pallas as pl
from jax.experimental.pallas import tpu as pltpu
from jax.sharding import Mesh, PartitionSpec as P

H = 64
KVH = 8
CW = 128
TILE = 128
HEADS = H // KVH
XS, YS, CORES, ZS = 4, 4, 2, 8
ROWS = XS * YS * CORES * TILE
SHARE = 512
SHARES = XS * CORES
BLOCK = 256
NEG_FILL = -1e30
SCALE2 = math.log2(math.e) / math.sqrt(CW)
STATS = 3
QUIET = 64.0
QROWS = HEADS * TILE
OUT_BLOCK = 640


def seq_index(x, y, c):
    return (lax.rem(x, XS) * YS + lax.rem(y, YS)) * CORES + c


def shifted(block, axis, step):
    n = lax.axis_size(axis)
    return lax.ppermute(block, axis, [((i + step) % n, i) for i in range(n)])


def own_bias(seg_ref, bias_s):
    device = seq_index(*(lax.axis_index(a) for a in ("x", "y", "core")))
    mine = seg_ref[pl.ds(device, 1), :]
    before = seg_ref[pl.ds(jnp.maximum(device - 1, 0), 1), :]
    before = jnp.where(device > 0, before, -1)
    rows = jnp.broadcast_to(mine, (TILE, TILE)).T
    r = lax.broadcasted_iota(jnp.int32, (TILE, TILE), 0)
    c = lax.broadcasted_iota(jnp.int32, (TILE, TILE), 1)
    bias_s[:, :TILE] = jnp.where(rows == before, 0.0, NEG_FILL)
    bias_s[:, TILE:] = jnp.where((rows == mine) & (c <= r), 0.0, NEG_FILL)


def prepare_kernel(pk_ref, pv_ref, rk_ref, rv_ref, q_hbm, kv_ref, rkv_ref, q_ref, sems):
    moves = (
        (pk_ref, kv_ref.at[:, :CW]),
        (pv_ref, kv_ref.at[:, CW:]),
        (rk_ref, rkv_ref.at[:, :CW]),
        (rv_ref, rkv_ref.at[:, CW:]),
    ) + tuple(
        (q_hbm.at[:, i : i + 2 * CW], q_ref.at[i // 2 : i // 2 + TILE])
        for i in range(0, HEADS * CW, 2 * CW)
    )
    copies = [pltpu.make_async_copy(a, b, sems.at[i]) for i, (a, b) in enumerate(moves)]
    for copy in copies:
        copy.start()
    for copy in copies:
        copy.wait()


def prepare(pkeys, pvalues, rkeys, rvalues, q):
    return pl.pallas_call(
        prepare_kernel,
        out_shape=[
            pltpu.VMEM((pkeys.shape[0], 2 * CW), jnp.bfloat16),
            pltpu.VMEM((TILE, 2 * CW), jnp.bfloat16),
            pltpu.VMEM((QROWS // 2, 2 * CW), q.dtype),
        ],
        in_specs=[pl.BlockSpec(memory_space=pltpu.HBM)] * 5,
        out_specs=[pl.BlockSpec(memory_space=pltpu.VMEM)] * 3,
        scratch_shapes=[pltpu.SemaphoreType.DMA((8,))],
        compiler_params=pltpu.CompilerParams(vmem_limit_bytes=8 << 20),
        cost_estimate=pl.CostEstimate(flops=1, bytes_accessed=1, transcendentals=0),
        name="prepare",
    )(
        *(
            pltpu.with_memory_space_constraint(a, pltpu.HBM)
            for a in (pkeys, pvalues, rkeys, rvalues, q)
        )
    )


def visibility_kernel(mask_hbm, *refs):
    flag_refs, (mask_ref, sem) = refs[:4], refs[4:]
    copy = pltpu.make_async_copy(mask_hbm, mask_ref, sem)
    copy.start()
    copy.wait()
    x, y, core = (lax.axis_index(a) for a in ("x", "y", "core"))
    tiles = SHARE // TILE
    step = XS + 1 - 2 * core
    back = XS - 1 + 2 * core
    other = 1 - core
    shares = (
        (0, core), (step, core), (back, core), (2, core),
        (0, other), (back, other), (step, other), (2, other),
    )
    for flags, dy in zip(flag_refs, (0, 2, 1 - 2 * core, 2 * core - 1)):
        row = seq_index(x, y + dy + YS, core)
        for p, (dx, c) in enumerate(shares):
            first = seq_index(x + dx, y, c) * tiles
            for t in range(tiles):
                flags[p * tiles + t] = mask_ref[row, first + t]


def visibility(block_mask):
    return pl.pallas_call(
        visibility_kernel,
        out_shape=[jax.ShapeDtypeStruct((SHARES * SHARE // TILE,), jnp.int32)] * 4,
        in_specs=[pl.BlockSpec(memory_space=pltpu.HBM)],
        out_specs=[pl.BlockSpec(memory_space=pltpu.SMEM)] * 4,
        scratch_shapes=[pltpu.SMEM(block_mask.shape, jnp.int32), pltpu.SemaphoreType.DMA(())],
        compiler_params=pltpu.CompilerParams(vmem_limit_bytes=4 << 20),
        cost_estimate=pl.CostEstimate(flops=1, bytes_accessed=1, transcendentals=0),
        name="visibility",
    )(pltpu.with_memory_space_constraint(block_mask, pltpu.HBM))


def split_three(value):
    parts = []
    for _ in range(STATS):
        parts.append(value.astype(jnp.bfloat16).astype(jnp.float32))
        value = value - parts[-1]
    return parts


def opposite(block, axis, step):
    n = lax.axis_size(axis)
    route = [
        (((i + (step if c == 0 else -step)) % n) * CORES + c, i * CORES + c)
        for i in range(n)
        for c in range(CORES)
    ]
    return lax.ppermute(block, (axis, "core"), route)


def attend_kernel(own, flags_ref, q_ref, *refs):
    kv_refs, refs = refs[:SHARES], refs[SHARES:]
    if own:
        (prev_ref, mine_ref, seg_hbm, w_hbm), refs = refs[:4], refs[4:]
        w_ref, refs = refs[1], refs[:1] + refs[2:]
    out_ref, kv_s, q_s, m_s, acc_s, list_s, again_s = refs[:7]
    last = SHARES * SHARE
    copies = []
    if own:
        bias_s, seg_ref, sems = refs[7:]
        targets = (
            kv_s.at[last : last + TILE, : 2 * CW],
            kv_s.at[last + TILE : last + BLOCK, : 2 * CW],
            seg_ref,
        )
        for i, (source, target) in enumerate(zip((prev_ref, mine_ref, seg_hbm), targets)):
            copies.append(pltpu.make_async_copy(source, target, sems.at[i]))
            copies[-1].start()
        weight_copy = pltpu.make_async_copy(w_hbm, w_ref, sems.at[3])
        weight_copy.start()
    lanes = lax.broadcasted_iota(jnp.int32, (TILE, CW), 1)

    count = 0
    block = 0
    for ref in kv_refs:
        for b in range(ref.shape[0] // BLOCK):
            seen = flags_ref[2 * block] + flags_ref[2 * block + 1] > 0
            list_s[count] = block

            @pl.when(seen)
            def _():
                rows = slice(block * BLOCK, (block + 1) * BLOCK)
                kv_s[rows, : 2 * CW] = ref[b * BLOCK : (b + 1) * BLOCK]
                kv_s[rows, 2 * CW :] = jnp.ones((BLOCK, CW), jnp.bfloat16)

            count = count + jnp.where(seen, 1, 0)
            block += 1
    if own:
        kv_s[last:, 2 * CW :] = jnp.ones((BLOCK, CW), jnp.bfloat16)
    for h in range(HEADS):
        at = h // 2 * TILE
        q_s[h * TILE : (h + 1) * TILE, :] = q_ref[at : at + TILE, h % 2 * CW : (h % 2 + 1) * CW]

    def rows_of(i):
        return pl.ds(pl.multiple_of(list_s[i] * BLOCK, BLOCK), BLOCK)

    def joined(parts, axis):
        return parts[0] if len(parts) == 1 else jnp.concatenate(parts, axis=axis)

    def scores(first, size):
        k = joined([kv_s[rows_of(first + i), :CW] for i in range(size)], 0)
        s = lax.dot_general(q_s[...], k, (((1,), (1,)), ((), ())), preferred_element_type=jnp.float32)
        halves = []
        for i in range(size):
            b = list_s[first + i]
            for t in range(2):
                bias = jnp.where(flags_ref[2 * b + t] > 0, 0.0, NEG_FILL)
                at = 2 * i + t
                halves.append(s[:, at * TILE : (at + 1) * TILE] * SCALE2 + bias)
        return halves

    def own_scores():
        s = lax.dot_general(q_s[...], kv_s[last:, :CW], (((1,), (1,)), ((), ())), preferred_element_type=jnp.float32)
        s = (s.reshape(HEADS, TILE, BLOCK) * SCALE2 + bias_s[...][None]).reshape(QROWS, BLOCK)
        return [s[:, :TILE], s[:, TILE:]]

    def top_of(halves):
        m = jnp.max(functools.reduce(jnp.maximum, halves), axis=1, keepdims=True)
        return jnp.broadcast_to(m, (QROWS, TILE))

    def weigh(halves, v):
        m = m_s[...]
        p = jnp.concatenate([jnp.exp2(s - m).astype(jnp.bfloat16) for s in halves], axis=1)
        return jnp.dot(p, v, preferred_element_type=jnp.float32)

    def absorb(first, size):
        v = joined([kv_s[rows_of(first + i), CW:] for i in range(size)], 0)
        acc_s[...] += weigh(scores(first, size), v)

    def attempt(a, _):
        @pl.when(jnp.logical_or(a == 0, again_s[0] == 1))
        def _():
            @pl.when(a == 0)
            def _():
                m_s[...] = jnp.zeros_like(m_s)

            @pl.when(a == 1)
            def _():
                m_s[...] = top_of(own_scores()) if own else jnp.full_like(m_s, NEG_FILL)

                def top(i, _):
                    m_s[...] = jnp.maximum(m_s[...], top_of(scores(i, 1)))
                    return 0

                lax.fori_loop(0, count, top, 0)

            acc_s[...] = jnp.zeros_like(acc_s)
            done = 0
            for size in (4, 2, 1):

                def group(j, _, size=size, done=done):
                    absorb(done + j * size, size)
                    return 0

                loops = (count - done) // size
                lax.fori_loop(0, loops, group, 0)
                done = done + loops * size
            if own:
                acc_s[...] += weigh(own_scores(), kv_s[last:, CW:])
            raw = acc_s[:, CW:]
            total = jnp.maximum(raw, 1e-30)
            inverse = 1.0 / total
            log_total = jnp.log2(total)
            loud = jnp.max(jnp.abs(log_total)) > QUIET
            if not own:
                loud = jnp.logical_and(loud, count > 0)
            again_s[0] = jnp.where(loud, 1, 0)
            lse = m_s[...] + log_total
            if not own:
                lse = jnp.where(raw > 0, lse, NEG_FILL)
            head = lanes // STATS
            stats = lse[:TILE]
            for h in range(HEADS):
                rows = slice(h * TILE, (h + 1) * TILE)
                out_ref[:, h * CW : (h + 1) * CW] = (acc_s[rows, :CW] * inverse[rows]).astype(out_ref.dtype)
                stats = jnp.where(head == h, lse[rows], stats)
            if not own:
                a_, b_, c_ = split_three(stats)
                which = lanes % STATS
                stats = jnp.where(which == 0, a_, jnp.where(which == 1, b_, c_))
            out_ref[:, HEADS * CW :] = stats.astype(out_ref.dtype)
        return 0

    again_s[0] = 0
    for copy in copies:
        copy.wait()
    if own:
        own_bias(seg_ref, bias_s)
    lax.fori_loop(0, 2, attempt, 0)
    if own:
        weight_copy.wait()


def attend(flags, q, pieces, own_parts=None):
    own = own_parts is not None
    args = [flags, q, *pieces]
    vmem = pl.BlockSpec(memory_space=pltpu.VMEM)
    out_shape = [pltpu.VMEM((TILE, HEADS * CW + CW), jnp.float32 if own else jnp.bfloat16)]
    if own:
        out_shape.append(pltpu.VMEM(own_parts[-1].shape, own_parts[-1].dtype))
    keys = SHARES * SHARE + BLOCK * own
    return pl.pallas_call(
        functools.partial(attend_kernel, own),
        out_shape=out_shape,
        in_specs=[pl.BlockSpec(memory_space=pltpu.SMEM)]
        + [vmem] * (len(args) - 1)
        + [pl.BlockSpec(memory_space=m) for m in (pl.ANY, pl.ANY, pltpu.HBM, pltpu.HBM)] * own,
        out_specs=[vmem] * len(out_shape),
        scratch_shapes=[
            pltpu.VMEM((keys, 3 * CW), jnp.bfloat16),
            pltpu.VMEM((QROWS, CW), jnp.bfloat16),
            pltpu.VMEM((QROWS, TILE), jnp.float32),
            pltpu.VMEM((QROWS, 2 * CW), jnp.float32),
            pltpu.SMEM((keys // BLOCK + 1,), jnp.int32),
            pltpu.SMEM((1,), jnp.int32),
        ]
        + [
            pltpu.VMEM((TILE, BLOCK), jnp.float32),
            pltpu.VMEM((ROWS // TILE, TILE), jnp.int32),
            pltpu.SemaphoreType.DMA((4,)),
        ]
        * own,
        compiler_params=pltpu.CompilerParams(vmem_limit_bytes=10 << 20),
        cost_estimate=pl.CostEstimate(
            flops=QROWS * 1024 * CW * 4, bytes_accessed=8388608, transcendentals=0
        ),
        name="attend_own" if own else "attend_other",
    )(*args, *(own_parts or ()))


def combine(refs, att_s):
    stats = [r[:, HEADS * CW :].astype(jnp.float32) for r in refs]
    for h in range(HEADS):
        cols = slice(h * CW, (h + 1) * CW)
        i = STATS * h
        lses = [stats[0][:, i : i + 1]]
        for st in stats[1:]:
            lses.append(st[:, i : i + 1] + st[:, i + 1 : i + 2] + st[:, i + 2 : i + 3])
        top = functools.reduce(jnp.maximum, lses)
        weights = [jnp.exp2(v - top) for v in lses]
        inverse = 1.0 / sum(weights)
        mixed = sum(r[:, cols].astype(jnp.float32) * (w * inverse) for r, w in zip(refs, weights))
        att_s[:, cols] = mixed.astype(jnp.bfloat16)


def project_kernel(first, *refs):
    if first:
        own_ref, a_ref, b_ref, c_ref, w_ref, *targets, att_ref = refs
        offsets = (-4, 3, -2)
        combine((own_ref, a_ref, b_ref, c_ref), att_ref)
    else:
        att_ref, w_ref, *targets = refs
        offsets = (1, -3, 2, -1, 0)
    z, sign = lax.axis_index("z"), 1 - 2 * lax.axis_index("core")
    for offset, target in zip(offsets, targets):
        block = lax.rem(z + sign * offset + ZS, ZS)
        start = pl.multiple_of(block * OUT_BLOCK, CW)
        weight = w_ref[:, pl.ds(start, OUT_BLOCK)]
        term = jnp.dot(att_ref[...], weight, preferred_element_type=jnp.float32)
        target[...] = term.astype(target.dtype)


def project(parts, weight):
    first = len(parts) > 1
    rows, width = TILE, HEADS * CW
    vmem = pl.BlockSpec(memory_space=pltpu.VMEM)
    one = jax.ShapeDtypeStruct((rows, OUT_BLOCK), jnp.bfloat16)
    if first:
        out_shape = [one] * 3 + [jax.ShapeDtypeStruct((rows, width), jnp.bfloat16)]
    else:
        out_shape = [one] + [jax.ShapeDtypeStruct(one.shape, jnp.float32)] * 4
    return pl.pallas_call(
        functools.partial(project_kernel, first),
        out_shape=out_shape,
        in_specs=[vmem] * (len(parts) + 1),
        out_specs=[vmem] * len(out_shape),
        compiler_params=pltpu.CompilerParams(vmem_limit_bytes=8 << 20),
        cost_estimate=pl.CostEstimate(
            flops=2 * rows * width * OUT_BLOCK * 4, bytes_accessed=6 << 20, transcendentals=0
        ),
        name="project_first" if first else "project_second",
    )(*parts, weight)


def along_z(block, step):
    route = [
        (c * ZS + z, c * ZS + (z + (step if c == 0 else -step)) % ZS)
        for c in range(CORES)
        for z in range(ZS)
    ]
    return lax.ppermute(block, ("core", "z"), route)


def body(q, rkeys, rvalues, pkeys, pvalues, weight, segment_ids, block_mask):
    kv, rkv, q = prepare(pkeys, pvalues, rkeys, rvalues, q)
    first, first_q = opposite(kv, "x", 1), opposite(q, "y", 1)
    second, second_q = opposite(kv, "x", -1), opposite(q, "y", -1)
    prev = shifted(rkv, ("x", "y", "core"), -1)
    first, first_q, prev, seen = lax.optimization_barrier(
        (first, first_q, prev, visibility(block_mask))
    )
    far, far_q = opposite(first, "x", 1), opposite(first_q, "y", 1)
    second, second_q, far_q = lax.optimization_barrier((second, second_q, far_q))
    mine = [kv, first, second, far]
    pieces = mine + [shifted(p, "core", 1) for p in mine]

    next_part = attend(seen[2], first_q, pieces)[0]
    next_part, far_q = lax.optimization_barrier((next_part, far_q))
    next_one = opposite(next_part, "y", -1)
    part = attend(seen[1], far_q, pieces)[0]
    part, second_q = lax.optimization_barrier((part, second_q))
    two = shifted(part, "y", 2)
    last_one = opposite(attend(seen[3], second_q, pieces)[0], "y", 1)
    segments = pltpu.with_memory_space_constraint(segment_ids.reshape(-1, TILE), pltpu.HBM)
    weight = pltpu.with_memory_space_constraint(weight, pltpu.HBM)
    own, weight = attend(seen[0], q, pieces, (prev, rkv, segments, weight))

    *sent, att = project([own, two, next_one, last_one], weight)
    for3, for2, for1 = (along_z(b, step) for b, step in zip(sent, (-1, 1, -1)))
    direct, rest3, rest2, rest1, total = project([att], weight)
    got_direct = along_z(direct, 1)
    back3 = along_z((rest3 + for3.astype(jnp.float32)).astype(jnp.bfloat16), -3)
    on2 = along_z((rest2 + for2.astype(jnp.float32)).astype(jnp.bfloat16), 2)
    back1 = along_z((rest1 + for1.astype(jnp.float32)).astype(jnp.bfloat16), -1)
    total = total + got_direct.astype(jnp.float32)
    for part in (back1, on2, back3):
        total = total + part.astype(jnp.float32)
    return total.astype(jnp.bfloat16)


def solution(mesh):
    split = Mesh(mesh.devices.reshape(XS, YS, CORES, ZS), ("x", "y", "core", "z"))
    seq = ("x", "y", "core")
    placed = (P(seq, "z"),) * 5 + (P("z", None), P(), P())
    return jax.shard_map(
        body, mesh=split, in_specs=placed, out_specs=P(seq, "z"), check_vma=False
    )
```

```python
import functools
import math

import jax
import jax.numpy as jnp
from jax import lax
from jax.experimental import pallas as pl
from jax.experimental.pallas import tpu as pltpu
from jax.sharding import Mesh, PartitionSpec as P

H = 64
KVH = 8
CW = 128
TILE = 128
HEADS = H // KVH
XS, YS, CORES, ZS = 4, 4, 2, 8
ROWS = XS * YS * CORES * TILE
SHARE = 512
SHARES = XS * CORES
BLOCK = 256
NEG_FILL = -1e30
SCALE2 = math.log2(math.e) / math.sqrt(CW)
STATS = 3
QUIET = 64.0
QROWS = HEADS * TILE
OUT_BLOCK = 640


def seq_index(x, y, c):
    return (lax.rem(x, XS) * YS + lax.rem(y, YS)) * CORES + c


def shifted(block, axis, step):
    n = lax.axis_size(axis)
    return lax.ppermute(block, axis, [((i + step) % n, i) for i in range(n)])


def own_bias(seg_ref, bias_s):
    device = seq_index(*(lax.axis_index(a) for a in ("x", "y", "core")))
    mine = seg_ref[pl.ds(device, 1), :]
    before = seg_ref[pl.ds(jnp.maximum(device - 1, 0), 1), :]
    before = jnp.where(device > 0, before, -1)
    rows = jnp.broadcast_to(mine, (TILE, TILE)).T
    r = lax.broadcasted_iota(jnp.int32, (TILE, TILE), 0)
    c = lax.broadcasted_iota(jnp.int32, (TILE, TILE), 1)
    bias_s[:, :TILE] = jnp.where(rows == before, 0.0, NEG_FILL)
    bias_s[:, TILE:] = jnp.where((rows == mine) & (c <= r), 0.0, NEG_FILL)


def prepare_kernel(pk_ref, pv_ref, rk_ref, rv_ref, q_hbm, kv_ref, rkv_ref, q_ref, sems):
    moves = (
        (pk_ref, kv_ref.at[:, :CW]),
        (pv_ref, kv_ref.at[:, CW:]),
        (rk_ref, rkv_ref.at[:, :CW]),
        (rv_ref, rkv_ref.at[:, CW:]),
    ) + tuple(
        (q_hbm.at[:, i : i + 2 * CW], q_ref.at[i // 2 : i // 2 + TILE])
        for i in range(0, HEADS * CW, 2 * CW)
    )
    copies = [pltpu.make_async_copy(a, b, sems.at[i]) for i, (a, b) in enumerate(moves)]
    for copy in copies:
        copy.start()
    for copy in copies:
        copy.wait()


def prepare(pkeys, pvalues, rkeys, rvalues, q):
    return pl.pallas_call(
        prepare_kernel,
        out_shape=[
            pltpu.VMEM((pkeys.shape[0], 2 * CW), jnp.bfloat16),
            pltpu.VMEM((TILE, 2 * CW), jnp.bfloat16),
            pltpu.VMEM((QROWS // 2, 2 * CW), q.dtype),
        ],
        in_specs=[pl.BlockSpec(memory_space=pltpu.HBM)] * 5,
        out_specs=[pl.BlockSpec(memory_space=pltpu.VMEM)] * 3,
        scratch_shapes=[pltpu.SemaphoreType.DMA((8,))],
        compiler_params=pltpu.CompilerParams(vmem_limit_bytes=8 << 20),
        cost_estimate=pl.CostEstimate(flops=1, bytes_accessed=1, transcendentals=0),
        name="prepare",
    )(
        *(
            pltpu.with_memory_space_constraint(a, pltpu.HBM)
            for a in (pkeys, pvalues, rkeys, rvalues, q)
        )
    )


def visibility_kernel(mask_hbm, *refs):
    flag_refs, (mask_ref, sem) = refs[:4], refs[4:]
    copy = pltpu.make_async_copy(mask_hbm, mask_ref, sem)
    copy.start()
    copy.wait()
    x, y, core = (lax.axis_index(a) for a in ("x", "y", "core"))
    tiles = SHARE // TILE
    step = XS + 1 - 2 * core
    back = XS - 1 + 2 * core
    other = 1 - core
    shares = (
        (0, core), (step, core), (back, core), (2, core),
        (0, other), (back, other), (step, other), (2, other),
    )
    for flags, dy in zip(flag_refs, (0, 2, 1 - 2 * core, 2 * core - 1)):
        row = seq_index(x, y + dy + YS, core)
        for p, (dx, c) in enumerate(shares):
            first = seq_index(x + dx, y, c) * tiles
            for t in range(tiles):
                flags[p * tiles + t] = mask_ref[row, first + t]


def visibility(block_mask):
    return pl.pallas_call(
        visibility_kernel,
        out_shape=[jax.ShapeDtypeStruct((SHARES * SHARE // TILE,), jnp.int32)] * 4,
        in_specs=[pl.BlockSpec(memory_space=pltpu.HBM)],
        out_specs=[pl.BlockSpec(memory_space=pltpu.SMEM)] * 4,
        scratch_shapes=[pltpu.SMEM(block_mask.shape, jnp.int32), pltpu.SemaphoreType.DMA(())],
        compiler_params=pltpu.CompilerParams(vmem_limit_bytes=4 << 20),
        cost_estimate=pl.CostEstimate(flops=1, bytes_accessed=1, transcendentals=0),
        name="visibility",
    )(pltpu.with_memory_space_constraint(block_mask, pltpu.HBM))


def split_three(value):
    parts = []
    for _ in range(STATS):
        parts.append(value.astype(jnp.bfloat16).astype(jnp.float32))
        value = value - parts[-1]
    return parts


def opposite(block, axis, step):
    n = lax.axis_size(axis)
    route = [
        (((i + (step if c == 0 else -step)) % n) * CORES + c, i * CORES + c)
        for i in range(n)
        for c in range(CORES)
    ]
    return lax.ppermute(block, (axis, "core"), route)


def attend_kernel(own, flags_ref, q_ref, *refs):
    kv_refs, refs = refs[:SHARES], refs[SHARES:]
    if own:
        (prev_ref, mine_ref, seg_hbm, w_hbm), refs = refs[:4], refs[4:]
        w_ref, refs = refs[1], refs[:1] + refs[2:]
    out_ref, kv_s, q_s, m_s, acc_s, list_s = refs[:6]
    last = SHARES * SHARE
    copies = []
    if own:
        bias_s, seg_ref, sems = refs[6:]
        targets = (
            kv_s.at[last : last + TILE, : 2 * CW],
            kv_s.at[last + TILE : last + BLOCK, : 2 * CW],
            seg_ref,
        )
        for i, (source, target) in enumerate(zip((prev_ref, mine_ref, seg_hbm), targets)):
            copies.append(pltpu.make_async_copy(source, target, sems.at[i]))
            copies[-1].start()
        weight_copy = pltpu.make_async_copy(w_hbm, w_ref, sems.at[3])
        weight_copy.start()
    lanes = lax.broadcasted_iota(jnp.int32, (TILE, CW), 1)

    count = 0
    block = 0
    for ref in kv_refs:
        for b in range(ref.shape[0] // BLOCK):
            seen = flags_ref[2 * block] + flags_ref[2 * block + 1] > 0
            list_s[count] = block

            @pl.when(seen)
            def _():
                rows = slice(block * BLOCK, (block + 1) * BLOCK)
                kv_s[rows, : 2 * CW] = ref[b * BLOCK : (b + 1) * BLOCK]
                kv_s[rows, 2 * CW :] = jnp.ones((BLOCK, CW), jnp.bfloat16)

            count = count + jnp.where(seen, 1, 0)
            block += 1
    if own:
        kv_s[last:, 2 * CW :] = jnp.ones((BLOCK, CW), jnp.bfloat16)
    for h in range(HEADS):
        at = h // 2 * TILE
        q_s[h * TILE : (h + 1) * TILE, :] = q_ref[at : at + TILE, h % 2 * CW : (h % 2 + 1) * CW]

    def rows_of(i):
        return pl.ds(pl.multiple_of(list_s[i] * BLOCK, BLOCK), BLOCK)

    def joined(parts, axis):
        return parts[0] if len(parts) == 1 else jnp.concatenate(parts, axis=axis)

    def scores(first, size):
        k = joined([kv_s[rows_of(first + i), :CW] for i in range(size)], 0)
        s = lax.dot_general(q_s[...], k, (((1,), (1,)), ((), ())), preferred_element_type=jnp.float32)
        halves = []
        for i in range(size):
            b = list_s[first + i]
            for t in range(2):
                bias = jnp.where(flags_ref[2 * b + t] > 0, 0.0, NEG_FILL)
                at = 2 * i + t
                halves.append(s[:, at * TILE : (at + 1) * TILE] * SCALE2 + bias)
        return halves

    def own_scores():
        s = lax.dot_general(q_s[...], kv_s[last:, :CW], (((1,), (1,)), ((), ())), preferred_element_type=jnp.float32)
        s = (s.reshape(HEADS, TILE, BLOCK) * SCALE2 + bias_s[...][None]).reshape(QROWS, BLOCK)
        return [s[:, :TILE], s[:, TILE:]]

    def top_of(halves):
        m = jnp.max(functools.reduce(jnp.maximum, halves), axis=1, keepdims=True)
        return jnp.broadcast_to(m, (QROWS, TILE))

    def weigh(halves, v):
        m = m_s[...]
        p = jnp.concatenate([jnp.exp2(s - m).astype(jnp.bfloat16) for s in halves], axis=1)
        return jnp.dot(p, v, preferred_element_type=jnp.float32)

    def absorb(first, size):
        v = joined([kv_s[rows_of(first + i), CW:] for i in range(size)], 0)
        acc_s[...] += weigh(scores(first, size), v)

    def attempt(a):
        acc_s[...] = jnp.zeros_like(acc_s)
        done = 0
        for size in (4, 2, 1):

            def group(j, _, size=size, done=done):
                absorb(done + j * size, size)
                return 0

            loops = (count - done) // size
            lax.fori_loop(0, loops, group, 0)
            done = done + loops * size
        if own:
            acc_s[...] += weigh(own_scores(), kv_s[last:, CW:])
        raw = acc_s[:, CW:]
        total = jnp.maximum(raw, 1e-30)
        inverse = 1.0 / total
        log_total = jnp.log2(total)
        loud = jnp.max(jnp.abs(log_total)) > QUIET
        if not own:
            loud = jnp.logical_and(loud, count > 0)
        again = jnp.logical_and(loud, a == 0)
        lse = m_s[...] + log_total
        if not own:
            lse = jnp.where(raw > 0, lse, NEG_FILL)
        head = lanes // STATS
        stats = lse[:TILE]
        for h in range(HEADS):
            rows = slice(h * TILE, (h + 1) * TILE)
            out_ref[:, h * CW : (h + 1) * CW] = (acc_s[rows, :CW] * inverse[rows]).astype(out_ref.dtype)
            stats = jnp.where(head == h, lse[rows], stats)
        if not own:
            a_, b_, c_ = split_three(stats)
            which = lanes % STATS
            stats = jnp.where(which == 0, a_, jnp.where(which == 1, b_, c_))
        out_ref[:, HEADS * CW :] = stats.astype(out_ref.dtype)

        @pl.when(again)
        def _():
            m_s[...] = top_of(own_scores()) if own else jnp.full_like(m_s, NEG_FILL)

            def top(i, _):
                m_s[...] = jnp.maximum(m_s[...], top_of(scores(i, 1)))
                return 0

            lax.fori_loop(0, count, top, 0)

        return jnp.where(again, 1, 2)

    m_s[...] = jnp.zeros_like(m_s)
    for copy in copies:
        copy.wait()
    if own:
        own_bias(seg_ref, bias_s)
    lax.while_loop(lambda a: a < 2, attempt, jnp.int32(0))
    if own:
        weight_copy.wait()


def attend(flags, q, pieces, own_parts=None):
    own = own_parts is not None
    args = [flags, q, *pieces]
    vmem = pl.BlockSpec(memory_space=pltpu.VMEM)
    out_shape = [pltpu.VMEM((TILE, HEADS * CW + CW), jnp.float32 if own else jnp.bfloat16)]
    if own:
        out_shape.append(pltpu.VMEM(own_parts[-1].shape, own_parts[-1].dtype))
    keys = SHARES * SHARE + BLOCK * own
    return pl.pallas_call(
        functools.partial(attend_kernel, own),
        out_shape=out_shape,
        in_specs=[pl.BlockSpec(memory_space=pltpu.SMEM)]
        + [vmem] * (len(args) - 1)
        + [pl.BlockSpec(memory_space=m) for m in (pl.ANY, pl.ANY, pltpu.HBM, pltpu.HBM)] * own,
        out_specs=[vmem] * len(out_shape),
        scratch_shapes=[
            pltpu.VMEM((keys, 3 * CW), jnp.bfloat16),
            pltpu.VMEM((QROWS, CW), jnp.bfloat16),
            pltpu.VMEM((QROWS, TILE), jnp.float32),
            pltpu.VMEM((QROWS, 2 * CW), jnp.float32),
            pltpu.SMEM((keys // BLOCK + 1,), jnp.int32),
        ]
        + [
            pltpu.VMEM((TILE, BLOCK), jnp.float32),
            pltpu.VMEM((ROWS // TILE, TILE), jnp.int32),
            pltpu.SemaphoreType.DMA((4,)),
        ]
        * own,
        compiler_params=pltpu.CompilerParams(vmem_limit_bytes=10 << 20),
        cost_estimate=pl.CostEstimate(
            flops=QROWS * 1024 * CW * 4, bytes_accessed=8388608, transcendentals=0
        ),
        name="attend_own" if own else "attend_other",
    )(*args, *(own_parts or ()))


def combine(refs, att_s):
    stats = [r[:, HEADS * CW :].astype(jnp.float32) for r in refs]
    for h in range(HEADS):
        cols = slice(h * CW, (h + 1) * CW)
        i = STATS * h
        lses = [stats[0][:, i : i + 1]]
        for st in stats[1:]:
            lses.append(st[:, i : i + 1] + st[:, i + 1 : i + 2] + st[:, i + 2 : i + 3])
        top = functools.reduce(jnp.maximum, lses)
        weights = [jnp.exp2(v - top) for v in lses]
        inverse = 1.0 / sum(weights)
        mixed = sum(r[:, cols].astype(jnp.float32) * (w * inverse) for r, w in zip(refs, weights))
        att_s[:, cols] = mixed.astype(jnp.bfloat16)


def project_kernel(first, *refs):
    if first:
        own_ref, a_ref, b_ref, c_ref, w_ref, *targets, att_ref = refs
        offsets = (-4, 3, -2)
        combine((own_ref, a_ref, b_ref, c_ref), att_ref)
    else:
        att_ref, w_ref, *targets = refs
        offsets = (1, -3, 2, -1, 0)
    z, sign = lax.axis_index("z"), 1 - 2 * lax.axis_index("core")
    for offset, target in zip(offsets, targets):
        block = lax.rem(z + sign * offset + ZS, ZS)
        start = pl.multiple_of(block * OUT_BLOCK, CW)
        weight = w_ref[:, pl.ds(start, OUT_BLOCK)]
        term = jnp.dot(att_ref[...], weight, preferred_element_type=jnp.float32)
        target[...] = term.astype(target.dtype)


def project(parts, weight):
    first = len(parts) > 1
    rows, width = TILE, HEADS * CW
    vmem = pl.BlockSpec(memory_space=pltpu.VMEM)
    one = jax.ShapeDtypeStruct((rows, OUT_BLOCK), jnp.bfloat16)
    if first:
        out_shape = [one] * 3 + [jax.ShapeDtypeStruct((rows, width), jnp.bfloat16)]
    else:
        out_shape = [one] + [jax.ShapeDtypeStruct(one.shape, jnp.float32)] * 4
    return pl.pallas_call(
        functools.partial(project_kernel, first),
        out_shape=out_shape,
        in_specs=[vmem] * (len(parts) + 1),
        out_specs=[vmem] * len(out_shape),
        compiler_params=pltpu.CompilerParams(vmem_limit_bytes=8 << 20),
        cost_estimate=pl.CostEstimate(
            flops=2 * rows * width * OUT_BLOCK * 4, bytes_accessed=6 << 20, transcendentals=0
        ),
        name="project_first" if first else "project_second",
    )(*parts, weight)


def along_z(block, step):
    route = [
        (c * ZS + z, c * ZS + (z + (step if c == 0 else -step)) % ZS)
        for c in range(CORES)
        for z in range(ZS)
    ]
    return lax.ppermute(block, ("core", "z"), route)


def body(q, rkeys, rvalues, pkeys, pvalues, weight, segment_ids, block_mask):
    kv, rkv, q = prepare(pkeys, pvalues, rkeys, rvalues, q)
    first, first_q = opposite(kv, "x", 1), opposite(q, "y", 1)
    second, second_q = opposite(kv, "x", -1), opposite(q, "y", -1)
    prev = shifted(rkv, ("x", "y", "core"), -1)
    first, first_q, prev, seen = lax.optimization_barrier(
        (first, first_q, prev, visibility(block_mask))
    )
    far, far_q = opposite(first, "x", 1), opposite(first_q, "y", 1)
    second, second_q, far_q = lax.optimization_barrier((second, second_q, far_q))
    mine = [kv, first, second, far]
    pieces = mine + [shifted(p, "core", 1) for p in mine]

    next_part = attend(seen[2], first_q, pieces)[0]
    next_part, far_q = lax.optimization_barrier((next_part, far_q))
    next_one = opposite(next_part, "y", -1)
    part = attend(seen[1], far_q, pieces)[0]
    part, second_q = lax.optimization_barrier((part, second_q))
    two = shifted(part, "y", 2)
    last_one = opposite(attend(seen[3], second_q, pieces)[0], "y", 1)
    segments = pltpu.with_memory_space_constraint(segment_ids.reshape(-1, TILE), pltpu.HBM)
    weight = pltpu.with_memory_space_constraint(weight, pltpu.HBM)
    own, weight = attend(seen[0], q, pieces, (prev, rkv, segments, weight))

    *sent, att = project([own, two, next_one, last_one], weight)
    for3, for2, for1 = (along_z(b, step) for b, step in zip(sent, (-1, 1, -1)))
    direct, rest3, rest2, rest1, total = project([att], weight)
    got_direct = along_z(direct, 1)
    back3 = along_z((rest3 + for3.astype(jnp.float32)).astype(jnp.bfloat16), -3)
    on2 = along_z((rest2 + for2.astype(jnp.float32)).astype(jnp.bfloat16), 2)
    back1 = along_z((rest1 + for1.astype(jnp.float32)).astype(jnp.bfloat16), -1)
    total = total + got_direct.astype(jnp.float32)
    for part in (back1, on2, back3):
        total = total + part.astype(jnp.float32)
    return total.astype(jnp.bfloat16)


def solution(mesh):
    split = Mesh(mesh.devices.reshape(XS, YS, CORES, ZS), ("x", "y", "core", "z"))
    seq = ("x", "y", "core")
    placed = (P(seq, "z"),) * 5 + (P("z", None), P(), P())
    return jax.shard_map(
        body, mesh=split, in_specs=placed, out_specs=P(seq, "z"), check_vma=False
    )
```
